32 devices in a mesh: pipe: 4 (over y, x), dp: 8 (over z, core).
Axes of the slice: x: 2, y: 2, z: 4, core: 2. Of those that a mesh axis runs over, the one named last changes fastest.
Arguments:
- x_in: bfloat16 [16, 1024, 512], P('dp', 'pipe'), may hold values from -6 to 6
- lengths: int32 [16], P('dp'), may hold values from 256 to 1024, as said below
- cotangent: bfloat16 [16, 1024, 512], P('dp', 'pipe'), may hold values from -6 to 6
- norm_gain: float32 [2, 512], replicated, may hold values from 0.5 to 1.5
- lambda_re: float32 [2, 384], replicated, may hold values from -1 to -0.1
- lambda_im: float32 [2, 384], replicated, may hold values from -8 to 8
- log_step: float32 [2, 384], replicated, may hold values from -6.9 to -2.3
- b_weight: float32 [2, 512, 768], P(None, 'dp'), may hold values from -0.25 to 0.25
- c_weight: float32 [2, 512, 768], P(None, 'dp'), may hold values from -2 to 2
- skip_weight: float32 [2, 512], replicated, may hold values from -4 to 4
- glu_weight: float32 [2, 512, 512], P(None, 'dp'), may hold values from -0.25 to 0.25
- glu_bias: float32 [2, 512], replicated, may hold values from -3 to 3
Outputs:
- output: bfloat16 [16, 1024, 512], P('dp', 'pipe')
- x_grad: bfloat16 [16, 1024, 512], P('dp', 'pipe')
- gain_grad: float32 [2, 512], replicated
- lambda_re_grad: float32 [2, 384], replicated
- lambda_im_grad: float32 [2, 384], replicated
- log_step_grad: float32 [2, 384], replicated
- b_grad: float32 [2, 512, 768], P(None, 'dp')
- c_grad: float32 [2, 512, 768], P(None, 'dp')
- skip_grad: float32 [2, 512], replicated
- glu_weight_grad: float32 [2, 512, 512], P(None, 'dp')
- glu_bias_grad: float32 [2, 512], replicated
The draws below stay inside these ranges and needn't reach their ends.
Inputs may be any that keep to these rules, and one draw needn't show every extreme that they name: `lengths`: every length is 1024 or 256, and some sequence has length 1024.
All inputs are finite; a program needn't handle non-finite values.
Results may differ from the reference program's by a relative error of at most 0.025.
Values may be sent and summed in bfloat16 or wider, within the bound.
A program may use at most 320 MiB of HBM per device.

```python
import jax
import jax.numpy as jnp
from jax import lax

H = 512
P_SIZE = 384
LEN = 1024
LAYERS = 2
SEQS = 16


def draw_lengths(key, part):
    key = jax.random.fold_in(key, 11)
    first_key, second_key = jax.random.split(key)
    shorter = jax.random.randint(first_key, (SEQS,), 0, 2)
    chosen = jax.random.randint(second_key, (), 0, SEQS)
    shorter = jnp.where(jnp.arange(SEQS) == chosen, 0, shorter)
    return jnp.where(shorter == 1, LEN // 4, LEN).astype(jnp.int32)


def level_of(key, dims, pieces, low, largest):
    loudness, own = 1.0, jax.random.fold_in(key, 6)
    for axis_at, shards_of in pieces:
        steps = jnp.exp(jax.random.uniform(jax.random.fold_in(own, axis_at), (shards_of,), jnp.float32, low / len(pieces), largest / len(pieces)))
        loudness = loudness * jnp.repeat(steps, dims[axis_at] // shards_of).reshape([-1 if axis == axis_at else 1 for axis in range(len(dims))])
    return loudness


def bell_draw(stream_key, extent, scale, bound, cuts=(), held_as=jnp.bfloat16):
    array = scale * jax.random.normal(stream_key, extent, jnp.float32)
    if cuts:
        array = array * level_of(stream_key, extent, cuts, -0.22, 0.18)
    return jnp.clip(array, -bound, bound).astype(held_as)


def setup_inputs(seed: int = 0) -> dict:
    splits = jax.random.split(jax.random.key(seed), 13)
    x_in = bell_draw(splits[0], (SEQS, LEN, H), 1.0, 6.0, ((0, 8), (1, 4)))
    lengths = draw_lengths(jax.random.fold_in(splits[12], 71), 0)
    cotangent = bell_draw(splits[2], (SEQS, LEN, H), 1.0, 6.0, ((0, 8), (1, 4)))
    norm_gain = jnp.clip(1.0 + 0.1 * jax.random.normal(splits[3], (LAYERS, H), jnp.float32), 0.5, 1.5)
    lambda_re = jnp.clip(jax.random.uniform(splits[4], (LAYERS, P_SIZE), jnp.float32, -1.0, -0.1), -1.0, -0.1)
    lambda_im = jnp.clip(jax.random.uniform(splits[5], (LAYERS, P_SIZE), jnp.float32, -8.0, 8.0), -8.0, 8.0)
    log_step = jnp.clip(jax.random.uniform(splits[6], (LAYERS, P_SIZE), jnp.float32, -6.9, -2.3), -6.9, -2.3)
    b_weight = bell_draw(splits[7], (LAYERS, H, 2 * P_SIZE), H ** -0.5, 0.25, ((1, 8),), jnp.float32)
    c_weight = bell_draw(splits[8], (LAYERS, H, 2 * P_SIZE), (max(P_SIZE // 48, 1)) ** -0.5, 2.0, ((1, 8),), jnp.float32)
    skip_weight = bell_draw(splits[9], (LAYERS, H), 1.0, 4.0, (), jnp.float32)
    glu_weight = bell_draw(splits[10], (LAYERS, H, H), H ** -0.5, 0.25, ((1, 8),), jnp.float32)
    glu_bias = bell_draw(splits[11], (LAYERS, H), 0.5, 3.0, (), jnp.float32)
    return dict(x_in=x_in, lengths=lengths, cotangent=cotangent, norm_gain=norm_gain, lambda_re=lambda_re, lambda_im=lambda_im, log_step=log_step, b_weight=b_weight, c_weight=c_weight, skip_weight=skip_weight, glu_weight=glu_weight, glu_bias=glu_bias)


EPSILON = 1e-05
HIGHEST = lax.Precision.HIGHEST

@jax.custom_vjp
def low(v):
    return lax.optimization_barrier(v.astype(jnp.bfloat16)).astype(jnp.float32)

@jax.custom_vjp
def low_back(v):
    return v

def low_keep(v):
    return (low(v), None)

def low_pass(kept, grad):
    return (grad,)

def back_keep(v):
    return (v, None)

def back_low(kept, grad):
    return (low(grad),)
low.defvjp(low_keep, low_pass)
low_back.defvjp(back_keep, back_low)

def discretize(lambda_real, lambda_imag, log_steps):
    step_size = jnp.exp(log_steps)
    radius = jnp.exp(lambda_real * step_size)
    angle_turn = lambda_imag * step_size
    decay_real = radius * jnp.cos(angle_turn)
    decay_imag = radius * jnp.sin(angle_turn)
    modulus = lambda_real * lambda_real + lambda_imag * lambda_imag
    coef_real = ((decay_real - 1.0) * lambda_real + decay_imag * lambda_imag) / modulus
    coef_imag = (decay_imag * lambda_real - (decay_real - 1.0) * lambda_imag) / modulus
    return (decay_real, decay_imag, coef_real, coef_imag)

def compose(earlier, latter):
    mul_real, mul_imag, add_real, add_imag = earlier
    next_mul_real, next_mul_imag, next_add_real, next_add_imag = latter
    return (next_mul_real * mul_real - next_mul_imag * mul_imag, next_mul_real * mul_imag + next_mul_imag * mul_real, next_mul_real * add_real - next_mul_imag * add_imag + next_add_real, next_mul_real * add_imag + next_mul_imag * add_real + next_add_imag)

def layer_pass(rows_in, row_mask, params, reverse_time):
    norm_gain, lambda_real, lambda_imag, log_steps, proj_in, proj_out, skip_gain, gate_mat, gate_bias = params
    average = lax.optimization_barrier(jnp.mean(rows_in, axis=1, keepdims=True))
    centred = rows_in - average
    spread = lax.optimization_barrier(jnp.mean(centred * centred, axis=1, keepdims=True))
    normed = low(centred * lax.rsqrt(spread + EPSILON) * norm_gain * row_mask[:, None])
    decay_real, decay_imag, coef_real, coef_imag = discretize(lambda_real, lambda_imag, log_steps)
    width_state = decay_real.shape[0]
    projected = low_back(jnp.dot(normed, proj_in, precision=HIGHEST))
    proj_real = projected[:, :width_state]
    proj_imag = projected[:, width_state:]
    drive_real = coef_real * proj_real - coef_imag * proj_imag
    drive_imag = coef_real * proj_imag + coef_imag * proj_real
    if reverse_time:
        drive_real = drive_real[::-1]
        drive_imag = drive_imag[::-1]
    scale_real = jnp.broadcast_to(decay_real, drive_real.shape)
    scale_imag = jnp.broadcast_to(decay_imag, drive_real.shape)
    _, _, state_real, state_imag = lax.associative_scan(compose, (scale_real, scale_imag, drive_real, drive_imag))
    if reverse_time:
        state_real = state_real[::-1]
        state_imag = state_imag[::-1]
    states = low(jnp.concatenate([state_real, -state_imag], axis=1))
    before = low_back(jnp.dot(states, proj_out.T, precision=HIGHEST) + skip_gain * normed)
    gated = low_back(low(jax.nn.gelu(before, approximate=False)))
    gate = low_back(jnp.dot(gated, gate_mat, precision=HIGHEST) + gate_bias)
    return rows_in + row_mask[:, None] * (gated * jax.nn.sigmoid(gate))

def reference(x_in, lengths, cotangent, norm_gain, lambda_re, lambda_im, log_step, b_weight, c_weight, skip_weight, glu_weight, glu_bias):
    positions = jnp.arange(x_in.shape[1], dtype=jnp.int32)

    def network(inputs, gain_all, lam_real, lam_imag, step_all, proj_in_all, proj_out_all, skip_all, gate_mats, bias_all):

        def layer_params(which_layer):
            return (gain_all[which_layer], lam_real[which_layer], lam_imag[which_layer], step_all[which_layer], proj_in_all[which_layer], proj_out_all[which_layer], skip_all[which_layer], gate_mats[which_layer], bias_all[which_layer])

        def per_sequence(packed):
            sequence, seq_length = packed
            row_mask = (positions < seq_length.astype(jnp.int32)).astype(jnp.float32)
            middle = layer_pass(sequence, row_mask, layer_params(0), False)
            middle = low_back(low(middle))
            return low(layer_pass(middle, row_mask, layer_params(1), True))
        return lax.map(jax.checkpoint(per_sequence), (inputs, lengths))
    floats = (x_in.astype(jnp.float32), norm_gain, lambda_re, lambda_im, log_step, b_weight, c_weight, skip_weight, glu_weight, glu_bias)
    output, pullback = jax.vjp(network, *floats)
    gradients = pullback(cotangent.astype(jnp.float32))
    return (output.astype(jnp.bfloat16), gradients[0].astype(jnp.bfloat16), gradients[1], gradients[2], gradients[3], gradients[4], gradients[5], gradients[6], gradients[7], gradients[8], gradients[9])
```

```python
import functools

import jax
import jax.numpy as jnp
from jax import lax
from jax.experimental import pallas as pl
from jax.experimental.pallas import tpu as pltpu
from jax.sharding import PartitionSpec as P

EPSILON = 1e-05
CHUNKS = 8
TILE = 32
MESH = pl.DeviceIdType.MESH
F32 = jnp.float32
BF16 = jnp.bfloat16
NN = (((1,), (0,)), ((), ()))
NT = (((1,), (1,)), ((), ()))
TN = (((0,), (0,)), ((), ()))


def cmul(u, v):
    return (u[0] * v[0] - u[1] * v[1], u[0] * v[1] + u[1] * v[0])


def conj(u):
    return (u[0], -u[1])


def dot(a, b, dims):
    return lax.dot_general(a, b, dims, preferred_element_type=F32)


def discretize(lam_re, lam_im, log_step):
    step = jnp.exp(log_step)
    radius = jnp.exp(lam_re * step)
    turn = lam_im * step
    decay = (radius * jnp.cos(turn), radius * jnp.sin(turn))
    modulus = lam_re * lam_re + lam_im * lam_im
    coef = (
        ((decay[0] - 1.0) * lam_re + decay[1] * lam_im) / modulus,
        (decay[1] * lam_re - (decay[0] - 1.0) * lam_im) / modulus,
    )
    return step, decay, coef


def discretize_grads(lam_re, lam_im, log_step, decay_grad, coef_grad):
    step, decay, coef = discretize(lam_re, lam_im, log_step)
    lam = (lam_re, lam_im)
    modulus = lam_re * lam_re + lam_im * lam_im
    inverse = (lam_re / modulus, -lam_im / modulus)
    through = cmul(coef_grad, conj(inverse))
    total = (decay_grad[0] + through[0], decay_grad[1] + through[1])
    first = cmul(total, (step * decay[0], -step * decay[1]))
    second = cmul(coef_grad, conj(cmul(coef, inverse)))
    turned = cmul(total, conj(cmul(lam, decay)))
    return first[0] - second[0], first[1] - second[1], step * turned[0]


def main_kernel(
    depth,
    x_ref, cot_ref, len_ref, gain_ref, lre_ref, lim_ref, lst_ref, skip_ref, bias_ref, w_ref,
    out_ref, xg_ref, gpart_ref, small_ref,
    h_ref, go_ref, xhat_ref, rstd_ref, normed_ref, p_ref, z_ref, zb_ref, dg_ref, gated_ref, sig_ref,
    gg_ref, gb_ref, gp_ref, src_ref, tmp_ref, acc_ref,
    ends_ref, got_ref, send_sems, recv_sems,
):
    seqs, pos, model = x_ref.shape
    state = lre_ref.shape[1]
    layers = gain_ref.shape[0]
    rows = seqs * pos
    steps = pos // CHUNKS
    me, dp = lax.axis_index("pipe"), lax.axis_index("dp")

    def peer(k):
        return lax.rem(me + k, depth)

    barrier = pltpu.get_barrier_semaphore()
    for k in range(1, depth):
        pl.semaphore_signal(barrier, inc=1, device_id=(peer(k), dp), device_id_type=MESH)

    row = lax.broadcasted_iota(jnp.int32, (pos, pos), 0)
    col = lax.broadcasted_iota(jnp.int32, (pos, pos), 1)
    spread = (lax.rem(row, CHUNKS) * steps + lax.div(row, CHUNKS) == col).astype(F32).astype(BF16)
    masks = [(len_ref[q] > me * pos).astype(F32) for q in range(seqs)]
    sublane = lax.broadcasted_iota(jnp.int32, (CHUNKS, state), 0)

    def seq_rows(q):
        return pl.ds(q * pos, pos)

    def tiles(body, q, init=0, unroll=1):
        def step(i, carry):
            return body(pl.ds(pl.multiple_of(q * pos + i * TILE, TILE), TILE), masks[q], carry)
        return lax.fori_loop(0, pos // TILE, step, init, unroll=unroll)

    def all_tiles(body, init=0):
        for q in range(seqs):
            init = tiles(body, q, init)
        return init

    def fold(value):
        total = value[0:8]
        for r in range(8, value.shape[0], 8):
            total = total + value[r:r + 8]
        return total

    for q in range(seqs):
        h_ref[0, seq_rows(q), :] = dot(spread, x_ref[q], NN).astype(BF16)
        go_ref[seq_rows(q), :] = dot(spread, cot_ref[q], NN).astype(BF16)

    step_all, decay_all, coef_all = discretize(lre_ref[...], lim_ref[...], lst_ref[...])
    pl.semaphore_wait(barrier, depth - 1)

    def complex_rows(src, r):
        return (src[r, 0:state], src[r, state:2 * state])

    zero = jnp.zeros((CHUNKS, state), F32)

    def scan_ends(src, decay, down):
        def step(i, carry):
            s = (steps - 1 - i) if down else i
            made = []
            for q in range(seqs):
                r = pl.ds(pl.multiple_of(q * pos + s * CHUNKS, CHUNKS), CHUNKS)
                add = complex_rows(src, r)
                moved = cmul(decay, carry[q])
                made.append((moved[0] + add[0], moved[1] + add[1]))
            return tuple(made)
        return lax.fori_loop(0, steps, step, ((zero, zero),) * seqs, unroll=4)

    def shifted(value, k, down):
        rolled = pltpu.roll(value, CHUNKS - k if down else k, axis=0)
        keep = (sublane < CHUNKS - k) if down else (sublane >= k)
        return jnp.where(keep, rolled, 0.0)

    def squared(value, times):
        for _ in range(times):
            value = cmul(value, value)
        return value

    def start_exchange(number, ends, decay, down):
        power = squared(decay, steps.bit_length() - 1)
        jump, before = power, []
        sums = list(ends)
        k = 1
        while k < CHUNKS:
            for q in range(seqs):
                moved = cmul(jump, (shifted(sums[q][0], k, down), shifted(sums[q][1], k, down)))
                sums[q] = (sums[q][0] + moved[0], sums[q][1] + moved[1])
            before.append(jump)
            jump = cmul(jump, jump)
            k *= 2
        last = 0 if down else CHUNKS - 1
        for q in range(seqs):
            ends_ref[number, q:q + 1, 0:state] = sums[q][0][last:last + 1]
            ends_ref[number, q:q + 1, state:2 * state] = sums[q][1][last:last + 1]
        copies = []
        for k in range(1, depth):
            copy = pltpu.make_async_remote_copy(
                src_ref=ends_ref.at[number],
                dst_ref=got_ref.at[number, k - 1],
                send_sem=send_sems.at[number, k - 1],
                recv_sem=recv_sems.at[number, k - 1],
                device_id=(peer(depth - k if down else k), dp),
                device_id_type=MESH,
            )
            copy.start()
            copies.append(copy)
        place = (CHUNKS - 1 - sublane) if down else sublane
        table = (jnp.ones((CHUNKS, state), F32), zero)
        for bit, factor in enumerate(before):
            moved = cmul(table, factor)
            take = lax.rem(lax.div(place, 1 << bit), 2) == 1
            table = (jnp.where(take, moved[0], table[0]), jnp.where(take, moved[1], table[1]))
        exclusive = [(shifted(s[0], 1, down), shifted(s[1], 1, down)) for s in sums]
        return copies, jump, table, exclusive

    def finish_exchange(number, pending, down):
        copies, jump, table, exclusive = pending
        for copy in copies:
            copy.wait()
        jump_row = (jump[0][0:1], jump[1][0:1])
        carries = []
        for q in range(seqs):
            total = (jnp.zeros((1, state), F32), jnp.zeros((1, state), F32))
            factor = (jnp.ones((1, state), F32), jnp.zeros((1, state), F32))
            for k in range(1, depth):
                there = (me + k < depth) if down else (me - k >= 0)
                there = there.astype(F32)
                came = got_ref[number, k - 1]
                came = (came[q:q + 1, 0:state] * there, came[q:q + 1, state:2 * state] * there)
                moved = cmul(factor, came)
                total = (total[0] + moved[0], total[1] + moved[1])
                factor = cmul(factor, jump_row)
            wide = (jnp.broadcast_to(total[0], (CHUNKS, state)), jnp.broadcast_to(total[1], (CHUNKS, state)))
            moved = cmul(table, wide)
            carries.append((exclusive[q][0] + moved[0], exclusive[q][1] + moved[1]))
        return carries

    def wide_decay(layer):
        return tuple(jnp.broadcast_to(part[layer:layer + 1], (CHUNKS, state)) for part in decay_all)

    small_ref[...] = jnp.zeros_like(small_ref)

    for layer in range(layers):
        down = layer % 2 == 1
        decay = wide_decay(layer)
        gain = gain_ref[layer:layer + 1, :]
        skip = skip_ref[layer:layer + 1, :]
        bias = bias_ref[layer:layer + 1, :]

        def norm_tile(r, mask, carry):
            h = h_ref[layer, r, :].astype(F32)
            mean = jnp.mean(h, axis=1, keepdims=True)
            centred = h - mean
            spread_ = jnp.mean(centred * centred, axis=1, keepdims=True)
            rstd = lax.rsqrt(spread_ + EPSILON)
            xhat = centred * rstd
            xhat_ref[layer, r, :] = xhat
            rstd_ref[layer, r, :] = jnp.broadcast_to(rstd, (TILE, 128))
            normed_ref[layer, r, :] = (xhat * gain * mask).astype(BF16)
            return carry
        all_tiles(norm_tile)

        p_ref[layer] = dot(normed_ref[layer], w_ref[layer, :, 0:2 * state], NN)
        ends = scan_ends(p_ref.at[layer], decay, down)
        pending = start_exchange(layer, ends, decay, down)
        carries = finish_exchange(layer, pending, down)
        pad = pos + CHUNKS
        for q in range(seqs):
            at = q * pad + (pos if down else 0)
            z_ref[layer, at:at + CHUNKS, 0:state] = carries[q][0]
            z_ref[layer, at:at + CHUNKS, state:2 * state] = carries[q][1]

        def state_pair(i, carry):
            carry = list(carry)
            for q in range(seqs):
                pieces = []
                for half in range(2):
                    s = (steps - 1 - 2 * i - half) if down else 2 * i + half
                    r = pl.ds(pl.multiple_of(q * pos + s * CHUNKS, CHUNKS), CHUNKS)
                    add = complex_rows(p_ref.at[layer], r)
                    moved = cmul(decay, carry[q])
                    carry[q] = (moved[0] + add[0], moved[1] + add[1])
                    r = pl.ds(pl.multiple_of(q * pad + (s + (0 if down else 1)) * CHUNKS, CHUNKS), CHUNKS)
                    z_ref[layer, r, 0:state] = carry[q][0]
                    z_ref[layer, r, state:2 * state] = carry[q][1]
                    pieces.append(carry[q])
                if down:
                    pieces = pieces[::-1]
                low = (steps - 2 - 2 * i) if down else 2 * i
                r = pl.ds(pl.multiple_of(q * pos + low * CHUNKS, 2 * CHUNKS), 2 * CHUNKS)
                for part in range(2):
                    both = jnp.concatenate([pieces[0][part], pieces[1][part]], axis=0)
                    zb_ref[layer, r, part * state:(part + 1) * state] = both.astype(BF16)
            return tuple(carry)
        lax.fori_loop(0, steps // 2, state_pair, tuple(carries), unroll=2)

        tmp_ref[...] = dot(zb_ref[layer], w_ref[layer, :, 2 * state:4 * state], NT)

        def gelu_tile(r, mask, carry):
            before = tmp_ref[r, :] + skip * normed_ref[layer, r, :].astype(F32)
            phi = 0.5 * (1.0 + lax.erf(before * 0.7071067811865476))
            dg_ref[layer, r, :] = phi + before * (0.3989422804014327 * jnp.exp(-0.5 * before * before))
            gated_ref[layer, r, :] = (before * phi).astype(BF16)
            return carry
        all_tiles(gelu_tile)

        tmp_ref[...] = dot(gated_ref[layer], w_ref[layer, :, 4 * state:], NN)

        def out_tile(r, mask, carry):
            sig = 1.0 / (1.0 + jnp.exp(-(tmp_ref[r, :] + bias)))
            sig_ref[layer, r, :] = sig
            made = h_ref[layer, r, :].astype(F32) + mask * (gated_ref[layer, r, :].astype(F32) * sig)
            h_ref[layer + 1, r, :] = made.astype(BF16)
            return carry
        all_tiles(out_tile)

    gather = (lax.rem(row, steps) * CHUNKS + lax.div(row, steps) == col).astype(F32).astype(BF16)
    for q in range(seqs):
        out_ref[q] = dot(gather, h_ref[layers, seq_rows(q), :], NN).astype(BF16)

    for layer in reversed(range(layers)):
        down = layer % 2 == 1
        decay = wide_decay(layer)
        gain = gain_ref[layer:layer + 1, :]
        skip = skip_ref[layer:layer + 1, :]
        zero_row = jnp.zeros((8, model), F32)

        def gate_tile(r, mask, carry):
            sig = sig_ref[layer, r, :]
            branch = mask * go_ref[r, :].astype(F32) * sig
            grad = (branch * gated_ref[layer, r, :].astype(F32) * (1.0 - sig)).astype(BF16)
            gg_ref[r, :] = grad
            acc_ref[r, :] = branch
            return carry + fold(grad.astype(F32))
        bias_sum = all_tiles(gate_tile, zero_row)
        tmp_ref[...] = dot(gg_ref[...], w_ref[layer, :, 4 * state:], NT)

        def before_tile(r, mask, carry):
            gated_grad = (acc_ref[r, :] + tmp_ref[r, :]).astype(BF16).astype(F32)
            grad = (gated_grad * dg_ref[layer, r, :]).astype(BF16)
            gb_ref[r, :] = grad
            return carry + fold(grad.astype(F32) * normed_ref[layer, r, :].astype(F32))
        skip_sum = all_tiles(before_tile, zero_row)

        src_ref[...] = dot(gb_ref[...], w_ref[layer, :, 2 * state:4 * state], NN)
        back = conj(decay)
        ends = scan_ends(src_ref, back, not down)
        pending = start_exchange(layers + layer, ends, back, not down)
        gpart_ref[layer, :, 4 * state:] = dot(gated_ref[layer], gg_ref[...], TN)
        gpart_ref[layer, :, 2 * state:4 * state] = dot(gb_ref[...], zb_ref[layer], TN)
        carries = finish_exchange(layers + layer, pending, not down)

        def adjoint_pair(i, loop):
            carry, sums = list(loop[0]), list(loop[1])
            for q in range(seqs):
                pieces = []
                for half in range(2):
                    s = 2 * i + half if down else (steps - 1 - 2 * i - half)
                    r = pl.ds(pl.multiple_of(q * pos + s * CHUNKS, CHUNKS), CHUNKS)
                    add = complex_rows(src_ref, r)
                    moved = cmul(back, carry[q])
                    adj = (moved[0] + add[0], moved[1] + add[1])
                    carry[q] = adj
                    pieces.append(adj)
                    proj = complex_rows(p_ref.at[layer], r)
                    r = pl.ds(pl.multiple_of(q * pad + (s + (1 if down else 0)) * CHUNKS, CHUNKS), CHUNKS)
                    prior = complex_rows(z_ref.at[layer], r)
                    sums[0] = sums[0] + (adj[0] * prior[0] + adj[1] * prior[1])
                    sums[1] = sums[1] + (adj[1] * prior[0] - adj[0] * prior[1])
                    sums[2] = sums[2] + (adj[0] * proj[0] + adj[1] * proj[1])
                    sums[3] = sums[3] + (adj[1] * proj[0] - adj[0] * proj[1])
                if not down:
                    pieces = pieces[::-1]
                low = 2 * i if down else (steps - 2 - 2 * i)
                r = pl.ds(pl.multiple_of(q * pos + low * CHUNKS, 2 * CHUNKS), 2 * CHUNKS)
                for part in range(2):
                    both = jnp.concatenate([pieces[0][part], pieces[1][part]], axis=0)
                    gp_ref[r, part * state:(part + 1) * state] = both.astype(BF16)
            return tuple(carry), tuple(sums)
        _, sums = lax.fori_loop(0, steps // 2, adjoint_pair, (tuple(carries), (zero,) * 4), unroll=1)

        gpart_ref[layer, :, 0:2 * state] = dot(normed_ref[layer], gp_ref[...], TN)
        tmp_ref[...] = dot(gp_ref[...], w_ref[layer, :, 0:2 * state], NT)

        def input_tile(r, mask, carry):
            grad = (tmp_ref[r, :] + skip * gb_ref[r, :].astype(F32)) * mask
            xhat = xhat_ref[layer, r, :]
            rstd = jnp.concatenate([rstd_ref[layer, r, :]] * (model // 128), axis=1)
            scaled = grad * gain
            first = jnp.mean(scaled, axis=1, keepdims=True)
            second = jnp.mean(scaled * xhat, axis=1, keepdims=True)
            made = go_ref[r, :].astype(F32) + rstd * (scaled - first - xhat * second)
            go_ref[r, :] = made.astype(BF16)
            return carry + fold(grad * xhat)
        gain_sum = all_tiles(input_tile, zero_row)

        for at, value in enumerate((gain_sum, skip_sum, bias_sum)):
            small_ref[layer, at:at + 1, :] = jnp.sum(value, axis=0, keepdims=True)
        for at, value in enumerate(sums):
            small_ref[layer, 3 + at:4 + at, 0:state] = jnp.sum(value, axis=0, keepdims=True)

    for q in range(seqs):
        xg_ref[q] = dot(gather, go_ref[seq_rows(q), :], NN).astype(BF16)


def run_main(depth, x_in, lengths, cotangent, norm_gain, lambda_re, lambda_im, log_step, weights, skip_weight, glu_bias):
    seqs, pos, model = x_in.shape
    layers, state = lambda_re.shape
    rows = seqs * pos
    wide = weights.shape[2]
    vmem = pl.BlockSpec(memory_space=pltpu.VMEM)
    smem = pl.BlockSpec(memory_space=pltpu.SMEM)
    return pl.pallas_call(
        functools.partial(main_kernel, depth),
        out_shape=(
            jax.ShapeDtypeStruct(x_in.shape, BF16),
            jax.ShapeDtypeStruct(x_in.shape, BF16),
            jax.ShapeDtypeStruct((layers, model, wide), F32),
            jax.ShapeDtypeStruct((layers, 8, model), F32),
        ),
        in_specs=[vmem, vmem, smem] + [vmem] * 7,
        out_specs=(vmem,) * 4,
        scratch_shapes=[
            pltpu.VMEM((layers + 1, rows, model), BF16),
            pltpu.VMEM((rows, model), BF16),
            pltpu.VMEM((layers, rows, model), F32),
            pltpu.VMEM((layers, rows, 128), F32),
            pltpu.VMEM((layers, rows, model), BF16),
            pltpu.VMEM((layers, rows, 2 * state), F32),
            pltpu.VMEM((layers, rows + seqs * CHUNKS, 2 * state), F32),
            pltpu.VMEM((layers, rows, 2 * state), BF16),
            pltpu.VMEM((layers, rows, model), F32),
            pltpu.VMEM((layers, rows, model), BF16),
            pltpu.VMEM((layers, rows, model), F32),
            pltpu.VMEM((rows, model), BF16),
            pltpu.VMEM((rows, model), BF16),
            pltpu.VMEM((rows, 2 * state), BF16),
            pltpu.VMEM((rows, 2 * state), F32),
            pltpu.VMEM((rows, model), F32),
            pltpu.VMEM((rows, model), F32),
            pltpu.VMEM((2 * layers, 8, 2 * state), F32),
            pltpu.VMEM((2 * layers, depth - 1, 8, 2 * state), F32),
            pltpu.SemaphoreType.DMA((2 * layers, depth - 1)),
            pltpu.SemaphoreType.DMA((2 * layers, depth - 1)),
        ],
        compiler_params=pltpu.CompilerParams(
            collective_id=0, has_side_effects=True, vmem_limit_bytes=60 * 2**20
        ),
    )(x_in, cotangent, lengths, norm_gain, lambda_re, lambda_im, log_step, skip_weight, glu_bias, weights)


def per_device(
    x_in, lengths, cotangent, norm_gain, lambda_re, lambda_im, log_step,
    b_weight, c_weight, skip_weight, glu_weight, glu_bias,
):
    depth = lax.axis_size("pipe")
    state = lambda_re.shape[1]
    _, _, coef = discretize(lambda_re, lambda_im, log_step)
    c_real, c_imag = c_weight[:, :, :state], c_weight[:, :, state:]
    turned = cmul((coef[0][:, None], coef[1][:, None]), (c_real, c_imag))
    shard = jnp.concatenate([b_weight, turned[0], -turned[1], glu_weight], axis=2).astype(BF16)
    weights = lax.all_gather(shard, "dp", axis=1, tiled=True)
    output, x_grad, gpart, small = run_main(
        depth, x_in, lengths, cotangent, norm_gain, lambda_re, lambda_im, log_step, weights, skip_weight, glu_bias
    )
    grads = lax.psum_scatter(gpart, "dp", scatter_dimension=1, tiled=True)
    grads = lax.psum(grads.astype(BF16), "pipe").astype(F32)
    small = lax.psum(small, ("pipe", "dp"))
    m_real, m_imag = grads[:, :, 2 * state:3 * state], grads[:, :, 3 * state:4 * state]
    turned = cmul((coef[0][:, None], coef[1][:, None]), (m_real, m_imag))
    c_grad = jnp.concatenate([turned[0], -turned[1]], axis=2)
    decay_grad = (small[:, 3, :state], small[:, 4, :state])
    scale = coef[0] * coef[0] + coef[1] * coef[1]
    coef_grad = cmul((small[:, 5, :state], small[:, 6, :state]), (coef[0] / scale, coef[1] / scale))
    lam_re_grad, lam_im_grad, step_grad = discretize_grads(lambda_re, lambda_im, log_step, decay_grad, coef_grad)
    return (
        output, x_grad, small[:, 0], lam_re_grad, lam_im_grad, step_grad,
        grads[:, :, :2 * state], c_grad, small[:, 1], grads[:, :, 4 * state:], small[:, 2],
    )


def solution(mesh):
    split, whole, rows = P("dp", "pipe", None), P(), P(None, "dp", None)
    return jax.shard_map(
        per_device,
        mesh=mesh,
        in_specs=(split, P("dp"), split, whole, whole, whole, whole, rows, rows, whole, rows, whole),
        out_specs=(split, split, whole, whole, whole, whole, rows, rows, whole, rows, whole),
        check_vma=False,
    )
```

```python
import functools

import jax
import jax.numpy as jnp
from jax import lax
from jax.experimental import pallas as pl
from jax.experimental.pallas import tpu as pltpu
from jax.sharding import PartitionSpec as P

EPSILON = 1e-05
CHUNKS = 8
TILE = 32
MESH = pl.DeviceIdType.MESH
F32 = jnp.float32
BF16 = jnp.bfloat16
NN = (((1,), (0,)), ((), ()))
NT = (((1,), (1,)), ((), ()))
TN = (((0,), (0,)), ((), ()))


def cmul(u, v):
    return (u[0] * v[0] - u[1] * v[1], u[0] * v[1] + u[1] * v[0])


def conj(u):
    return (u[0], -u[1])


def dot(a, b, dims):
    return lax.dot_general(a, b, dims, preferred_element_type=F32)


def discretize(lam_re, lam_im, log_step):
    step = jnp.exp(log_step)
    radius = jnp.exp(lam_re * step)
    turn = lam_im * step
    decay = (radius * jnp.cos(turn), radius * jnp.sin(turn))
    modulus = lam_re * lam_re + lam_im * lam_im
    coef = (
        ((decay[0] - 1.0) * lam_re + decay[1] * lam_im) / modulus,
        (decay[1] * lam_re - (decay[0] - 1.0) * lam_im) / modulus,
    )
    return step, decay, coef


def discretize_grads(lam_re, lam_im, log_step, decay_grad, coef_grad):
    step, decay, coef = discretize(lam_re, lam_im, log_step)
    lam = (lam_re, lam_im)
    modulus = lam_re * lam_re + lam_im * lam_im
    inverse = (lam_re / modulus, -lam_im / modulus)
    through = cmul(coef_grad, conj(inverse))
    total = (decay_grad[0] + through[0], decay_grad[1] + through[1])
    first = cmul(total, (step * decay[0], -step * decay[1]))
    second = cmul(coef_grad, conj(cmul(coef, inverse)))
    turned = cmul(total, conj(cmul(lam, decay)))
    return first[0] - second[0], first[1] - second[1], step * turned[0]


def weight_gather(refs, pieces, depth, planes, me, plane, core, at_pipe, at_plane, at_core, remote):
    w_ref = refs["w"]
    sems = (refs["w_send"], refs["w_recv"])
    along, onward, across = {}, {}, {}

    def part(piece):
        layer, low, high = pieces[piece]
        return w_ref.at[layer], pl.ds(low, high - low)

    def send(piece):
        ref, cols = part(piece)
        along[piece] = []
        for k in range(1, planes):
            block = ref.at[plane, core, me, :, cols]
            along[piece].append(remote(block, block, sems, (piece, k - 1), at_plane(k)))

    def relay(piece):
        ref, cols = part(piece)
        onward[piece] = []
        for k in range(1, planes):
            along[piece][k - 1].wait_recv()
            block = ref.at[lax.rem(plane - k + planes, planes), core, me, :, cols]
            for j in range(1, depth):
                at = planes - 1 + (k - 1) * (depth - 1) + j - 1
                onward[piece].append(remote(block, block, sems, (piece, at), at_pipe(j)))

    def swap(piece):
        ref, cols = part(piece)
        for copy in onward[piece]:
            copy.wait_recv()
        block = ref.at[:, core, :, :, cols]
        across[piece] = remote(block, block, sems, (piece, planes * depth - 1), at_core)

    def ready(piece):
        across[piece].wait_recv()

    return send, relay, swap, ready


def gradient_sums(refs, kinds, depth, planes, me, plane, core, at_pipe, at_plane, at_core, remote):
    sems = (refs["g_send"], refs["g_recv"])
    copies = {}

    def of(name, piece):
        return refs[name + str(piece % kinds)].at[piece // kinds]

    def stage(piece, matrix, low, high):
        part = of("part", piece)
        part[..., low:high] = matrix.astype(BF16).reshape(part.shape[:-1] + (high - low,))

    def start(piece):
        part, other = of("part", piece), of("other", piece)
        copies[piece, 0] = remote(part.at[:, 1 - core], other, sems, (piece, 0), at_core)

    def to_pipe(piece):
        copies[piece, 0].wait_recv()
        part, other, pair = of("part", piece), of("other", piece), of("pair", piece)

        def add(i, carry):
            z, j = lax.div(i, depth), lax.rem(i, depth)
            pair[j, z] = (part[z, core, j].astype(F32) + other[z, j].astype(F32)).astype(BF16)
            return carry
        lax.fori_loop(0, planes * depth, add, 0)
        copies[piece, 1] = [
            remote(pair.at[lax.rem(me + k, depth)], of("quad", piece).at[k - 1], sems, (piece, k), at_pipe(k))
            for k in range(1, depth)
        ]

    def to_plane(piece):
        pair, quad, line = of("pair", piece), of("quad", piece), of("line", piece)
        for copy in copies[piece, 1]:
            copy.wait_recv()

        def add(z, carry):
            total = pair[me, z].astype(F32)
            for k in range(1, depth):
                total = total + quad[k - 1, z].astype(F32)
            line[z] = total.astype(BF16)
            return carry
        lax.fori_loop(0, planes, add, 0)
        copies[piece, 2] = [
            remote(line.at[lax.rem(plane + k, planes)], of("came", piece).at[k - 1], sems, (piece, depth + k - 1), at_plane(k))
            for k in range(1, planes)
        ]

    def to_peers(piece):
        line, came, done = of("line", piece), of("came", piece), of("done", piece)
        for copy in copies[piece, 2]:
            copy.wait_recv()
        total = line[plane].astype(F32)
        for k in range(1, planes):
            total = total + came[k - 1].astype(F32)
        done[me] = total.astype(BF16)
        copies[piece, 3] = [
            remote(done.at[me], done.at[me], sems, (piece, depth + planes + k - 2), at_pipe(k))
            for k in range(1, depth)
        ]

    def finish(piece):
        for copy in copies[piece, 3]:
            copy.wait_recv()
        done = of("done", piece)[...]
        return done.reshape(done.shape[0] * done.shape[1], done.shape[2])

    return stage, start, to_pipe, to_plane, to_peers, finish


def small_sums(refs, depth, planes, me, plane, core, at_pipe, at_plane, at_core, remote):
    sems = (refs["s_send"], refs["s_recv"])
    own, other, quad, line = refs["small"], refs["s_other"], refs["s_quad"], refs["s_line"]
    copies = {}

    def start(layer):
        copies[layer, 0] = remote(own.at[layer], other.at[layer], sems, (layer, 0), at_core)

    def to_pipe(layer):
        copies[layer, 0].wait_recv()
        quad[layer, me] = own[layer] + other[layer]
        copies[layer, 1] = [
            remote(quad.at[layer, me], quad.at[layer, me], sems, (layer, k), at_pipe(k)) for k in range(1, depth)
        ]

    def to_plane(layer):
        for copy in copies[layer, 1]:
            copy.wait_recv()
        total = quad[layer, 0]
        for j in range(1, depth):
            total = total + quad[layer, j]
        line[layer, plane] = total
        copies[layer, 2] = [
            remote(line.at[layer, plane], line.at[layer, plane], sems, (layer, depth + k - 1), at_plane(k))
            for k in range(1, planes)
        ]

    def finish(layer):
        for copy in copies[layer, 2]:
            copy.wait_recv()
        total = line[layer, 0]
        for z in range(1, planes):
            total = total + line[layer, z]
        return total

    return start, to_pipe, to_plane, finish


def main_kernel(depth, planes, names, *refs):
    r_ = dict(zip(names, refs))
    x_ref, cot_ref, len_ref, gain_ref = r_["x"], r_["cot"], r_["len"], r_["gain"]
    lre_ref, lim_ref, lst_ref, skip_ref, bias_ref = r_["lre"], r_["lim"], r_["lst"], r_["skip"], r_["bias"]
    out_ref, xg_ref, small_ref = r_["out"], r_["xg"], r_["small"]
    h_ref, go_ref, xhat_ref, rstd_ref, normed_ref = r_["h"], r_["go"], r_["xhat"], r_["rstd"], r_["normed"]
    p_ref, z_ref, zb_ref, dg_ref, gated_ref, sig_ref = r_["p"], r_["z"], r_["zb"], r_["dg"], r_["gated"], r_["sig"]
    gg_ref, gb_ref, gp_ref, src_ref, tmp_ref, acc_ref = r_["gg"], r_["gb"], r_["gp"], r_["src"], r_["tmp"], r_["acc"]
    ends_ref, got_ref, send_sems, recv_sems = r_["ends"], r_["got"], r_["send"], r_["recv"]
    w_ref = r_["w"]
    seqs, pos, model = x_ref.shape
    state = lre_ref.shape[1]
    layers = gain_ref.shape[0]
    rows = seqs * pos
    steps = pos // CHUNKS
    me, dp = lax.axis_index("pipe"), lax.axis_index("dp")
    plane, core = lax.div(dp, 2), lax.rem(dp, 2)

    def peer(k):
        return lax.rem(me + k, depth)

    def at_pipe(k):
        return (peer(k), dp)

    def at_plane(k):
        return (me, 2 * lax.rem(plane + k, planes) + core)

    at_core = (me, 2 * plane + (1 - core))
    others = [at_pipe(k) for k in range(1, depth)]
    if planes:
        others += [at_plane(k) for k in range(1, planes)] + [at_core]
    barrier = pltpu.get_barrier_semaphore()
    for device in others:
        pl.semaphore_signal(barrier, inc=1, device_id=device, device_id_type=MESH)

    unsent = []

    def remote(src, dst, sems, at, device):
        copy = pltpu.make_async_remote_copy(
            src_ref=src, dst_ref=dst, send_sem=sems[0].at[at], recv_sem=sems[1].at[at],
            device_id=device, device_id_type=MESH,
        )
        copy.start()
        unsent.append(copy)
        return copy

    row = lax.broadcasted_iota(jnp.int32, (pos, pos), 0)
    col = lax.broadcasted_iota(jnp.int32, (pos, pos), 1)
    spread = (lax.rem(row, CHUNKS) * steps + lax.div(row, CHUNKS) == col).astype(F32).astype(BF16)
    masks = [(len_ref[q] > me * pos).astype(F32) for q in range(seqs)]
    sublane = lax.broadcasted_iota(jnp.int32, (CHUNKS, state), 0)

    def seq_rows(q):
        return pl.ds(q * pos, pos)

    def tiles(body, q, init=0, unroll=1):
        def step(i, carry):
            return body(pl.ds(pl.multiple_of(q * pos + i * TILE, TILE), TILE), masks[q], carry)
        return lax.fori_loop(0, pos // TILE, step, init, unroll=unroll)

    def all_tiles(body, init=0):
        for q in range(seqs):
            init = tiles(body, q, init)
        return init

    def fold(value):
        total = value[0:8]
        for r in range(8, value.shape[0], 8):
            total = total + value[r:r + 8]
        return total

    step_all, decay_all, coef_all = discretize(lre_ref[...], lim_ref[...], lst_ref[...])
    if planes:
        ways = (depth, planes, me, plane, core, at_pipe, at_plane, at_core, remote)
        pieces = ((0, 0, 2 * state), (0, 2 * state, 4 * state + model), (1, 0, 4 * state + model))
        w_send, w_relay, w_swap, w_ready = weight_gather(r_, pieces, *ways)
        g_stage, g_start, g_pipe, g_plane, g_peers, g_finish = gradient_sums(r_, 2, *ways)
        s_start, s_pipe, s_plane, s_finish = small_sums(r_, *ways)
        for layer in range(layers):
            own = w_ref.at[layer, plane, core]

            def keep(matrix, low):
                high = low + matrix.shape[1]
                own[:, :, low:high] = matrix.astype(BF16).reshape(depth, matrix.shape[0] // depth, high - low)
            keep(r_["b"][layer], 0)
            coef = (coef_all[0][layer:layer + 1], coef_all[1][layer:layer + 1])
            turned = cmul(coef, (r_["c"][layer, :, 0:state], r_["c"][layer, :, state:2 * state]))
            keep(turned[0], 2 * state)
            keep(-turned[1], 3 * state)
            keep(r_["glu"][layer], 4 * state)
    pl.semaphore_wait(barrier, len(others))
    if planes:
        w_send(0)
    for q in range(seqs):
        h_ref[0, seq_rows(q), :] = dot(spread, x_ref[q], NN).astype(BF16)

    def matrix(layer, which):
        low, high = (0, 2 * state, 4 * state)[which], (2 * state, 4 * state, w_ref.shape[-1])[which]
        value = w_ref[layer, ..., low:high]
        return value.reshape(model, high - low)

    def complex_rows(src, r):
        return (src[r, 0:state], src[r, state:2 * state])

    zero = jnp.zeros((CHUNKS, state), F32)

    def scan_ends(src, decay, down):
        def step(i, carry):
            s = (steps - 1 - i) if down else i
            made = []
            for q in range(seqs):
                r = pl.ds(pl.multiple_of(q * pos + s * CHUNKS, CHUNKS), CHUNKS)
                add = complex_rows(src, r)
                moved = cmul(decay, carry[q])
                made.append((moved[0] + add[0], moved[1] + add[1]))
            return tuple(made)
        return lax.fori_loop(0, steps, step, ((zero, zero),) * seqs, unroll=4)

    def shifted(value, k, down):
        rolled = pltpu.roll(value, CHUNKS - k if down else k, axis=0)
        keep = (sublane < CHUNKS - k) if down else (sublane >= k)
        return jnp.where(keep, rolled, 0.0)

    def squared(value, times):
        for _ in range(times):
            value = cmul(value, value)
        return value

    def start_exchange(number, ends, decay, down):
        power = squared(decay, steps.bit_length() - 1)
        jump, before = power, []
        sums = list(ends)
        k = 1
        while k < CHUNKS:
            for q in range(seqs):
                moved = cmul(jump, (shifted(sums[q][0], k, down), shifted(sums[q][1], k, down)))
                sums[q] = (sums[q][0] + moved[0], sums[q][1] + moved[1])
            before.append(jump)
            jump = cmul(jump, jump)
            k *= 2
        last = 0 if down else CHUNKS - 1
        for q in range(seqs):
            ends_ref[number, q:q + 1, 0:state] = sums[q][0][last:last + 1]
            ends_ref[number, q:q + 1, state:2 * state] = sums[q][1][last:last + 1]
        copies = [
            remote(ends_ref.at[number], got_ref.at[number, k - 1], (send_sems, recv_sems), (number, k - 1),
                   at_pipe(depth - k if down else k))
            for k in range(1, depth)
        ]
        place = (CHUNKS - 1 - sublane) if down else sublane
        table = (jnp.ones((CHUNKS, state), F32), zero)
        for bit, factor in enumerate(before):
            moved = cmul(table, factor)
            take = lax.rem(lax.div(place, 1 << bit), 2) == 1
            table = (jnp.where(take, moved[0], table[0]), jnp.where(take, moved[1], table[1]))
        exclusive = [(shifted(s[0], 1, down), shifted(s[1], 1, down)) for s in sums]
        return copies, jump, table, exclusive

    def finish_exchange(number, pending, down):
        copies, jump, table, exclusive = pending
        for copy in copies:
            copy.wait_recv()
        jump_row = (jump[0][0:1], jump[1][0:1])
        carries = []
        for q in range(seqs):
            total = (jnp.zeros((1, state), F32), jnp.zeros((1, state), F32))
            factor = (jnp.ones((1, state), F32), jnp.zeros((1, state), F32))
            for k in range(1, depth):
                there = (me + k < depth) if down else (me - k >= 0)
                there = there.astype(F32)
                came = got_ref[number, k - 1]
                came = (came[q:q + 1, 0:state] * there, came[q:q + 1, state:2 * state] * there)
                moved = cmul(factor, came)
                total = (total[0] + moved[0], total[1] + moved[1])
                factor = cmul(factor, jump_row)
            wide = (jnp.broadcast_to(total[0], (CHUNKS, state)), jnp.broadcast_to(total[1], (CHUNKS, state)))
            moved = cmul(table, wide)
            carries.append((exclusive[q][0] + moved[0], exclusive[q][1] + moved[1]))
        return carries

    def wide_decay(layer):
        return tuple(jnp.broadcast_to(part[layer:layer + 1], (CHUNKS, state)) for part in decay_all)

    small_ref[...] = jnp.zeros_like(small_ref)

    for layer in range(layers):
        down = layer % 2 == 1
        decay = wide_decay(layer)
        gain = gain_ref[layer:layer + 1, :]
        skip = skip_ref[layer:layer + 1, :]
        bias = bias_ref[layer:layer + 1, :]

        def norm_tile(r, mask, carry):
            h = h_ref[layer, r, :].astype(F32)
            mean = jnp.mean(h, axis=1, keepdims=True)
            centred = h - mean
            spread_ = jnp.mean(centred * centred, axis=1, keepdims=True)
            rstd = lax.rsqrt(spread_ + EPSILON)
            xhat = centred * rstd
            xhat_ref[layer, r, :] = xhat
            rstd_ref[layer, r, :] = jnp.broadcast_to(rstd, (TILE, 128))
            normed_ref[layer, r, :] = (xhat * gain * mask).astype(BF16)
            return carry
        all_tiles(norm_tile)

        if planes and layer == 0:
            w_relay(0)
            w_send(1)
        if layer == 0:
            for q in range(seqs):
                go_ref[seq_rows(q), :] = dot(spread, cot_ref[q], NN).astype(BF16)
        if planes and layer == 0:
            w_swap(0)
            w_relay(1)
            w_send(2)
            w_ready(0)
        if planes and layer == 1:
            w_swap(2)
            w_ready(2)

        p_ref[layer] = dot(normed_ref[layer], matrix(layer, 0), NN)
        ends = scan_ends(p_ref.at[layer], decay, down)
        pending = start_exchange(layer, ends, decay, down)
        if planes and layer == 0:
            w_relay(2)
        carries = finish_exchange(layer, pending, down)
        pad = pos + CHUNKS
        for q in range(seqs):
            at = q * pad + (pos if down else 0)
            z_ref[layer, at:at + CHUNKS, 0:state] = carries[q][0]
            z_ref[layer, at:at + CHUNKS, state:2 * state] = carries[q][1]

        def state_pair(i, carry):
            carry = list(carry)
            for q in range(seqs):
                pieces = []
                for half in range(2):
                    s = (steps - 1 - 2 * i - half) if down else 2 * i + half
                    r = pl.ds(pl.multiple_of(q * pos + s * CHUNKS, CHUNKS), CHUNKS)
                    add = complex_rows(p_ref.at[layer], r)
                    moved = cmul(decay, carry[q])
                    carry[q] = (moved[0] + add[0], moved[1] + add[1])
                    r = pl.ds(pl.multiple_of(q * pad + (s + (0 if down else 1)) * CHUNKS, CHUNKS), CHUNKS)
                    z_ref[layer, r, 0:state] = carry[q][0]
                    z_ref[layer, r, state:2 * state] = carry[q][1]
                    pieces.append(carry[q])
                if down:
                    pieces = pieces[::-1]
                low = (steps - 2 - 2 * i) if down else 2 * i
                r = pl.ds(pl.multiple_of(q * pos + low * CHUNKS, 2 * CHUNKS), 2 * CHUNKS)
                for part in range(2):
                    both = jnp.concatenate([pieces[0][part], pieces[1][part]], axis=0)
                    zb_ref[layer, r, part * state:(part + 1) * state] = both.astype(BF16)
            return tuple(carry)
        lax.fori_loop(0, steps // 2, state_pair, tuple(carries), unroll=2)

        if planes and layer == 0:
            w_swap(1)
            w_ready(1)
        tmp_ref[...] = dot(zb_ref[layer], matrix(layer, 1), NT)

        def gelu_tile(r, mask, carry):
            before = tmp_ref[r, :] + skip * normed_ref[layer, r, :].astype(F32)
            phi = 0.5 * (1.0 + lax.erf(before * 0.7071067811865476))
            dg_ref[layer, r, :] = phi + before * (0.3989422804014327 * jnp.exp(-0.5 * before * before))
            gated_ref[layer, r, :] = (before * phi).astype(BF16)
            return carry
        all_tiles(gelu_tile)

        tmp_ref[...] = dot(gated_ref[layer], matrix(layer, 2), NN)

        def out_tile(r, mask, carry):
            sig = 1.0 / (1.0 + jnp.exp(-(tmp_ref[r, :] + bias)))
            sig_ref[layer, r, :] = sig
            made = h_ref[layer, r, :].astype(F32) + mask * (gated_ref[layer, r, :].astype(F32) * sig)
            h_ref[layer + 1, r, :] = made.astype(BF16)
            return carry
        all_tiles(out_tile)

    gather = (lax.rem(row, steps) * CHUNKS + lax.div(row, steps) == col).astype(F32).astype(BF16)
    for q in range(seqs):
        out_ref[q] = dot(gather, h_ref[layers, seq_rows(q), :], NN).astype(BF16)

    for layer in reversed(range(layers)):
        down = layer % 2 == 1
        decay = wide_decay(layer)
        gain = gain_ref[layer:layer + 1, :]
        skip = skip_ref[layer:layer + 1, :]
        zero_row = jnp.zeros((8, model), F32)

        def gate_tile(r, mask, carry):
            sig = sig_ref[layer, r, :]
            branch = mask * go_ref[r, :].astype(F32) * sig
            grad = (branch * gated_ref[layer, r, :].astype(F32) * (1.0 - sig)).astype(BF16)
            gg_ref[r, :] = grad
            acc_ref[r, :] = branch
            return carry + fold(grad.astype(F32))
        bias_sum = all_tiles(gate_tile, zero_row)
        tmp_ref[...] = dot(gg_ref[...], matrix(layer, 2), NT)

        def before_tile(r, mask, carry):
            gated_grad = (acc_ref[r, :] + tmp_ref[r, :]).astype(BF16).astype(F32)
            grad = (gated_grad * dg_ref[layer, r, :]).astype(BF16)
            gb_ref[r, :] = grad
            return carry + fold(grad.astype(F32) * normed_ref[layer, r, :].astype(F32))
        skip_sum = all_tiles(before_tile, zero_row)

        src_ref[...] = dot(gb_ref[...], matrix(layer, 1), NN)
        back = conj(decay)
        ends = scan_ends(src_ref, back, not down)
        pending = start_exchange(layers + layer, ends, back, not down)
        glu_part = dot(gated_ref[layer], gg_ref[...], TN)
        c_part = dot(gb_ref[...], zb_ref[layer], TN)
        if planes:
            g_stage(2 * layer, c_part, 0, 2 * state)
            g_stage(2 * layer, glu_part, 2 * state, 2 * state + model)
            g_start(2 * layer)
            if layer == 0:
                g_plane(2)
        else:
            r_["gpart"][layer, :, 4 * state:] = glu_part
            r_["gpart"][layer, :, 2 * state:4 * state] = c_part
        carries = finish_exchange(layers + layer, pending, not down)

        def adjoint_pair(i, loop):
            carry, sums = list(loop[0]), list(loop[1])
            for q in range(seqs):
                pieces = []
                for half in range(2):
                    s = 2 * i + half if down else (steps - 1 - 2 * i - half)
                    r = pl.ds(pl.multiple_of(q * pos + s * CHUNKS, CHUNKS), CHUNKS)
                    add = complex_rows(src_ref, r)
                    moved = cmul(back, carry[q])
                    adj = (moved[0] + add[0], moved[1] + add[1])
                    carry[q] = adj
                    pieces.append(adj)
                    proj = complex_rows(p_ref.at[layer], r)
                    r = pl.ds(pl.multiple_of(q * pad + (s + (1 if down else 0)) * CHUNKS, CHUNKS), CHUNKS)
                    prior = complex_rows(z_ref.at[layer], r)
                    sums[0] = sums[0] + (adj[0] * prior[0] + adj[1] * prior[1])
                    sums[1] = sums[1] + (adj[1] * prior[0] - adj[0] * prior[1])
                    sums[2] = sums[2] + (adj[0] * proj[0] + adj[1] * proj[1])
                    sums[3] = sums[3] + (adj[1] * proj[0] - adj[0] * proj[1])
                if not down:
                    pieces = pieces[::-1]
                low = 2 * i if down else (steps - 2 - 2 * i)
                r = pl.ds(pl.multiple_of(q * pos + low * CHUNKS, 2 * CHUNKS), 2 * CHUNKS)
                for part in range(2):
                    both = jnp.concatenate([pieces[0][part], pieces[1][part]], axis=0)
                    gp_ref[r, part * state:(part + 1) * state] = both.astype(BF16)
            return tuple(carry), tuple(sums)
        _, sums = lax.fori_loop(0, steps // 2, adjoint_pair, (tuple(carries), (zero,) * 4), unroll=1)

        b_part = dot(normed_ref[layer], gp_ref[...], TN)
        if planes:
            g_stage(2 * layer + 1, b_part, 0, 2 * state)
            g_start(2 * layer + 1)
            g_pipe(2 * layer)
            if layer == 0:
                g_plane(3)
                g_peers(2)
        else:
            r_["gpart"][layer, :, 0:2 * state] = b_part
        tmp_ref[...] = dot(gp_ref[...], matrix(layer, 0), NT)

        def input_tile(r, mask, carry):
            grad = (tmp_ref[r, :] + skip * gb_ref[r, :].astype(F32)) * mask
            xhat = xhat_ref[layer, r, :]
            rstd = jnp.concatenate([rstd_ref[layer, r, :]] * (model // 128), axis=1)
            scaled = grad * gain
            first = jnp.mean(scaled, axis=1, keepdims=True)
            second = jnp.mean(scaled * xhat, axis=1, keepdims=True)
            made = go_ref[r, :].astype(F32) + rstd * (scaled - first - xhat * second)
            go_ref[r, :] = made.astype(BF16)
            return carry + fold(grad * xhat)
        gain_sum = all_tiles(input_tile, zero_row)

        for at, value in enumerate((gain_sum, skip_sum, bias_sum)):
            small_ref[layer, at:at + 1, :] = jnp.sum(value, axis=0, keepdims=True)
        for at, value in enumerate(sums):
            small_ref[layer, 3 + at:4 + at, 0:state] = jnp.sum(value, axis=0, keepdims=True)
        if planes:
            s_start(layer)
            g_pipe(2 * layer + 1)
            s_pipe(layer)

    for q in range(seqs):
        xg_ref[q] = dot(gather, go_ref[seq_rows(q), :], NN).astype(BF16)
    if not planes:
        for copy in unsent:
            copy.wait_send()
        return
    g_peers(3)
    g_plane(0)
    s_plane(1)
    g_plane(1)
    s_plane(0)
    g_peers(0)
    g_peers(1)

    def store_small(layer):
        total = s_finish(layer)
        for at, name in enumerate(("gain_grad", "skip_grad", "bias_grad")):
            r_[name][layer:layer + 1, :] = total[at:at + 1, :]
        one = slice(layer, layer + 1)
        coef = (coef_all[0][one], coef_all[1][one])
        sums = [total[at:at + 1, 0:state] for at in range(3, 7)]
        scale = coef[0] * coef[0] + coef[1] * coef[1]
        coef_grad = cmul((sums[2], sums[3]), (coef[0] / scale, coef[1] / scale))
        made = discretize_grads(lre_ref[one], lim_ref[one], lst_ref[one], (sums[0], sums[1]), coef_grad)
        for name, value in zip(("lre_grad", "lim_grad", "lst_grad"), made):
            r_[name][one, :] = value

    def store_rest(layer):
        done = g_finish(2 * layer).astype(F32)
        coef = (coef_all[0][layer:layer + 1], coef_all[1][layer:layer + 1])
        turned = cmul(coef, (done[:, 0:state], done[:, state:2 * state]))
        r_["c_grad"][layer, :, 0:state] = turned[0]
        r_["c_grad"][layer, :, state:2 * state] = -turned[1]
        r_["glu_grad"][layer] = done[:, 2 * state:]

    store_small(1)
    store_rest(1)
    r_["b_grad"][1] = g_finish(3).astype(F32)
    store_small(0)
    store_rest(0)
    r_["b_grad"][0] = g_finish(1).astype(F32)
    for copy in unsent:
        copy.wait_send()


def run_main(planes, x_in, lengths, cotangent, norm_gain, lambda_re, lambda_im, log_step, skip_weight, glu_bias, weights):
    depth = lax.axis_size("pipe")
    seqs, pos, model = x_in.shape
    layers, state = lambda_re.shape
    rows = seqs * pos
    wide = 4 * state + model
    vmem = pl.BlockSpec(memory_space=pltpu.VMEM)
    smem = pl.BlockSpec(memory_space=pltpu.SMEM)
    ins = dict(x=x_in, cot=cotangent, len=lengths, gain=norm_gain, lre=lambda_re, lim=lambda_im, lst=log_step,
               skip=skip_weight, bias=glu_bias)
    ins.update(zip(("b", "c", "glu") if planes else ("w",), weights))
    outs = dict(out=(x_in.shape, BF16), xg=(x_in.shape, BF16))
    scratch = dict(
        h=pltpu.VMEM((layers + 1, rows, model), BF16),
        go=pltpu.VMEM((rows, model), BF16),
        xhat=pltpu.VMEM((layers, rows, model), F32),
        rstd=pltpu.VMEM((layers, rows, 128), F32),
        normed=pltpu.VMEM((layers, rows, model), BF16),
        p=pltpu.VMEM((layers, rows, 2 * state), F32),
        z=pltpu.VMEM((layers, rows + seqs * CHUNKS, 2 * state), F32),
        zb=pltpu.VMEM((layers, rows, 2 * state), BF16),
        dg=pltpu.VMEM((layers, rows, model), F32),
        gated=pltpu.VMEM((layers, rows, model), BF16),
        sig=pltpu.VMEM((layers, rows, model), F32),
        gg=pltpu.VMEM((rows, model), BF16),
        gb=pltpu.VMEM((rows, model), BF16),
        gp=pltpu.VMEM((rows, 2 * state), BF16),
        src=pltpu.VMEM((rows, 2 * state), F32),
        tmp=pltpu.VMEM((rows, model), F32),
        acc=pltpu.VMEM((rows, model), F32),
        ends=pltpu.VMEM((2 * layers, 8, 2 * state), F32),
        got=pltpu.VMEM((2 * layers, depth - 1, 8, 2 * state), F32),
        send=pltpu.SemaphoreType.DMA((2 * layers, depth - 1)),
        recv=pltpu.SemaphoreType.DMA((2 * layers, depth - 1)),
    )
    if planes:
        local = weights[0].shape[1]
        part = local // depth
        full, halves = (layers, model), (layers, state)
        outs.update(
            gain_grad=(full, F32), lre_grad=(halves, F32), lim_grad=(halves, F32), lst_grad=(halves, F32),
            b_grad=((layers, local, 2 * state), F32), c_grad=((layers, local, 2 * state), F32),
            skip_grad=(full, F32), glu_grad=((layers, local, model), F32), bias_grad=(full, F32),
        )
        scratch.update(
            small=pltpu.VMEM((layers, 8, model), F32),
            s_other=pltpu.VMEM((layers, 8, model), F32),
            s_quad=pltpu.VMEM((layers, depth, 8, model), F32),
            s_line=pltpu.VMEM((layers, planes, 8, model), F32),
            w=pltpu.VMEM((layers, planes, 2, depth, part, wide), BF16),
        )
        for kind, width in enumerate((2 * state + model, 2 * state)):
            scratch.update({
                f"part{kind}": pltpu.VMEM((layers, planes, 2, depth, part, width), BF16),
                f"other{kind}": pltpu.VMEM((layers, planes, depth, part, width), BF16),
                f"pair{kind}": pltpu.VMEM((layers, depth, planes, part, width), BF16),
                f"quad{kind}": pltpu.VMEM((layers, depth - 1, planes, part, width), BF16),
                f"line{kind}": pltpu.VMEM((layers, planes, part, width), BF16),
                f"came{kind}": pltpu.VMEM((layers, planes - 1, part, width), BF16),
                f"done{kind}": pltpu.VMEM((layers, depth, part, width), BF16),
            })
        for name, shape in dict(
            w=(3, planes * depth), g=(2 * layers, 2 * depth + planes - 2), s=(layers, depth + planes - 1)
        ).items():
            scratch[name + "_send"] = pltpu.SemaphoreType.DMA(shape)
            scratch[name + "_recv"] = pltpu.SemaphoreType.DMA(shape)
    else:
        outs.update(gpart=((layers, model, wide), F32), small=((layers, 8, model), F32))
    names = tuple(ins) + tuple(outs) + tuple(scratch)
    return pl.pallas_call(
        functools.partial(main_kernel, depth, planes, names),
        out_shape=tuple(jax.ShapeDtypeStruct(*o) for o in outs.values()),
        in_specs=[smem if name == "len" else vmem for name in ins],
        out_specs=(vmem,) * len(outs),
        scratch_shapes=list(scratch.values()),
        compiler_params=pltpu.CompilerParams(
            collective_id=0, has_side_effects=True, vmem_limit_bytes=60 * 2**20
        ),
    )(*ins.values())


def per_device(
    x_in, lengths, cotangent, norm_gain, lambda_re, lambda_im, log_step,
    b_weight, c_weight, skip_weight, glu_weight, glu_bias,
):
    depth, owners = lax.axis_size("pipe"), lax.axis_size("dp")
    state = lambda_re.shape[1]
    rest = (lambda_re, lambda_im, log_step, skip_weight, glu_bias)
    if b_weight.shape[1] % (16 * depth) == 0 and owners % 2 == 0:
        return run_main(owners // 2, x_in, lengths, cotangent, norm_gain, *rest, (b_weight, c_weight, glu_weight))
    _, _, coef = discretize(lambda_re, lambda_im, log_step)
    c_real, c_imag = c_weight[:, :, :state], c_weight[:, :, state:]
    turned = cmul((coef[0][:, None], coef[1][:, None]), (c_real, c_imag))
    shard = jnp.concatenate([b_weight, turned[0], -turned[1], glu_weight], axis=2).astype(BF16)
    weights = lax.all_gather(shard, "dp", axis=1, tiled=True)
    output, x_grad, gpart, small = run_main(
        0, x_in, lengths, cotangent, norm_gain, *rest, (weights,)
    )
    grads = lax.psum_scatter(gpart, "dp", scatter_dimension=1, tiled=True)
    grads = lax.psum(grads.astype(BF16), "pipe").astype(F32)
    small = lax.psum(small, ("pipe", "dp"))
    m_real, m_imag = grads[:, :, 2 * state:3 * state], grads[:, :, 3 * state:4 * state]
    turned = cmul((coef[0][:, None], coef[1][:, None]), (m_real, m_imag))
    c_grad = jnp.concatenate([turned[0], -turned[1]], axis=2)
    decay_grad = (small[:, 3, :state], small[:, 4, :state])
    scale = coef[0] * coef[0] + coef[1] * coef[1]
    coef_grad = cmul((small[:, 5, :state], small[:, 6, :state]), (coef[0] / scale, coef[1] / scale))
    lam_re_grad, lam_im_grad, step_grad = discretize_grads(lambda_re, lambda_im, log_step, decay_grad, coef_grad)
    return (
        output, x_grad, small[:, 0], lam_re_grad, lam_im_grad, step_grad,
        grads[:, :, :2 * state], c_grad, small[:, 1], grads[:, :, 4 * state:], small[:, 2],
    )


def solution(mesh):
    split, whole, rows = P("dp", "pipe", None), P(), P(None, "dp", None)
    return jax.shard_map(
        per_device,
        mesh=mesh,
        in_specs=(split, P("dp"), split, whole, whole, whole, whole, rows, rows, whole, rows, whole),
        out_specs=(split, split, whole, whole, whole, whole, rows, rows, whole, rows, whole),
        check_vma=False,
    )
```

```python
import functools

import jax
import jax.numpy as jnp
from jax import lax
from jax.experimental import pallas as pl
from jax.experimental.pallas import tpu as pltpu
from jax.sharding import PartitionSpec as P

EPSILON = 1e-05
CHUNKS = 8
TILE = 32
G1, C1, B1, G0, C0, B0 = range(6)
GRAD_ORDERS = (True, False, False, True, False, False)
MESH = pl.DeviceIdType.MESH
F32 = jnp.float32
BF16 = jnp.bfloat16
NN = (((1,), (0,)), ((), ()))
NT = (((1,), (1,)), ((), ()))
TN = (((0,), (0,)), ((), ()))


def cmul(u, v):
    return (u[0] * v[0] - u[1] * v[1], u[0] * v[1] + u[1] * v[0])


def conj(u):
    return (u[0], -u[1])


def dot(a, b, dims):
    return lax.dot_general(a, b, dims, preferred_element_type=F32)


def discretize(lam_re, lam_im, log_step):
    step = jnp.exp(log_step)
    radius = jnp.exp(lam_re * step)
    turn = lam_im * step
    decay = (radius * jnp.cos(turn), radius * jnp.sin(turn))
    modulus = lam_re * lam_re + lam_im * lam_im
    coef = (
        ((decay[0] - 1.0) * lam_re + decay[1] * lam_im) / modulus,
        (decay[1] * lam_re - (decay[0] - 1.0) * lam_im) / modulus,
    )
    return step, decay, coef


def discretize_grads(lam_re, lam_im, log_step, decay_grad, coef_grad):
    step, decay, coef = discretize(lam_re, lam_im, log_step)
    lam = (lam_re, lam_im)
    modulus = lam_re * lam_re + lam_im * lam_im
    inverse = (lam_re / modulus, -lam_im / modulus)
    through = cmul(coef_grad, conj(inverse))
    total = (decay_grad[0] + through[0], decay_grad[1] + through[1])
    first = cmul(total, (step * decay[0], -step * decay[1]))
    second = cmul(coef_grad, conj(cmul(coef, inverse)))
    turned = cmul(total, conj(cmul(lam, decay)))
    return first[0] - second[0], first[1] - second[1], step * turned[0]


def weight_gather(refs, pieces, depth, planes, me, plane, core, at_pipe, at_plane, at_core, remote):
    w_ref = refs["w"]
    sems = (refs["w_send"], refs["w_recv"])
    along, onward, across = {}, {}, {}

    def part(piece):
        layer, low, high = pieces[piece]
        return w_ref.at[layer], pl.ds(low, high - low)

    def send(piece):
        ref, cols = part(piece)
        along[piece] = []
        for k in range(1, planes):
            block = ref.at[plane, core, me, :, cols]
            along[piece].append(remote(block, block, sems, (piece, k - 1), at_plane(k)))

    def relay(piece):
        ref, cols = part(piece)
        onward[piece] = []
        for k in range(1, planes):
            along[piece][k - 1].wait_recv()
            block = ref.at[lax.rem(plane - k + planes, planes), core, me, :, cols]
            for j in range(1, depth):
                at = planes - 1 + (k - 1) * (depth - 1) + j - 1
                onward[piece].append(remote(block, block, sems, (piece, at), at_pipe(j)))

    def swap(piece):
        ref, cols = part(piece)
        for copy in onward[piece]:
            copy.wait_recv()
        block = ref.at[:, core, :, :, cols]
        across[piece] = remote(block, block, sems, (piece, planes * depth - 1), at_core)

    def ready(piece):
        across[piece].wait_recv()

    return send, relay, swap, ready


def gradient_sums(refs, orders, depth, planes, me, plane, core, at_pipe, at_plane, at_core, remote):
    sems = (refs["g_send"], refs["g_recv"])
    copies = {}
    pipe_axis, plane_axis = (depth, me, at_pipe), (planes, plane, at_plane)

    def axes(piece):
        return (plane_axis, pipe_axis) if orders[piece] else (pipe_axis, plane_axis)

    def start(piece, matrix):
        part, other = refs[f"part{piece}"], refs[f"other{piece}"]
        part[...] = matrix.astype(BF16).reshape(part.shape)
        copies[piece, 0] = remote(part.at[:, 1 - core], other, sems, (piece, 0), at_core)

    def first(piece):
        copies[piece, 0].wait_recv()
        part, other, pair, quad = (refs[f"{name}{piece}"] for name in ("part", "other", "pair", "quad"))

        def add(i, carry):
            z, j = lax.div(i, depth), lax.rem(i, depth)
            total = (part[z, core, j].astype(F32) + other[z, j].astype(F32)).astype(BF16)
            if orders[piece]:
                pair[z, j] = total
            else:
                pair[j, z] = total
            return carry
        lax.fori_loop(0, planes * depth, add, 0, unroll=4)
        count, here, there = axes(piece)[0]
        copies[piece, 1] = [
            remote(pair.at[lax.rem(here + k, count)], quad.at[k - 1], sems, (piece, k), there(k)) for k in range(1, count)
        ]

    def second(piece):
        pair, quad, line, came = (refs[f"{name}{piece}"] for name in ("pair", "quad", "line", "came"))
        for copy in copies[piece, 1]:
            copy.wait_recv()
        (count, here, _), (wide, there, go) = axes(piece)

        def add(i, carry):
            total = pair[here, i].astype(F32)
            for k in range(1, count):
                total = total + quad[k - 1, i].astype(F32)
            line[i] = total.astype(BF16)
            return carry
        lax.fori_loop(0, wide, add, 0, unroll=2)
        copies[piece, 2] = [
            remote(line.at[lax.rem(there + k, wide)], came.at[k - 1], sems, (piece, count - 1 + k), go(k))
            for k in range(1, wide)
        ]

    def third(piece):
        line, came, done = (refs[f"{name}{piece}"] for name in ("line", "came", "done"))
        for copy in copies[piece, 2]:
            copy.wait_recv()
        wide, there, _ = axes(piece)[1]
        total = line[there].astype(F32)
        for k in range(1, wide):
            total = total + came[k - 1].astype(F32)
        done[me] = total.astype(BF16)
        copies[piece, 3] = [
            remote(done.at[me], done.at[me], sems, (piece, depth + planes + k - 2), at_pipe(k)) for k in range(1, depth)
        ]

    def finish(piece):
        for copy in copies[piece, 3]:
            copy.wait_recv()
        done = refs[f"done{piece}"][...]
        return done.reshape(done.shape[0] * done.shape[1], done.shape[2]).astype(F32)

    return start, first, second, third, finish


def small_sums(refs, depth, planes, me, plane, core, at_pipe, at_plane, at_core, remote):
    sems = (refs["s_send"], refs["s_recv"])
    own, other, quad, line = refs["small"], refs["s_other"], refs["s_quad"], refs["s_line"]
    copies = {}

    def start(layer):
        copies[layer, 0] = remote(own.at[layer], other.at[layer], sems, (layer, 0), at_core)

    def to_pipe(layer):
        copies[layer, 0].wait_recv()
        quad[layer, me] = own[layer] + other[layer]
        copies[layer, 1] = [
            remote(quad.at[layer, me], quad.at[layer, me], sems, (layer, k), at_pipe(k)) for k in range(1, depth)
        ]

    def to_plane(layer):
        for copy in copies[layer, 1]:
            copy.wait_recv()
        total = quad[layer, 0]
        for j in range(1, depth):
            total = total + quad[layer, j]
        line[layer, plane] = total
        copies[layer, 2] = [
            remote(line.at[layer, plane], line.at[layer, plane], sems, (layer, depth + k - 1), at_plane(k))
            for k in range(1, planes)
        ]

    def finish(layer):
        for copy in copies[layer, 2]:
            copy.wait_recv()
        total = line[layer, 0]
        for z in range(1, planes):
            total = total + line[layer, z]
        return total

    return start, to_pipe, to_plane, finish


def main_kernel(depth, planes, names, *refs):
    r_ = dict(zip(names, refs))
    x_ref, cot_ref, len_ref, gain_ref = r_["x"], r_["cot"], r_["len"], r_["gain"]
    lre_ref, lim_ref, lst_ref, skip_ref, bias_ref = r_["lre"], r_["lim"], r_["lst"], r_["skip"], r_["bias"]
    small_ref = r_["small"]
    h_ref, go_ref, xhat_ref, rstd_ref, normed_ref = r_["h"], r_["go"], r_["xhat"], r_["rstd"], r_["normed"]
    p_ref, z_ref, zb_ref, dg_ref, gated_ref, sig_ref = r_["p"], r_["z"], r_["zb"], r_["dg"], r_["gated"], r_["sig"]
    gg_ref, gb_ref, gp_ref, src_ref, tmp_ref, acc_ref = r_["gg"], r_["gb"], r_["gp"], r_["src"], r_["tmp"], r_["acc"]
    ends_ref, got_ref, send_sems, recv_sems = r_["ends"], r_["got"], r_["send"], r_["recv"]
    w_ref = r_["w"]
    seqs, pos, model = x_ref.shape
    state = lre_ref.shape[1]
    layers = gain_ref.shape[0]
    rows = seqs * pos
    steps = pos // CHUNKS
    me, dp = lax.axis_index("pipe"), lax.axis_index("dp")
    plane, core = lax.div(dp, 2), lax.rem(dp, 2)

    def peer(k):
        return lax.rem(me + k, depth)

    def at_pipe(k):
        return (peer(k), dp)

    def at_plane(k):
        return (me, 2 * lax.rem(plane + k, planes) + core)

    at_core = (me, 2 * plane + (1 - core))
    others = [at_pipe(k) for k in range(1, depth)]
    if planes:
        others += [at_plane(k) for k in range(1, planes)] + [at_core]
    barrier = pltpu.get_barrier_semaphore()
    for device in others:
        pl.semaphore_signal(barrier, inc=1, device_id=device, device_id_type=MESH)

    unsent = []

    def remote(src, dst, sems, at, device):
        copy = pltpu.make_async_remote_copy(
            src_ref=src, dst_ref=dst, send_sem=sems[0].at[at], recv_sem=sems[1].at[at],
            device_id=device, device_id_type=MESH,
        )
        copy.start()
        unsent.append(copy)
        return copy

    row = lax.broadcasted_iota(jnp.int32, (pos, pos), 0)
    col = lax.broadcasted_iota(jnp.int32, (pos, pos), 1)
    spread = (lax.rem(row, CHUNKS) * steps + lax.div(row, CHUNKS) == col).astype(F32).astype(BF16)
    masks = [(len_ref[q] > me * pos).astype(F32) for q in range(seqs)]
    sublane = lax.broadcasted_iota(jnp.int32, (CHUNKS, state), 0)

    def seq_rows(q):
        return pl.ds(q * pos, pos)

    def tiles(body, q, init=0, unroll=1):
        def step(i, carry):
            return body(pl.ds(pl.multiple_of(q * pos + i * TILE, TILE), TILE), masks[q], carry)
        return lax.fori_loop(0, pos // TILE, step, init, unroll=unroll)

    def all_tiles(body, init=0, unroll=2):
        for q in range(seqs):
            init = tiles(body, q, init, unroll)
        return init

    def fold(value):
        total = value[0:8]
        for r in range(8, value.shape[0], 8):
            total = total + value[r:r + 8]
        return total

    fetches = {}
    for at, name in enumerate(("b", "x", "c", "glu", "cot") if planes else ("x", "cot")):
        fetches[name] = pltpu.make_async_copy(r_[name], r_[name + "_here"], r_["fetch"].at[at])
        fetches[name].start()
    x_here, cot_here = r_["x_here"], r_["cot_here"]
    step_all, decay_all, coef_all = discretize(lre_ref[...], lim_ref[...], lst_ref[...])
    if planes:
        ways = (depth, planes, me, plane, core, at_pipe, at_plane, at_core, remote)
        wide = 4 * state + model
        pieces = ((0, 0, 2 * state), (0, 2 * state, wide), (1, 0, 2 * state), (1, 2 * state, wide))
        w_send, w_relay, w_swap, w_ready = weight_gather(r_, pieces, *ways)
        g_start, g_first, g_second, g_third, g_finish = gradient_sums(r_, GRAD_ORDERS, *ways)
        s_start, s_pipe, s_plane, s_finish = small_sums(r_, *ways)

        def keep(layer, matrix, low):
            high = low + matrix.shape[1]
            w_ref[layer, plane, core, :, :, low:high] = matrix.astype(BF16).reshape(depth, -1, high - low)

        fetches["b"].wait()
        for layer in range(layers):
            keep(layer, r_["b_here"][layer], 0)
    pl.semaphore_wait(barrier, len(others))
    if planes:
        w_send(0)
        fetches["c"].wait()
        fetches["glu"].wait()
        for layer in range(layers):
            coef = (coef_all[0][layer:layer + 1], coef_all[1][layer:layer + 1])
            turned = cmul(coef, (r_["c_here"][layer, :, 0:state], r_["c_here"][layer, :, state:2 * state]))
            keep(layer, turned[0], 2 * state)
            keep(layer, -turned[1], 3 * state)
            keep(layer, r_["glu_here"][layer], 4 * state)
        w_send(1)
        w_send(2)
        w_send(3)
    fetches["x"].wait()
    for q in range(seqs):
        h_ref[0, seq_rows(q), :] = dot(spread, x_here[q], NN).astype(BF16)

    def matrix(layer, which):
        low, high = (0, 2 * state, 4 * state)[which], (2 * state, 4 * state, w_ref.shape[-1])[which]
        value = w_ref[layer, ..., low:high]
        return value.reshape(model, high - low)

    def complex_rows(src, r):
        return (src[r, 0:state], src[r, state:2 * state])

    zero = jnp.zeros((CHUNKS, state), F32)

    def scan_ends(src, decay, down):
        def step(i, carry):
            s = (steps - 1 - i) if down else i
            made = []
            for q in range(seqs):
                r = pl.ds(pl.multiple_of(q * pos + s * CHUNKS, CHUNKS), CHUNKS)
                add = complex_rows(src, r)
                moved = cmul(decay, carry[q])
                made.append((moved[0] + add[0], moved[1] + add[1]))
            return tuple(made)
        return lax.fori_loop(0, steps, step, ((zero, zero),) * seqs, unroll=4)

    def shifted(value, k, down):
        rolled = pltpu.roll(value, CHUNKS - k if down else k, axis=0)
        keep = (sublane < CHUNKS - k) if down else (sublane >= k)
        return jnp.where(keep, rolled, 0.0)

    def squared(value, times):
        for _ in range(times):
            value = cmul(value, value)
        return value

    lanes = 128
    spans = state // lanes

    def chunk_powers(layer):
        powers = [squared(wide_decay(layer), steps.bit_length() - 1)]
        while len(powers) < CHUNKS.bit_length():
            powers.append(cmul(powers[-1], powers[-1]))
        return powers

    def place_table(powers, down):
        place = (CHUNKS - 1 - sublane) if down else sublane
        table = (jnp.ones((CHUNKS, state), F32), zero)
        for bit, factor in enumerate(powers[:-1]):
            moved = cmul(table, factor)
            take = lax.rem(lax.div(place, 1 << bit), 2) == 1
            table = (jnp.where(take, moved[0], table[0]), jnp.where(take, moved[1], table[1]))
        return table

    def start_exchange(number, ends, powers, down):
        sums = list(ends)
        for bit, jump in enumerate(powers[:-1]):
            for q in range(seqs):
                moved = cmul(jump, (shifted(sums[q][0], 1 << bit, down), shifted(sums[q][1], 1 << bit, down)))
                sums[q] = (sums[q][0] + moved[0], sums[q][1] + moved[1])
        last = 0 if down else CHUNKS - 1
        for q in range(seqs):
            for part in range(2):
                for j in range(spans):
                    at = (q * 2 + part) * spans + j
                    ends_ref[number, at:at + 1, :] = sums[q][part][last:last + 1, j * lanes:(j + 1) * lanes]
        copies = [
            remote(ends_ref.at[number], got_ref.at[number, k - 1], (send_sems, recv_sems), (number, k - 1),
                   at_pipe(depth - k if down else k))
            for k in range(1, depth)
        ]
        return copies, sums

    def finish_exchange(number, pending, powers, down):
        copies, sums = pending
        table = place_table(powers, down)
        exclusive = [(shifted(s[0], 1, down), shifted(s[1], 1, down)) for s in sums]
        for copy in copies:
            copy.wait_recv()
        jump = powers[-1]
        carries = []
        for q in range(seqs):
            total, factor = (zero, zero), (jnp.ones((CHUNKS, state), F32), zero)
            for k in range(1, depth):
                there = ((me + k < depth) if down else (me - k >= 0)).astype(F32)
                came = []
                for part in range(2):
                    at = (q * 2 + part) * spans
                    pieces_ = [
                        jnp.broadcast_to(got_ref[number, k - 1, at + j:at + j + 1, :], (CHUNKS, lanes))
                        for j in range(spans)
                    ]
                    came.append(jnp.concatenate(pieces_, axis=1) * there)
                moved = cmul(factor, came)
                total = (total[0] + moved[0], total[1] + moved[1])
                factor = cmul(factor, jump)
            moved = cmul(table, total)
            carries.append((exclusive[q][0] + moved[0], exclusive[q][1] + moved[1]))
        return carries

    def wide_decay(layer):
        return tuple(jnp.broadcast_to(part[layer:layer + 1], (CHUNKS, state)) for part in decay_all)

    small_ref[...] = jnp.zeros_like(small_ref)
    powers_of = [chunk_powers(layer) for layer in range(layers)]

    def back_powers(layer):
        return [conj(power) for power in powers_of[layer]]

    for layer in range(layers):
        down = layer % 2 == 1
        decay = wide_decay(layer)
        gain = gain_ref[layer:layer + 1, :]
        skip = skip_ref[layer:layer + 1, :]
        bias = bias_ref[layer:layer + 1, :]

        def norm_tile(r, mask, carry):
            h = h_ref[layer, r, :].astype(F32)
            mean = jnp.mean(h, axis=1, keepdims=True)
            centred = h - mean
            spread_ = jnp.mean(centred * centred, axis=1, keepdims=True)
            rstd = lax.rsqrt(spread_ + EPSILON)
            xhat = centred * rstd
            xhat_ref[layer, r, :] = xhat
            rstd_ref[layer, r, :] = jnp.broadcast_to(rstd, (TILE, 128))
            normed_ref[layer, r, :] = (xhat * gain * mask).astype(BF16)
            return carry
        all_tiles(norm_tile, unroll=4)

        if layer == 0:
            if planes:
                w_relay(0)
            fetches["cot"].wait()
            for q in range(seqs):
                go_ref[seq_rows(q), :] = dot(spread, cot_here[q], NN).astype(BF16)
        if planes and layer == 0:
            w_relay(1)
            w_swap(0)
            w_ready(0)
        if planes and layer == 1:
            w_ready(2)
        p_ref[layer] = dot(normed_ref[layer], matrix(layer, 0), NN)
        ends = scan_ends(p_ref.at[layer], decay, down)
        pending = start_exchange(layer, ends, powers_of[layer], down)
        if planes and layer == 0:
            w_relay(2)
            w_relay(3)
            w_swap(1)
        if planes and layer == 1:
            w_swap(3)
        carries = finish_exchange(layer, pending, powers_of[layer], down)
        pad = pos + CHUNKS
        for q in range(seqs):
            at = q * pad + (pos if down else 0)
            z_ref[layer, at:at + CHUNKS, 0:state] = carries[q][0]
            z_ref[layer, at:at + CHUNKS, state:2 * state] = carries[q][1]

        def state_pair(i, carry):
            carry = list(carry)
            for q in range(seqs):
                pieces = []
                for half in range(2):
                    s = (steps - 1 - 2 * i - half) if down else 2 * i + half
                    r = pl.ds(pl.multiple_of(q * pos + s * CHUNKS, CHUNKS), CHUNKS)
                    add = complex_rows(p_ref.at[layer], r)
                    moved = cmul(decay, carry[q])
                    carry[q] = (moved[0] + add[0], moved[1] + add[1])
                    r = pl.ds(pl.multiple_of(q * pad + (s + (0 if down else 1)) * CHUNKS, CHUNKS), CHUNKS)
                    z_ref[layer, r, 0:state] = carry[q][0]
                    z_ref[layer, r, state:2 * state] = carry[q][1]
                    pieces.append(carry[q])
                if down:
                    pieces = pieces[::-1]
                low = (steps - 2 - 2 * i) if down else 2 * i
                r = pl.ds(pl.multiple_of(q * pos + low * CHUNKS, 2 * CHUNKS), 2 * CHUNKS)
                for part in range(2):
                    both = jnp.concatenate([pieces[0][part], pieces[1][part]], axis=0)
                    zb_ref[layer, r, part * state:(part + 1) * state] = both.astype(BF16)
            return tuple(carry)
        lax.fori_loop(0, steps // 2, state_pair, tuple(carries), unroll=2)

        if planes:
            w_ready(2 * layer + 1)
        tmp_ref[...] = dot(zb_ref[layer], matrix(layer, 1), NT)

        def gelu_tile(r, mask, carry):
            before = tmp_ref[r, :] + skip * normed_ref[layer, r, :].astype(F32)
            phi = 0.5 * (1.0 + lax.erf(before * 0.7071067811865476))
            dg_ref[layer, r, :] = phi + before * (0.3989422804014327 * jnp.exp(-0.5 * before * before))
            gated_ref[layer, r, :] = (before * phi).astype(BF16)
            return carry
        all_tiles(gelu_tile)

        tmp_ref[...] = dot(gated_ref[layer], matrix(layer, 2), NN)

        def out_tile(r, mask, carry):
            sig = 1.0 / (1.0 + jnp.exp(-(tmp_ref[r, :] + bias)))
            sig_ref[layer, r, :] = sig
            made = h_ref[layer, r, :].astype(F32) + mask * (gated_ref[layer, r, :].astype(F32) * sig)
            h_ref[layer + 1, r, :] = made.astype(BF16)
            return carry
        if planes and layer == 0:
            w_swap(2)
        all_tiles(out_tile)

    puts = []

    def put(name, at=None):
        source, target = r_[name + "_here"], r_[name]
        if at is not None:
            source, target = source.at[at], target.at[at]
        copy = pltpu.make_async_copy(source, target, r_["put"].at[len(puts)])
        copy.start()
        puts.append(copy)

    gather = (lax.rem(row, steps) * CHUNKS + lax.div(row, steps) == col).astype(F32).astype(BF16)
    for q in range(seqs):
        r_["out_here"][q] = dot(gather, h_ref[layers, seq_rows(q), :], NN).astype(BF16)
    put("out")

    for layer in reversed(range(layers)):
        down = layer % 2 == 1
        decay = wide_decay(layer)
        gain = gain_ref[layer:layer + 1, :]
        skip = skip_ref[layer:layer + 1, :]
        zero_row = jnp.zeros((8, model), F32)

        def gate_tile(r, mask, carry):
            sig = sig_ref[layer, r, :]
            branch = mask * go_ref[r, :].astype(F32) * sig
            grad = (branch * gated_ref[layer, r, :].astype(F32) * (1.0 - sig)).astype(BF16)
            gg_ref[r, :] = grad
            acc_ref[r, :] = branch
            return carry + fold(grad.astype(F32))
        bias_sum = all_tiles(gate_tile, zero_row)
        if planes and layer == 0:
            g_start(G0, dot(gated_ref[layer], gg_ref[...], TN))
        tmp_ref[...] = dot(gg_ref[...], matrix(layer, 2), NT)

        def before_tile(r, mask, carry):
            gated_grad = (acc_ref[r, :] + tmp_ref[r, :]).astype(BF16).astype(F32)
            grad = (gated_grad * dg_ref[layer, r, :]).astype(BF16)
            gb_ref[r, :] = grad
            return carry + fold(grad.astype(F32) * normed_ref[layer, r, :].astype(F32))
        skip_sum = all_tiles(before_tile, zero_row)

        if planes and layer == 0:
            g_first(G0)
        src_ref[...] = dot(gb_ref[...], matrix(layer, 1), NN)
        back = conj(decay)
        ends = scan_ends(src_ref, back, not down)
        pending = start_exchange(layers + layer, ends, back_powers(layer), not down)
        if planes and layer == 0:
            g_first(B1)
        c_part = dot(gb_ref[...], zb_ref[layer], TN)
        if not planes:
            r_["gpart"][layer, :, 4 * state:] = dot(gated_ref[layer], gg_ref[...], TN)
            r_["gpart"][layer, :, 2 * state:4 * state] = c_part
        elif layer == 1:
            g_start(C1, c_part)
            g_start(G1, dot(gated_ref[layer], gg_ref[...], TN))
            g_first(C1)
        else:
            g_start(C0, c_part)
            g_second(C1)
            s_pipe(1)
            g_first(C0)
        carries = finish_exchange(layers + layer, pending, back_powers(layer), not down)

        def adjoint_pair(i, loop):
            carry, sums = list(loop[0]), list(loop[1])
            for q in range(seqs):
                pieces = []
                for half in range(2):
                    s = 2 * i + half if down else (steps - 1 - 2 * i - half)
                    r = pl.ds(pl.multiple_of(q * pos + s * CHUNKS, CHUNKS), CHUNKS)
                    add = complex_rows(src_ref, r)
                    moved = cmul(back, carry[q])
                    adj = (moved[0] + add[0], moved[1] + add[1])
                    carry[q] = adj
                    pieces.append(adj)
                    proj = complex_rows(p_ref.at[layer], r)
                    r = pl.ds(pl.multiple_of(q * pad + (s + (1 if down else 0)) * CHUNKS, CHUNKS), CHUNKS)
                    prior = complex_rows(z_ref.at[layer], r)
                    sums[0] = sums[0] + (adj[0] * prior[0] + adj[1] * prior[1])
                    sums[1] = sums[1] + (adj[1] * prior[0] - adj[0] * prior[1])
                    sums[2] = sums[2] + (adj[0] * proj[0] + adj[1] * proj[1])
                    sums[3] = sums[3] + (adj[1] * proj[0] - adj[0] * proj[1])
                if not down:
                    pieces = pieces[::-1]
                low = 2 * i if down else (steps - 2 - 2 * i)
                r = pl.ds(pl.multiple_of(q * pos + low * CHUNKS, 2 * CHUNKS), 2 * CHUNKS)
                for part in range(2):
                    both = jnp.concatenate([pieces[0][part], pieces[1][part]], axis=0)
                    gp_ref[r, part * state:(part + 1) * state] = both.astype(BF16)
            return tuple(carry), tuple(sums)
        _, sums = lax.fori_loop(0, steps // 2, adjoint_pair, (tuple(carries), (zero,) * 4), unroll=1)

        b_part = dot(normed_ref[layer], gp_ref[...], TN)
        if not planes:
            r_["gpart"][layer, :, 0:2 * state] = b_part
        elif layer == 1:
            g_start(B1, b_part)
            g_first(G1)
        else:
            g_start(B0, b_part)
        tmp_ref[...] = dot(gp_ref[...], matrix(layer, 0), NT)
        if planes and layer == 0:
            g_first(B0)
            g_second(G1)

        def input_tile(r, mask, carry):
            grad = (tmp_ref[r, :] + skip * gb_ref[r, :].astype(F32)) * mask
            xhat = xhat_ref[layer, r, :]
            rstd = jnp.concatenate([rstd_ref[layer, r, :]] * (model // 128), axis=1)
            scaled = grad * gain
            first = jnp.mean(scaled, axis=1, keepdims=True)
            second = jnp.mean(scaled * xhat, axis=1, keepdims=True)
            made = go_ref[r, :].astype(F32) + rstd * (scaled - first - xhat * second)
            go_ref[r, :] = made.astype(BF16)
            return carry + fold(grad * xhat)
        gain_sum = all_tiles(input_tile, zero_row, unroll=4)

        for at, value in enumerate((gain_sum, skip_sum, bias_sum)):
            small_ref[layer, at:at + 1, :] = jnp.sum(value, axis=0, keepdims=True)
        for at, value in enumerate(sums):
            small_ref[layer, 3 + at:4 + at, 0:state] = jnp.sum(value, axis=0, keepdims=True)
        if planes:
            s_start(layer)

    for q in range(seqs):
        r_["xg_here"][q] = dot(gather, go_ref[seq_rows(q), :], NN).astype(BF16)
    put("xg")
    if planes:
        def store_small(layer):
            total = s_finish(layer)
            for at, name in enumerate(("gain_grad", "skip_grad", "bias_grad")):
                r_[name][layer:layer + 1, :] = total[at:at + 1, :]
            one = slice(layer, layer + 1)
            coef = (coef_all[0][one], coef_all[1][one])
            sums = [total[at:at + 1, 0:state] for at in range(3, 7)]
            scale = coef[0] * coef[0] + coef[1] * coef[1]
            coef_grad = cmul((sums[2], sums[3]), (coef[0] / scale, coef[1] / scale))
            made = discretize_grads(lre_ref[one], lim_ref[one], lst_ref[one], (sums[0], sums[1]), coef_grad)
            for name, value in zip(("lre_grad", "lim_grad", "lst_grad"), made):
                r_[name][one, :] = value

        def store_b(layer, piece):
            r_["b_grad_here"][layer] = g_finish(piece)
            put("b_grad", layer)

        def store_c(layer, piece):
            coef = (coef_all[0][layer:layer + 1], coef_all[1][layer:layer + 1])
            done = g_finish(piece)
            turned = cmul(coef, (done[:, 0:state], done[:, state:2 * state]))
            r_["c_grad_here"][layer, :, 0:state] = turned[0]
            r_["c_grad_here"][layer, :, state:2 * state] = -turned[1]
            put("c_grad", layer)

        def store_glu(layer, piece):
            r_["glu_grad_here"][layer] = g_finish(piece)
            put("glu_grad", layer)

        s_pipe(0)
        s_plane(1)
        g_second(B1)
        g_third(C1)
        g_second(G0)
        g_second(C0)
        g_third(G1)
        g_second(B0)
        s_plane(0)
        g_third(B1)
        g_third(G0)
        store_small(1)
        store_c(1, C1)
        store_glu(1, G1)
        g_third(C0)
        store_b(1, B1)
        g_third(B0)
        store_small(0)
        store_glu(0, G0)
        store_c(0, C0)
        store_b(0, B0)
    for copy in puts:
        copy.wait()
    for copy in unsent:
        copy.wait_send()


def copy_kernel(*refs):
    count = (len(refs) - 2) // 3
    sources, targets, held, (in_sems, out_sems) = refs[:count], refs[count:2 * count], refs[2 * count:3 * count], refs[3 * count:]
    arrive = [pltpu.make_async_copy(sources[i], held[i], in_sems.at[i]) for i in range(count)]
    leave = [pltpu.make_async_copy(held[i], targets[i], out_sems.at[i]) for i in range(count)]
    for copy in arrive:
        copy.start()
    for first, then in zip(arrive, leave):
        first.wait()
        then.start()
    for copy in leave:
        copy.wait()


def copied(results):
    anywhere = pl.BlockSpec(memory_space=pl.ANY)
    return pl.pallas_call(
        copy_kernel,
        out_shape=tuple(jax.ShapeDtypeStruct(r.shape, r.dtype) for r in results),
        in_specs=[anywhere] * len(results),
        out_specs=(anywhere,) * len(results),
        scratch_shapes=[pltpu.VMEM(r.shape, r.dtype) for r in results] + [pltpu.SemaphoreType.DMA((len(results),))] * 2,
        compiler_params=pltpu.CompilerParams(vmem_limit_bytes=60 * 2**20),
    )(*results)


def run_main(planes, x_in, lengths, cotangent, norm_gain, lambda_re, lambda_im, log_step, skip_weight, glu_bias, weights):
    depth = lax.axis_size("pipe")
    seqs, pos, model = x_in.shape
    layers, state = lambda_re.shape
    rows = seqs * pos
    wide = 4 * state + model
    message = -(-seqs * 2 * state // (8 * 128)) * 8
    vmem = pl.BlockSpec(memory_space=pltpu.VMEM)
    smem = pl.BlockSpec(memory_space=pltpu.SMEM)
    anywhere = pl.BlockSpec(memory_space=pl.ANY)
    ins = dict(x=x_in, cot=cotangent, len=lengths, gain=norm_gain, lre=lambda_re, lim=lambda_im, lst=log_step,
               skip=skip_weight, bias=glu_bias)
    ins.update(zip(("b", "c", "glu") if planes else ("w",), weights))
    outs = dict(out=(x_in.shape, BF16), xg=(x_in.shape, BF16))
    scratch = dict(
        h=pltpu.VMEM((layers + 1, rows, model), BF16),
        go=pltpu.VMEM((rows, model), BF16),
        xhat=pltpu.VMEM((layers, rows, model), F32),
        rstd=pltpu.VMEM((layers, rows, 128), F32),
        normed=pltpu.VMEM((layers, rows, model), BF16),
        p=pltpu.VMEM((layers, rows, 2 * state), F32),
        z=pltpu.VMEM((layers, rows + seqs * CHUNKS, 2 * state), F32),
        zb=pltpu.VMEM((layers, rows, 2 * state), BF16),
        dg=pltpu.VMEM((layers, rows, model), F32),
        gated=pltpu.VMEM((layers, rows, model), BF16),
        sig=pltpu.VMEM((layers, rows, model), F32),
        gg=pltpu.VMEM((rows, model), BF16),
        gb=pltpu.VMEM((rows, model), BF16),
        gp=pltpu.VMEM((rows, 2 * state), BF16),
        src=pltpu.VMEM((rows, 2 * state), F32),
        tmp=pltpu.VMEM((rows, model), F32),
        acc=pltpu.VMEM((rows, model), F32),
        ends=pltpu.VMEM((2 * layers, message, 128), F32),
        got=pltpu.VMEM((2 * layers, depth - 1, message, 128), F32),
        fetch=pltpu.SemaphoreType.DMA((5,)),
        put=pltpu.SemaphoreType.DMA((8,)),
        send=pltpu.SemaphoreType.DMA((2 * layers, depth - 1)),
        recv=pltpu.SemaphoreType.DMA((2 * layers, depth - 1)),
    )
    if planes:
        local = weights[0].shape[1]
        part = local // depth
        full, halves = (layers, model), (layers, state)
        outs.update(
            gain_grad=(full, F32), lre_grad=(halves, F32), lim_grad=(halves, F32), lst_grad=(halves, F32),
            b_grad=((layers, local, 2 * state), F32), c_grad=((layers, local, 2 * state), F32),
            skip_grad=(full, F32), glu_grad=((layers, local, model), F32), bias_grad=(full, F32),
        )
        scratch.update(
            small=pltpu.VMEM((layers, 8, model), F32),
            s_other=pltpu.VMEM((layers, 8, model), F32),
            s_quad=pltpu.VMEM((layers, depth, 8, model), F32),
            s_line=pltpu.VMEM((layers, planes, 8, model), F32),
            w=pltpu.VMEM((layers, planes, 2, depth, part, wide), BF16),
        )
        for piece, first_plane in enumerate(GRAD_ORDERS):
            width = model if piece in (G0, G1) else 2 * state
            count, other = (planes, depth) if first_plane else (depth, planes)
            scratch.update({
                f"part{piece}": pltpu.VMEM((planes, 2, depth, part, width), BF16),
                f"other{piece}": pltpu.VMEM((planes, depth, part, width), BF16),
                f"pair{piece}": pltpu.VMEM((count, other, part, width), BF16),
                f"quad{piece}": pltpu.VMEM((count - 1, other, part, width), BF16),
                f"line{piece}": pltpu.VMEM((other, part, width), BF16),
                f"came{piece}": pltpu.VMEM((other - 1, part, width), BF16),
                f"done{piece}": pltpu.VMEM((depth, part, width), BF16),
            })
        for name, shape in dict(
            w=(4, planes * depth), g=(6, 2 * depth + planes - 2), s=(layers, depth + planes - 1)
        ).items():
            scratch[name + "_send"] = pltpu.SemaphoreType.DMA(shape)
            scratch[name + "_recv"] = pltpu.SemaphoreType.DMA(shape)
    else:
        outs.update(gpart=((layers, model, wide), F32), small=((layers, 8, model), F32))
    fetched = ("x", "cot", "b", "c", "glu") if planes else ("x", "cot")
    for name in fetched:
        scratch[name + "_here"] = pltpu.VMEM(ins[name].shape, ins[name].dtype)
    stored = ("out", "xg", "b_grad", "c_grad", "glu_grad") if planes else ("out", "xg")
    for name in stored:
        scratch[name + "_here"] = pltpu.VMEM(*outs[name])
    names = tuple(ins) + tuple(outs) + tuple(scratch)
    return pl.pallas_call(
        functools.partial(main_kernel, depth, planes, names),
        out_shape=tuple(jax.ShapeDtypeStruct(*o) for o in outs.values()),
        in_specs=[smem if name == "len" else anywhere if name in fetched else vmem for name in ins],
        out_specs=tuple(anywhere if name in stored else vmem for name in outs),
        scratch_shapes=list(scratch.values()),
        compiler_params=pltpu.CompilerParams(
            collective_id=0, has_side_effects=True, vmem_limit_bytes=60 * 2**20
        ),
    )(*ins.values())


def per_device(
    x_in, lengths, cotangent, norm_gain, lambda_re, lambda_im, log_step,
    b_weight, c_weight, skip_weight, glu_weight, glu_bias,
):
    depth, owners = lax.axis_size("pipe"), lax.axis_size("dp")
    state = lambda_re.shape[1]
    rest = (lambda_re, lambda_im, log_step, skip_weight, glu_bias)
    if b_weight.shape[1] % (16 * depth) == 0 and owners % 2 == 0:
        return copied(run_main(owners // 2, x_in, lengths, cotangent, norm_gain, *rest, (b_weight, c_weight, glu_weight)))
    _, _, coef = discretize(lambda_re, lambda_im, log_step)
    c_real, c_imag = c_weight[:, :, :state], c_weight[:, :, state:]
    turned = cmul((coef[0][:, None], coef[1][:, None]), (c_real, c_imag))
    shard = jnp.concatenate([b_weight, turned[0], -turned[1], glu_weight], axis=2).astype(BF16)
    weights = lax.all_gather(shard, "dp", axis=1, tiled=True)
    output, x_grad, gpart, small = run_main(
        0, x_in, lengths, cotangent, norm_gain, *rest, (weights,)
    )
    grads = lax.psum_scatter(gpart, "dp", scatter_dimension=1, tiled=True)
    grads = lax.psum(grads.astype(BF16), "pipe").astype(F32)
    small = lax.psum(small, ("pipe", "dp"))
    m_real, m_imag = grads[:, :, 2 * state:3 * state], grads[:, :, 3 * state:4 * state]
    turned = cmul((coef[0][:, None], coef[1][:, None]), (m_real, m_imag))
    c_grad = jnp.concatenate([turned[0], -turned[1]], axis=2)
    decay_grad = (small[:, 3, :state], small[:, 4, :state])
    scale = coef[0] * coef[0] + coef[1] * coef[1]
    coef_grad = cmul((small[:, 5, :state], small[:, 6, :state]), (coef[0] / scale, coef[1] / scale))
    lam_re_grad, lam_im_grad, step_grad = discretize_grads(lambda_re, lambda_im, log_step, decay_grad, coef_grad)
    return (
        output, x_grad, small[:, 0], lam_re_grad, lam_im_grad, step_grad,
        grads[:, :, :2 * state], c_grad, small[:, 1], grads[:, :, 4 * state:], small[:, 2],
    )


def solution(mesh):
    split, whole, rows = P("dp", "pipe", None), P(), P(None, "dp", None)
    return jax.shard_map(
        per_device,
        mesh=mesh,
        in_specs=(split, P("dp"), split, whole, whole, whole, whole, rows, rows, whole, rows, whole),
        out_specs=(split, split, whole, whole, whole, whole, rows, rows, whole, rows, whole),
        check_vma=False,
    )
```

```python
import functools

import jax
import jax.numpy as jnp
from jax import lax
from jax.experimental import pallas as pl
from jax.experimental.pallas import tpu as pltpu
from jax.sharding import PartitionSpec as P

EPSILON = 1e-05
CHUNKS = 8
TILE = 64
X, COT, NORM, PROJ, ENDS, SCAN, CDOT, GELU, GDOT, OUT, RESULT, GATE, GBACK, BEFORE, SRC, BENDS, BSCAN, CGRAD, GGRAD, BGRAD, XDOT, BNORM, XG = range(23)
FOLD, WSEND, WRELAY, WFORWARD, WSWAP, WREADY, FIRST, MIDDLE, SECOND, THIRD, FOURTH, SAVE, SSTART, SPIPE, SPLANE, SSAVE = range(23, 39)
ORDER = (
    (WSEND, 1), (X, 0), (WSEND, 0), (FOLD, 0), (FOLD, 1), (WSEND, 4), (WSEND, 3), (WRELAY, 1), (WRELAY, 0),
    (WSEND, 2), (WRELAY, 4), (WSWAP, 1), (WSEND, 6), (WRELAY, 3), (WSWAP, 0), (WSEND, 5), (COT, 0), (WRELAY, 2),
    (WFORWARD, 4), (WFORWARD, 3), (WREADY, 1), (WREADY, 0), (NORM, 0), (PROJ, 0), (ENDS, 0), (WFORWARD, 2),
    (WSWAP, 4), (WRELAY, 5), (WSWAP, 3), (WREADY, 3), (WSWAP, 2), (WRELAY, 6), (WREADY, 4), (SCAN, 0), (WREADY, 2),
    (CDOT, 0), (GELU, 0), (WFORWARD, 5), (GDOT, 0), (OUT, 0), (NORM, 1), (PROJ, 1), (ENDS, 1), (WSWAP, 5), (WSWAP, 6),
    (WREADY, 6), (WREADY, 5), (SCAN, 1), (CDOT, 1), (GELU, 1), (GDOT, 1), (OUT, 1), (GATE, 1), (GBACK, 1),
    (BEFORE, 1), (SRC, 1), (BENDS, 1), (CGRAD, 1), (GGRAD, 1), (FIRST, 0), (FIRST, 1), (BSCAN, 1), (XDOT, 1),
    (BGRAD, 1), (BNORM, 1), (GATE, 0), (GGRAD, 0), (GBACK, 0), (MIDDLE, 0), (BEFORE, 0), (FIRST, 2), (CGRAD, 0),
    (FIRST, 3), (SRC, 0), (BENDS, 0), (FIRST, 4), (SECOND, 0), (MIDDLE, 1), (MIDDLE, 2), (BSCAN, 0), (BGRAD, 0),
    (SSTART, 1), (MIDDLE, 4), (SECOND, 1), (FIRST, 5), (FIRST, 6), (XDOT, 0), (SECOND, 2), (SECOND, 3), (BNORM, 0),
    (SSTART, 0), (SECOND, 4), (SPIPE, 0), (THIRD, 1), (SPIPE, 1), (SECOND, 5), (THIRD, 0), (SECOND, 6), (THIRD, 2),
    (THIRD, 3), (SPLANE, 0), (FOURTH, 1), (XG, 0), (THIRD, 4), (SPLANE, 1), (FOURTH, 0), (THIRD, 5), (FOURTH, 2),
    (FOURTH, 3), (THIRD, 6), (FOURTH, 4), (SSAVE, 0), (RESULT, 0), (SAVE, 0), (SAVE, 2), (SAVE, 5), (SAVE, 1),
    (SSAVE, 1), (SAVE, 3), (SAVE, 6), (SAVE, 4),
)
RELAY, PIPE_FIRST, PLANE_ONLY, PLANE_FIRST = range(4)
WAYS = (RELAY, RELAY, RELAY, PLANE_FIRST, RELAY, PIPE_FIRST, PIPE_FIRST)
DIRECT = (True, True, False, False, False, False, True)


def grad_parts(state, model):
    wide = 4 * state + model
    return ((1, 4 * state, wide), (1, 2 * state, 4 * state), (1, 0, 2 * state), (0, 4 * state, wide), (0, 2 * state, 4 * state), (0, 0, state), (0, state, 2 * state))


def weight_parts(state, model):
    wide = 4 * state + model
    return ((0, 0, state), (0, state, 2 * state), (0, 2 * state, 4 * state), (0, 4 * state, wide), (1, 0, 2 * state), (1, 2 * state, 4 * state), (1, 4 * state, wide))


MESH = pl.DeviceIdType.MESH
F32 = jnp.float32
BF16 = jnp.bfloat16
NN = (((1,), (0,)), ((), ()))
NT = (((1,), (1,)), ((), ()))
TN = (((0,), (0,)), ((), ()))
FETCHES = ("lre", "lim", "lst", "b", "x", "c", "glu", "gain", "skip", "bias", "cot")


def cmul(u, v):
    return (u[0] * v[0] - u[1] * v[1], u[0] * v[1] + u[1] * v[0])


def conj(u):
    return (u[0], -u[1])


def dot(a, b, dims):
    return lax.dot_general(a, b, dims, preferred_element_type=F32)


def discretize(lam_re, lam_im, log_step):
    step = jnp.exp(log_step)
    radius = jnp.exp(lam_re * step)
    turn = lam_im * step
    decay = (radius * jnp.cos(turn), radius * jnp.sin(turn))
    modulus = lam_re * lam_re + lam_im * lam_im
    coef = (
        ((decay[0] - 1.0) * lam_re + decay[1] * lam_im) / modulus,
        (decay[1] * lam_re - (decay[0] - 1.0) * lam_im) / modulus,
    )
    return step, decay, coef


def discretize_grads(lam_re, lam_im, log_step, decay_grad, coef_grad):
    step, decay, coef = discretize(lam_re, lam_im, log_step)
    lam = (lam_re, lam_im)
    modulus = lam_re * lam_re + lam_im * lam_im
    inverse = (lam_re / modulus, -lam_im / modulus)
    through = cmul(coef_grad, conj(inverse))
    total = (decay_grad[0] + through[0], decay_grad[1] + through[1])
    first = cmul(total, (step * decay[0], -step * decay[1]))
    second = cmul(coef_grad, conj(cmul(coef, inverse)))
    turned = cmul(total, conj(cmul(lam, decay)))
    return first[0] - second[0], first[1] - second[1], step * turned[0]


def weight_gather(refs, pieces, depth, planes, me, plane, core, at_pipe, at_plane, at_core, remote):
    w_ref = refs["w"]
    sems = (refs["w_send"], refs["w_recv"])
    along, onward, across = {}, {}, {}
    (to_x, by_x), (to_y, by_y) = neighbours(me, at_pipe)

    def cols_of(piece, half=None):
        _, low, high = pieces[piece]
        middle = low + (high - low) // 256 * 128
        return pl.ds(*((low, high - low), (low, middle - low), (middle, high - middle))[0 if half is None else half + 1])

    def block(piece, z, member, half=None):
        return w_ref.at[pieces[piece][0], z, core, member, :, cols_of(piece, half)]

    def send(piece):
        own = block(piece, plane, me)
        along[piece] = [remote(own, own, sems, (piece, k - 1), at_plane(k)) for k in range(1, planes)]

    def place(k):
        return lax.rem(plane - k + planes, planes)

    def relay(piece):
        onward[piece] = []
        direct = DIRECT[piece]
        for k in range(1, planes):
            along[piece][k - 1].wait_recv()
            own = block(piece, place(k), me)
            for j, device in enumerate([at_pipe(j) for j in range(1, depth)] if direct else (to_x, to_y)):
                onward[piece].append(remote(own, own, sems, (piece, planes - 1 + 4 * (k - 1) + j), device))

    def forward(piece):
        made = []
        for k in range(1, planes):
            for j, (member, device) in enumerate(((by_x, to_y), (by_y, to_x))):
                onward[piece][2 * (k - 1) + j].wait_recv()
                half = block(piece, place(k), member, j)
                made.append(remote(half, half, sems, (piece, planes - 1 + 4 * (k - 1) + 2 + j), device))
        onward[piece] = made

    def swap(piece):
        for copy in onward[piece]:
            copy.wait_recv()
        both = w_ref.at[pieces[piece][0], :, core, :, :, cols_of(piece)]
        across[piece] = remote(both, both, sems, (piece, 5 * (planes - 1)), at_core)

    def ready(piece):
        across[piece].wait_recv()

    return send, relay, forward, swap, ready


def neighbours(me, at_pipe):
    x, y = lax.rem(me, 2), lax.div(me, 2)
    by_x, by_y = 2 * y + 1 - x, 2 * (1 - y) + x
    return (at_pipe(by_x - me + 4), by_x), (at_pipe(by_y - me + 4), by_y)


def gradient_sums(refs, depth, planes, me, plane, core, at_pipe, at_plane, at_core, remote):
    sems = (refs["g_send"], refs["g_recv"])
    copies = {}
    x, y = lax.rem(me, 2), lax.div(me, 2)
    (to_x, by_x), (to_y, by_y) = neighbours(me, at_pipe)

    def of(piece, *names):
        return [refs[f"{name}{piece}"] for name in names]

    def halves(piece):
        width = refs[f"done{piece}"].shape[-1]
        return pl.ds(0, width // 2), pl.ds(width // 2, width // 2)

    def back_by_relay(piece):
        return WAYS[piece] in (RELAY, PLANE_FIRST) and refs[f"done{piece}"].shape[-1] % 256 == 0

    def start(piece, matrix):
        part, other = of(piece, "part", "other")
        part[...] = matrix.astype(BF16).reshape(part.shape)
        copies[piece, 0] = remote(part.at[:, 1 - core], other, sems, (piece, 0), at_core)

    def first(piece):
        copies[piece, 0].wait_recv()
        part, other, pair, quad = of(piece, "part", "other", "pair", "quad")

        def add(i, carry):
            z, j = lax.div(i, depth), lax.rem(i, depth)
            total = part[z, core, j] + other[z, j]
            if WAYS[piece] in (PLANE_ONLY, PLANE_FIRST):
                pair[z, j] = total
            else:
                pair[j, z] = total
            return carry
        lax.fori_loop(0, planes * depth, add, 0, unroll=4)
        if WAYS[piece] == RELAY:
            low, high = halves(piece)
            made = []
            for i in range(2):
                made.append(remote(pair.at[2 * i + 1 - x, :, :, low], quad.at[0, i], sems, (piece, 1 + i), to_x))
                made.append(remote(pair.at[2 * (1 - y) + i, :, :, high], quad.at[1, i], sems, (piece, 3 + i), to_y))
        else:
            by_plane = WAYS[piece] in (PLANE_ONLY, PLANE_FIRST)
            count, here, there = (planes, plane, at_plane) if by_plane else (depth, me, at_pipe)
            made = [
                remote(pair.at[lax.rem(here + k, count)], quad.at[k - 1], sems, (piece, k), there(k))
                for k in range(1, count)
            ]
        copies[piece, 1] = made

    def middle(piece):
        pair, quad, pass_on, last = of(piece, "pair", "quad", "pass", "last")
        for copy in copies[piece, 1]:
            copy.wait_recv()
        low, high = halves(piece)

        def add(z, carry):
            pass_on[0, z] = pair[by_y, z, :, low] + quad[0, 1 - y, z]
            pass_on[1, z] = pair[by_x, z, :, high] + quad[1, 1 - x, z]
            return carry
        lax.fori_loop(0, planes, add, 0, unroll=2)
        copies[piece, 2] = [
            remote(pass_on.at[0], last.at[0], sems, (piece, 5), to_y),
            remote(pass_on.at[1], last.at[1], sems, (piece, 6), to_x),
        ]

    def second(piece):
        way = WAYS[piece]
        pair, quad, line, came = of(piece, "pair", "quad", "line", "came")
        for copy in copies[piece, 2 if way == RELAY else 1]:
            copy.wait_recv()
        if way == RELAY:
            low, high = halves(piece)
            last = refs[f"last{piece}"]

            def add(z, carry):
                for half, (cols, own) in enumerate(((low, y), (high, x))):
                    total = pair[me, z, :, cols].astype(F32) + quad[half, own, z].astype(F32) + last[half, z].astype(F32)
                    line[z, :, cols] = total.astype(BF16)
                return carry
        else:
            here, count = (plane, planes) if way in (PLANE_ONLY, PLANE_FIRST) else (me, depth)

            def add(i, carry):
                total = pair[here, i].astype(F32)
                for k in range(1, count):
                    total = total + quad[k - 1, i].astype(F32)
                if way == PLANE_ONLY:
                    came[me, i] = total.astype(BF16)
                else:
                    line[i] = total.astype(BF16)
                return carry
        lax.fori_loop(0, depth if way in (PLANE_ONLY, PLANE_FIRST) else planes, add, 0, unroll=2)
        if way == PLANE_ONLY:
            made = [remote(came.at[me], came.at[me], sems, (piece, 6 + k), at_pipe(k)) for k in range(1, depth)]
        elif way == PLANE_FIRST:
            made = [
                remote(line.at[lax.rem(me + k, depth)], came.at[k - 1], sems, (piece, 6 + k), at_pipe(k))
                for k in range(1, depth)
            ]
        else:
            made = [
                remote(line.at[lax.rem(plane + k, planes)], came.at[k - 1], sems, (piece, 6 + k), at_plane(k))
                for k in range(1, planes)
            ]
        copies[piece, 3] = made

    def third(piece):
        line, came, done = of(piece, "line", "came", "done")
        for copy in copies[piece, 3]:
            copy.wait_recv()
        by_plane = WAYS[piece] == PLANE_FIRST
        total = line[me if by_plane else plane].astype(F32)
        for k in range(1, depth if by_plane else planes):
            total = total + came[k - 1].astype(F32)
        done[me] = total.astype(BF16)
        devices = (to_x, to_y) if back_by_relay(piece) else [at_pipe(k) for k in range(1, depth)]
        copies[piece, 4] = [
            remote(done.at[me], done.at[me], sems, (piece, 6 + planes + i), device) for i, device in enumerate(devices)
        ]

    def fourth(piece):
        done = refs[f"done{piece}"]
        low, high = halves(piece)
        made = []
        for i, (member, cols, device) in enumerate(((by_x, low, to_y), (by_y, high, to_x))):
            copies[piece, 4][i].wait_recv()
            half = done.at[member, :, cols]
            made.append(remote(half, half, sems, (piece, 8 + planes + i), device))
        copies[piece, 4] = made

    def finish(piece):
        if WAYS[piece] == PLANE_ONLY:
            came = refs[f"came{piece}"]
            for copy in copies[piece, 3]:
                copy.wait_recv()
            done = came[0].astype(F32)
            for j in range(1, depth):
                done = done + came[j].astype(F32)
        else:
            for copy in copies[piece, 4]:
                copy.wait_recv()
            done = refs[f"done{piece}"][...].astype(F32)
        return done.reshape(done.shape[0] * done.shape[1], done.shape[2])

    return start, first, middle, second, third, fourth, finish


def small_sums(refs, depth, planes, me, plane, core, at_pipe, at_plane, at_core, remote):
    sems = (refs["s_send"], refs["s_recv"])
    own, other, quad, line = refs["small"], refs["s_other"], refs["s_quad"], refs["s_line"]
    copies = {}

    def start(layer):
        copies[layer, 0] = remote(own.at[layer], other.at[layer], sems, (layer, 0), at_core)

    def to_pipe(layer):
        copies[layer, 0].wait_recv()
        quad[layer, me] = own[layer] + other[layer]
        copies[layer, 1] = [
            remote(quad.at[layer, me], quad.at[layer, me], sems, (layer, k), at_pipe(k)) for k in range(1, depth)
        ]

    def to_plane(layer):
        for copy in copies[layer, 1]:
            copy.wait_recv()
        total = quad[layer, 0]
        for j in range(1, depth):
            total = total + quad[layer, j]
        line[layer, plane] = total
        copies[layer, 2] = [
            remote(line.at[layer, plane], line.at[layer, plane], sems, (layer, depth + k - 1), at_plane(k))
            for k in range(1, planes)
        ]

    def finish(layer):
        for copy in copies[layer, 2]:
            copy.wait_recv()
        total = line[layer, 0]
        for z in range(1, planes):
            total = total + line[layer, z]
        return total

    return start, to_pipe, to_plane, finish


def main_kernel(depth, planes, names, *refs):
    r_ = dict(zip(names, refs))
    x_ref, len_ref = r_["x"], r_["len"]
    small_ref = r_["small"]
    h_ref, go_ref, xhat_ref, rstd_ref, normed_ref = r_["h"], r_["go"], r_["xhat"], r_["rstd"], r_["normed"]
    p_ref, z_ref, zb_ref, dg_ref, gated_ref, sig_ref = r_["p"], r_["z"], r_["zb"], r_["dg"], r_["gated"], r_["sig"]
    gg_ref, gb_ref, gp_ref, src_ref, tmp_ref, acc_ref = r_["gg"], r_["gb"], r_["gp"], r_["src"], r_["tmp"], r_["acc"]
    ends_ref, got_ref, send_sems, recv_sems = r_["ends"], r_["got"], r_["send"], r_["recv"]
    w_ref = r_["w"]
    seqs, pos, model = x_ref.shape
    layers, state = r_["lre"].shape
    rows = seqs * pos
    steps = pos // CHUNKS
    me, dp = lax.axis_index("pipe"), lax.axis_index("dp")
    plane, core = lax.div(dp, 2), lax.rem(dp, 2)

    def peer(k):
        return lax.rem(me + k, depth)

    def at_pipe(k):
        return (peer(k), dp)

    def at_plane(k):
        return (me, 2 * lax.rem(plane + k, planes) + core)

    at_core = (me, 2 * plane + (1 - core))
    others = [at_pipe(k) for k in range(1, depth)]
    if planes:
        others += [at_plane(k) for k in range(1, planes)] + [at_core]
    barrier = pltpu.get_barrier_semaphore()
    for device in others:
        pl.semaphore_signal(barrier, inc=1, device_id=device, device_id_type=MESH)

    unsent = []

    def remote(src, dst, sems, at, device):
        copy = pltpu.make_async_remote_copy(
            src_ref=src, dst_ref=dst, send_sem=sems[0].at[at], recv_sem=sems[1].at[at],
            device_id=device, device_id_type=MESH,
        )
        copy.start()
        unsent.append(copy)
        return copy

    row = lax.broadcasted_iota(jnp.int32, (pos, pos), 0)
    col = lax.broadcasted_iota(jnp.int32, (pos, pos), 1)
    spread = (lax.rem(row, CHUNKS) * steps + lax.div(row, CHUNKS) == col).astype(F32).astype(BF16)
    masks = [(len_ref[q] > me * pos).astype(F32) for q in range(seqs)]
    sublane = lax.broadcasted_iota(jnp.int32, (CHUNKS, state), 0)

    def seq_rows(q):
        return pl.ds(q * pos, pos)

    def tiles(body, q, init=0, unroll=1):
        def step(i, carry):
            return body(pl.ds(pl.multiple_of(q * pos + i * TILE, TILE), TILE), masks[q], carry)
        return lax.fori_loop(0, pos // TILE, step, init, unroll=unroll)

    def all_tiles(body, init=0, unroll=4):
        for q in range(seqs):
            init = tiles(body, q, init, unroll)
        return init

    def fold(value):
        total = value[0:8]
        for r in range(8, value.shape[0], 8):
            total = total + value[r:r + 8]
        return total

    fetches = {}
    for at, name in enumerate(FETCHES):
        if name not in r_:
            continue
        fetches[name] = pltpu.make_async_copy(r_[name], r_[name + "_here"], r_["fetch"].at[at])
        fetches[name].start()
    x_here, cot_here = r_["x_here"], r_["cot_here"]
    gain_ref, skip_ref, bias_ref = r_["gain_here"], r_["skip_here"], r_["bias_here"]
    lre_ref, lim_ref, lst_ref = r_["lre_here"], r_["lim_here"], r_["lst_here"]
    for name in ("lre", "lim", "lst"):
        fetches[name].wait()
    step_all, decay_all, coef_all = discretize(lre_ref[...], lim_ref[...], lst_ref[...])
    if planes:
        ways = (depth, planes, me, plane, core, at_pipe, at_plane, at_core, remote)
        wide = 4 * state + model
        pieces = weight_parts(state, model)
        w_send, w_relay, w_forward, w_swap, w_ready = weight_gather(r_, pieces, *ways)
        g_start, g_first, g_middle, g_second, g_third, g_fourth, g_finish = gradient_sums(r_, *ways)
        parts = grad_parts(state, model)
        s_start, s_pipe, s_plane, s_finish = small_sums(r_, *ways)

        def keep(layer, matrix, low):
            high = low + matrix.shape[1]
            w_ref[layer, plane, core, :, :, low:high] = matrix.astype(BF16).reshape(depth, -1, high - low)

        fetches["b"].wait()
        for layer in range(layers):
            keep(layer, r_["b_here"][layer], 0)
    pl.semaphore_wait(barrier, len(others))

    def matrix(layer, which):
        low, high = (0, 2 * state, 4 * state)[which], (2 * state, 4 * state, w_ref.shape[-1])[which]
        value = w_ref[layer, ..., low:high]
        return value.reshape(model, high - low)

    def complex_rows(src, r):
        return (src[r, 0:state], src[r, state:2 * state])

    zero = jnp.zeros((CHUNKS, state), F32)

    def scan_ends(src, decay, down):
        def step(i, carry):
            s = (steps - 1 - i) if down else i
            made = []
            for q in range(seqs):
                r = pl.ds(pl.multiple_of(q * pos + s * CHUNKS, CHUNKS), CHUNKS)
                add = complex_rows(src, r)
                moved = cmul(decay, carry[q])
                made.append((moved[0] + add[0], moved[1] + add[1]))
            return tuple(made)
        return lax.fori_loop(0, steps, step, ((zero, zero),) * seqs, unroll=32)

    def shifted(value, k, down):
        rolled = pltpu.roll(value, CHUNKS - k if down else k, axis=0)
        keep = (sublane < CHUNKS - k) if down else (sublane >= k)
        return jnp.where(keep, rolled, 0.0)

    def squared(value, times):
        for _ in range(times):
            value = cmul(value, value)
        return value

    lanes = 128
    spans = state // lanes

    def chunk_powers(layer):
        powers = [squared(wide_decay(layer), steps.bit_length() - 1)]
        while len(powers) < CHUNKS.bit_length():
            powers.append(cmul(powers[-1], powers[-1]))
        return powers

    def place_table(powers, down):
        place = (CHUNKS - 1 - sublane) if down else sublane
        table = (jnp.ones((CHUNKS, state), F32), zero)
        for bit, factor in enumerate(powers[:-1]):
            moved = cmul(table, factor)
            take = lax.rem(lax.div(place, 1 << bit), 2) == 1
            table = (jnp.where(take, moved[0], table[0]), jnp.where(take, moved[1], table[1]))
        return table

    def start_exchange(number, ends, powers, down):
        sums = list(ends)
        for bit, jump in enumerate(powers[:-1]):
            for q in range(seqs):
                moved = cmul(jump, (shifted(sums[q][0], 1 << bit, down), shifted(sums[q][1], 1 << bit, down)))
                sums[q] = (sums[q][0] + moved[0], sums[q][1] + moved[1])
        last = 0 if down else CHUNKS - 1
        for q in range(seqs):
            for part in range(2):
                for j in range(spans):
                    at = (q * 2 + part) * spans + j
                    ends_ref[number, at:at + 1, :] = sums[q][part][last:last + 1, j * lanes:(j + 1) * lanes]
        copies = [
            remote(ends_ref.at[number], got_ref.at[number, k - 1], (send_sems, recv_sems), (number, k - 1),
                   at_pipe(depth - k if down else k))
            for k in range(1, depth)
        ]
        return copies, sums

    def finish_exchange(number, pending, powers, down):
        copies, sums = pending
        table = place_table(powers, down)
        exclusive = [(shifted(s[0], 1, down), shifted(s[1], 1, down)) for s in sums]
        for copy in copies:
            copy.wait_recv()
        jump = powers[-1]
        carries = []
        for q in range(seqs):
            total, factor = (zero, zero), (jnp.ones((CHUNKS, state), F32), zero)
            for k in range(1, depth):
                there = ((me + k < depth) if down else (me - k >= 0)).astype(F32)
                came = []
                for part in range(2):
                    at = (q * 2 + part) * spans
                    pieces_ = [
                        jnp.broadcast_to(got_ref[number, k - 1, at + j:at + j + 1, :], (CHUNKS, lanes))
                        for j in range(spans)
                    ]
                    came.append(jnp.concatenate(pieces_, axis=1) * there)
                moved = cmul(factor, came)
                total = (total[0] + moved[0], total[1] + moved[1])
                factor = cmul(factor, jump)
            moved = cmul(table, total)
            carries.append((exclusive[q][0] + moved[0], exclusive[q][1] + moved[1]))
        return carries

    def wide_decay(layer):
        return tuple(jnp.broadcast_to(part[layer:layer + 1], (CHUNKS, state)) for part in decay_all)

    small_ref[...] = jnp.zeros_like(small_ref)
    powers_of = [chunk_powers(layer) for layer in range(layers)]

    def back_powers(layer):
        return [conj(power) for power in powers_of[layer]]

    pad = pos + CHUNKS
    gather = (lax.rem(row, steps) * CHUNKS + lax.div(row, steps) == col).astype(F32).astype(BF16)
    zero_row = jnp.zeros((8, model), F32)
    puts, held = [], {}

    def put(name, at=None, cols=None):
        source, target = r_[name + "_here"], r_[name]
        if cols is not None:
            source, target = source.at[at, :, cols], target.at[at, :, cols]
        elif at is not None:
            source, target = source.at[at], target.at[at]
        copy = pltpu.make_async_copy(source, target, r_["put"].at[len(puts)])
        copy.start()
        puts.append(copy)

    def one(ref, layer):
        return ref[layer:layer + 1, :]

    def turn(layer, real, imag):
        return cmul((coef_all[0][layer:layer + 1], coef_all[1][layer:layer + 1]), (real, imag))

    def step_fold(layer):
        if layer == 0:
            fetches["c"].wait()
            fetches["glu"].wait()
        turned = turn(layer, r_["c_here"][layer, :, 0:state], r_["c_here"][layer, :, state:2 * state])
        keep(layer, turned[0], 2 * state)
        keep(layer, -turned[1], 3 * state)
        keep(layer, r_["glu_here"][layer], 4 * state)

    def step_x(_):
        for name in ("x", "gain", "skip", "bias"):
            fetches[name].wait()
        for q in range(seqs):
            h_ref[0, seq_rows(q), :] = dot(spread, x_here[q], NN).astype(BF16)

    def step_cot(_):
        fetches["cot"].wait()
        for q in range(seqs):
            go_ref[seq_rows(q), :] = dot(spread, cot_here[q], NN).astype(BF16)

    def step_norm(layer):
        gain = one(gain_ref, layer)

        def tile(r, mask, carry):
            h = h_ref[layer, r, :].astype(F32)
            mean = jnp.mean(h, axis=1, keepdims=True)
            centred = h - mean
            variance = jnp.mean(centred * centred, axis=1, keepdims=True)
            rstd = lax.rsqrt(variance + EPSILON)
            xhat = centred * rstd
            xhat_ref[layer, r, :] = xhat
            rstd_ref[layer, r, :] = jnp.broadcast_to(rstd, (TILE, 128))
            normed_ref[layer, r, :] = (xhat * gain * mask).astype(BF16)
            return carry
        all_tiles(tile, unroll=4)

    def step_proj(layer):
        p_ref[layer] = dot(normed_ref[layer], matrix(layer, 0), NN)

    def step_ends(layer):
        ends = scan_ends(p_ref.at[layer], wide_decay(layer), layer % 2 == 1)
        held["pending", layer] = start_exchange(layer, ends, powers_of[layer], layer % 2 == 1)

    def step_scan(layer):
        down = layer % 2 == 1
        decay = wide_decay(layer)
        carries = finish_exchange(layer, held["pending", layer], powers_of[layer], down)
        for q in range(seqs):
            at = q * pad + (pos if down else 0)
            z_ref[layer, at:at + CHUNKS, 0:state] = carries[q][0]
            z_ref[layer, at:at + CHUNKS, state:2 * state] = carries[q][1]

        def pair(i, carry):
            carry = list(carry)
            for q in range(seqs):
                pieces = []
                for half in range(2):
                    s = (steps - 1 - 2 * i - half) if down else 2 * i + half
                    r = pl.ds(pl.multiple_of(q * pos + s * CHUNKS, CHUNKS), CHUNKS)
                    add = complex_rows(p_ref.at[layer], r)
                    moved = cmul(decay, carry[q])
                    carry[q] = (moved[0] + add[0], moved[1] + add[1])
                    r = pl.ds(pl.multiple_of(q * pad + (s + (0 if down else 1)) * CHUNKS, CHUNKS), CHUNKS)
                    z_ref[layer, r, 0:state] = carry[q][0]
                    z_ref[layer, r, state:2 * state] = carry[q][1]
                    pieces.append(carry[q])
                if down:
                    pieces = pieces[::-1]
                low = (steps - 2 - 2 * i) if down else 2 * i
                r = pl.ds(pl.multiple_of(q * pos + low * CHUNKS, 2 * CHUNKS), 2 * CHUNKS)
                for part in range(2):
                    both = jnp.concatenate([pieces[0][part], pieces[1][part]], axis=0)
                    zb_ref[layer, r, part * state:(part + 1) * state] = both.astype(BF16)
            return tuple(carry)
        lax.fori_loop(0, steps // 2, pair, tuple(carries), unroll=16)

    def step_cdot(layer):
        tmp_ref[...] = dot(zb_ref[layer], matrix(layer, 1), NT)

    def step_gelu(layer):
        skip = one(skip_ref, layer)

        def tile(r, mask, carry):
            before = tmp_ref[r, :] + skip * normed_ref[layer, r, :].astype(F32)
            phi = 0.5 * (1.0 + lax.erf(before * 0.7071067811865476))
            dg_ref[layer, r, :] = phi + before * (0.3989422804014327 * jnp.exp(-0.5 * before * before))
            gated_ref[layer, r, :] = (before * phi).astype(BF16)
            return carry
        all_tiles(tile)

    def step_gdot(layer):
        tmp_ref[...] = dot(gated_ref[layer], matrix(layer, 2), NN)

    def step_out(layer):
        bias = one(bias_ref, layer)

        def tile(r, mask, carry):
            sig = 1.0 / (1.0 + jnp.exp(-(tmp_ref[r, :] + bias)))
            sig_ref[layer, r, :] = sig
            made = h_ref[layer, r, :].astype(F32) + mask * (gated_ref[layer, r, :].astype(F32) * sig)
            h_ref[layer + 1, r, :] = made.astype(BF16)
            return carry
        all_tiles(tile)

    def step_result(_):
        for q in range(seqs):
            r_["out_here"][q] = dot(gather, h_ref[layers, seq_rows(q), :], NN).astype(BF16)
        put("out")

    def step_gate(layer):
        def tile(r, mask, carry):
            sig = sig_ref[layer, r, :]
            branch = mask * go_ref[r, :].astype(F32) * sig
            grad = (branch * gated_ref[layer, r, :].astype(F32) * (1.0 - sig)).astype(BF16)
            gg_ref[r, :] = grad
            acc_ref[r, :] = branch
            return carry + fold(grad.astype(F32))
        held["bias", layer] = all_tiles(tile, zero_row)

    def step_gback(layer):
        tmp_ref[...] = dot(gg_ref[...], matrix(layer, 2), NT)

    def step_before(layer):
        def tile(r, mask, carry):
            gated_grad = (acc_ref[r, :] + tmp_ref[r, :]).astype(BF16).astype(F32)
            grad = (gated_grad * dg_ref[layer, r, :]).astype(BF16)
            gb_ref[r, :] = grad
            return carry + fold(grad.astype(F32) * normed_ref[layer, r, :].astype(F32))
        held["skip", layer] = all_tiles(tile, zero_row)

    def step_src(layer):
        src_ref[...] = dot(gb_ref[...], matrix(layer, 1), NN)

    def step_bends(layer):
        ends = scan_ends(src_ref, conj(wide_decay(layer)), layer % 2 == 0)
        held["back", layer] = start_exchange(layers + layer, ends, back_powers(layer), layer % 2 == 0)

    def step_bscan(layer):
        down = layer % 2 == 1
        back = conj(wide_decay(layer))
        carries = finish_exchange(layers + layer, held["back", layer], back_powers(layer), not down)

        def pair(i, loop):
            carry, sums = list(loop[0]), list(loop[1])
            for q in range(seqs):
                pieces = []
                for half in range(2):
                    s = 2 * i + half if down else (steps - 1 - 2 * i - half)
                    r = pl.ds(pl.multiple_of(q * pos + s * CHUNKS, CHUNKS), CHUNKS)
                    add = complex_rows(src_ref, r)
                    moved = cmul(back, carry[q])
                    adj = (moved[0] + add[0], moved[1] + add[1])
                    carry[q] = adj
                    pieces.append(adj)
                    proj = complex_rows(p_ref.at[layer], r)
                    r = pl.ds(pl.multiple_of(q * pad + (s + (1 if down else 0)) * CHUNKS, CHUNKS), CHUNKS)
                    prior = complex_rows(z_ref.at[layer], r)
                    sums[0] = sums[0] + (adj[0] * prior[0] + adj[1] * prior[1])
                    sums[1] = sums[1] + (adj[1] * prior[0] - adj[0] * prior[1])
                    sums[2] = sums[2] + (adj[0] * proj[0] + adj[1] * proj[1])
                    sums[3] = sums[3] + (adj[1] * proj[0] - adj[0] * proj[1])
                if not down:
                    pieces = pieces[::-1]
                low = 2 * i if down else (steps - 2 - 2 * i)
                r = pl.ds(pl.multiple_of(q * pos + low * CHUNKS, 2 * CHUNKS), 2 * CHUNKS)
                for part in range(2):
                    both = jnp.concatenate([pieces[0][part], pieces[1][part]], axis=0)
                    gp_ref[r, part * state:(part + 1) * state] = both.astype(BF16)
            return tuple(carry), tuple(sums)
        held["sums", layer] = lax.fori_loop(0, steps // 2, pair, (tuple(carries), (zero,) * 4), unroll=16)[1]

    def send_part(layer, low, made):
        high = low + made.shape[1]
        if not planes:
            r_["gpart"][layer, :, low:high] = made
            return
        for piece, (of_layer, first, last) in enumerate(parts):
            if of_layer == layer and low <= first and last <= high:
                g_start(piece, made[:, first - low:last - low])

    def step_cgrad(layer):
        send_part(layer, 2 * state, dot(gb_ref[...], zb_ref[layer], TN))

    def step_ggrad(layer):
        send_part(layer, 4 * state, dot(gated_ref[layer], gg_ref[...], TN))

    def step_bgrad(layer):
        send_part(layer, 0, dot(normed_ref[layer], gp_ref[...], TN))

    def step_xdot(layer):
        tmp_ref[...] = dot(gp_ref[...], matrix(layer, 0), NT)

    def step_bnorm(layer):
        gain, skip = one(gain_ref, layer), one(skip_ref, layer)

        def tile(r, mask, carry):
            grad = (tmp_ref[r, :] + skip * gb_ref[r, :].astype(F32)) * mask
            xhat = xhat_ref[layer, r, :]
            rstd = jnp.concatenate([rstd_ref[layer, r, :]] * (model // 128), axis=1)
            scaled = grad * gain
            first = jnp.mean(scaled, axis=1, keepdims=True)
            second = jnp.mean(scaled * xhat, axis=1, keepdims=True)
            made = go_ref[r, :].astype(F32) + rstd * (scaled - first - xhat * second)
            go_ref[r, :] = made.astype(BF16)
            return carry + fold(grad * xhat)
        gain_sum = all_tiles(tile, zero_row, unroll=4)
        for at, value in enumerate((gain_sum, held["skip", layer], held["bias", layer])):
            small_ref[layer, at:at + 1, :] = jnp.sum(value, axis=0, keepdims=True)
        for at, value in enumerate(held["sums", layer]):
            small_ref[layer, 3 + at:4 + at, 0:state] = jnp.sum(value, axis=0, keepdims=True)

    def step_xg(_):
        for q in range(seqs):
            r_["xg_here"][q] = dot(gather, go_ref[seq_rows(q), :], NN).astype(BF16)
        put("xg")

    def step_ssave(layer):
        total = s_finish(layer)
        for at, name in enumerate(("gain_grad", "skip_grad", "bias_grad")):
            r_[name + "_here"][layer:layer + 1, :] = total[at:at + 1, :]
        coef = (coef_all[0][layer:layer + 1], coef_all[1][layer:layer + 1])
        sums = [total[at:at + 1, 0:state] for at in range(3, 7)]
        scale = coef[0] * coef[0] + coef[1] * coef[1]
        coef_grad = cmul((sums[2], sums[3]), (coef[0] / scale, coef[1] / scale))
        made = discretize_grads(
            one(lre_ref, layer), one(lim_ref, layer), one(lst_ref, layer), (sums[0], sums[1]), coef_grad)
        for name, value in zip(("lre_grad", "lim_grad", "lst_grad"), made):
            r_[name + "_here"][layer:layer + 1, :] = value

    def step_save(piece):
        layer, low, high = parts[piece]
        done = g_finish(piece)
        if low >= 4 * state:
            r_["glu_grad_here"][layer] = done
            put("glu_grad", layer)
        elif low >= 2 * state:
            turned = turn(layer, done[:, 0:state], done[:, state:2 * state])
            r_["c_grad_here"][layer, :, 0:state] = turned[0]
            r_["c_grad_here"][layer, :, state:2 * state] = -turned[1]
            put("c_grad", layer)
        else:
            r_["b_grad_here"][layer, :, low:high] = done
            put("b_grad", layer, pl.ds(low, high - low))

    do = {
        X: step_x, COT: step_cot, NORM: step_norm, PROJ: step_proj, ENDS: step_ends, SCAN: step_scan, CDOT: step_cdot,
        GELU: step_gelu, GDOT: step_gdot, OUT: step_out, RESULT: step_result, GATE: step_gate, GBACK: step_gback,
        BEFORE: step_before, SRC: step_src, BENDS: step_bends, BSCAN: step_bscan, CGRAD: step_cgrad, GGRAD: step_ggrad,
        BGRAD: step_bgrad, XDOT: step_xdot, BNORM: step_bnorm, XG: step_xg,
    }
    if planes:
        do.update({
            FOLD: step_fold, WSEND: w_send, WRELAY: w_relay, WFORWARD: w_forward, WSWAP: w_swap, WREADY: w_ready,
            FIRST: g_first, MIDDLE: g_middle, SECOND: g_second, THIRD: g_third, FOURTH: g_fourth, SAVE: step_save,
            SSTART: s_start, SPIPE: s_pipe, SPLANE: s_plane, SSAVE: step_ssave,
        })
    for name, at in ORDER:
        if name in do:
            do[name](at)
    if planes:
        for name in ("gain_grad", "skip_grad", "bias_grad", "lre_grad", "lim_grad", "lst_grad"):
            put(name)
    for copy in puts:
        copy.wait()
    for copy in unsent:
        copy.wait_send()


def copy_kernel(*refs):
    count = (len(refs) - 2) // 3
    sources, targets, held, (in_sems, out_sems) = refs[:count], refs[count:2 * count], refs[2 * count:3 * count], refs[3 * count:]
    arrive = [pltpu.make_async_copy(sources[i], held[i], in_sems.at[i]) for i in range(count)]
    leave = [pltpu.make_async_copy(held[i], targets[i], out_sems.at[i]) for i in range(count)]
    for copy in arrive:
        copy.start()
    for first, then in zip(arrive, leave):
        first.wait()
        then.start()
    for copy in leave:
        copy.wait()


def copied(results):
    anywhere = pl.BlockSpec(memory_space=pl.ANY)
    return pl.pallas_call(
        copy_kernel,
        out_shape=tuple(jax.ShapeDtypeStruct(r.shape, r.dtype) for r in results),
        in_specs=[anywhere] * len(results),
        out_specs=(anywhere,) * len(results),
        scratch_shapes=[pltpu.VMEM(r.shape, r.dtype) for r in results] + [pltpu.SemaphoreType.DMA((len(results),))] * 2,
        compiler_params=pltpu.CompilerParams(vmem_limit_bytes=60 * 2**20),
    )(*results)


def run_main(planes, x_in, lengths, cotangent, norm_gain, lambda_re, lambda_im, log_step, skip_weight, glu_bias, weights):
    depth = lax.axis_size("pipe")
    seqs, pos, model = x_in.shape
    layers, state = lambda_re.shape
    rows = seqs * pos
    wide = 4 * state + model
    message = -(-seqs * 2 * state // (8 * 128)) * 8
    vmem = pl.BlockSpec(memory_space=pltpu.VMEM)
    smem = pl.BlockSpec(memory_space=pltpu.SMEM)
    anywhere = pl.BlockSpec(memory_space=pl.ANY)
    ins = dict(x=x_in, cot=cotangent, len=lengths, gain=norm_gain, lre=lambda_re, lim=lambda_im, lst=log_step,
               skip=skip_weight, bias=glu_bias)
    ins.update(zip(("b", "c", "glu") if planes else ("w",), weights))
    outs = dict(out=(x_in.shape, BF16), xg=(x_in.shape, BF16))
    scratch = dict(
        h=pltpu.VMEM((layers + 1, rows, model), BF16),
        go=pltpu.VMEM((rows, model), BF16),
        xhat=pltpu.VMEM((layers, rows, model), F32),
        rstd=pltpu.VMEM((layers, rows, 128), F32),
        normed=pltpu.VMEM((layers, rows, model), BF16),
        p=pltpu.VMEM((layers, rows, 2 * state), F32),
        z=pltpu.VMEM((layers, rows + seqs * CHUNKS, 2 * state), F32),
        zb=pltpu.VMEM((layers, rows, 2 * state), BF16),
        dg=pltpu.VMEM((layers, rows, model), F32),
        gated=pltpu.VMEM((layers, rows, model), BF16),
        sig=pltpu.VMEM((layers, rows, model), F32),
        gg=pltpu.VMEM((rows, model), BF16),
        gb=pltpu.VMEM((rows, model), BF16),
        gp=pltpu.VMEM((rows, 2 * state), BF16),
        src=pltpu.VMEM((rows, 2 * state), F32),
        tmp=pltpu.VMEM((rows, model), F32),
        acc=pltpu.VMEM((rows, model), F32),
        ends=pltpu.VMEM((2 * layers, message, 128), F32),
        got=pltpu.VMEM((2 * layers, depth - 1, message, 128), F32),
        fetch=pltpu.SemaphoreType.DMA((len(FETCHES),)),
        put=pltpu.SemaphoreType.DMA((8 + len(WAYS),)),
        send=pltpu.SemaphoreType.DMA((2 * layers, depth - 1)),
        recv=pltpu.SemaphoreType.DMA((2 * layers, depth - 1)),
    )
    if planes:
        local = weights[0].shape[1]
        part = local // depth
        full, halves = (layers, model), (layers, state)
        outs.update(
            gain_grad=(full, F32), lre_grad=(halves, F32), lim_grad=(halves, F32), lst_grad=(halves, F32),
            b_grad=((layers, local, 2 * state), F32), c_grad=((layers, local, 2 * state), F32),
            skip_grad=(full, F32), glu_grad=((layers, local, model), F32), bias_grad=(full, F32),
        )
        scratch.update(
            small=pltpu.VMEM((layers, 8, model), F32),
            s_other=pltpu.VMEM((layers, 8, model), F32),
            s_quad=pltpu.VMEM((layers, depth, 8, model), F32),
            s_line=pltpu.VMEM((layers, planes, 8, model), F32),
            w=pltpu.VMEM((layers, planes, 2, depth, part, wide), BF16),
        )
        spans = [high - low for _, low, high in grad_parts(state, model)]
        for piece, way in enumerate(WAYS):
            width = spans[piece]
            count, other = (planes, depth) if way in (PLANE_ONLY, PLANE_FIRST) else (depth, planes)
            shapes = dict(
                part=(planes, 2, depth, part, width), other=(planes, depth, part, width),
                pair=(count, other, part, width), quad=(count - 1, other, part, width),
                line=(other, part, width), came=(other - 1, part, width), done=(depth, part, width),
            )
            if way == RELAY:
                shapes.update(quad=(2, 2, planes, part, width // 2))
                shapes.update({"pass": (2, planes, part, width // 2), "last": (2, planes, part, width // 2)})
            if way == PLANE_ONLY:
                shapes.update(came=(depth, depth, part, width))
            scratch.update({f"{name}{piece}": pltpu.VMEM(shape, BF16) for name, shape in shapes.items()})
        for name, shape in dict(
            w=(len(DIRECT), 5 * planes - 4), g=(len(WAYS), 10 + planes), s=(layers, depth + planes - 1)
        ).items():
            scratch[name + "_send"] = pltpu.SemaphoreType.DMA(shape)
            scratch[name + "_recv"] = pltpu.SemaphoreType.DMA(shape)
    else:
        outs.update(gpart=((layers, model, wide), F32), small=((layers, 8, model), F32))
    fetched = tuple(name for name in FETCHES if name in ins)
    for name in fetched:
        scratch[name + "_here"] = pltpu.VMEM(ins[name].shape, ins[name].dtype)
    stored = tuple(name for name in outs if name not in ("gpart", "small"))
    for name in stored:
        scratch[name + "_here"] = pltpu.VMEM(*outs[name])
    names = tuple(ins) + tuple(outs) + tuple(scratch)
    return pl.pallas_call(
        functools.partial(main_kernel, depth, planes, names),
        out_shape=tuple(jax.ShapeDtypeStruct(*o) for o in outs.values()),
        in_specs=[smem if name == "len" else anywhere if name in fetched else vmem for name in ins],
        out_specs=tuple(anywhere if name in stored else vmem for name in outs),
        scratch_shapes=list(scratch.values()),
        compiler_params=pltpu.CompilerParams(
            collective_id=0, has_side_effects=True, vmem_limit_bytes=60 * 2**20
        ),
    )(*ins.values())


def per_device(
    x_in, lengths, cotangent, norm_gain, lambda_re, lambda_im, log_step,
    b_weight, c_weight, skip_weight, glu_weight, glu_bias,
):
    depth, owners = lax.axis_size("pipe"), lax.axis_size("dp")
    state = lambda_re.shape[1]
    rest = (lambda_re, lambda_im, log_step, skip_weight, glu_bias)
    if depth == 4 and b_weight.shape[1] % (16 * depth) == 0 and owners % 2 == 0:
        return copied(run_main(owners // 2, x_in, lengths, cotangent, norm_gain, *rest, (b_weight, c_weight, glu_weight)))
    _, _, coef = discretize(lambda_re, lambda_im, log_step)
    c_real, c_imag = c_weight[:, :, :state], c_weight[:, :, state:]
    turned = cmul((coef[0][:, None], coef[1][:, None]), (c_real, c_imag))
    shard = jnp.concatenate([b_weight, turned[0], -turned[1], glu_weight], axis=2).astype(BF16)
    weights = lax.all_gather(shard, "dp", axis=1, tiled=True)
    output, x_grad, gpart, small = run_main(
        0, x_in, lengths, cotangent, norm_gain, *rest, (weights,)
    )
    grads = lax.psum_scatter(gpart, "dp", scatter_dimension=1, tiled=True)
    grads = lax.psum(grads.astype(BF16), "pipe").astype(F32)
    small = lax.psum(small, ("pipe", "dp"))
    m_real, m_imag = grads[:, :, 2 * state:3 * state], grads[:, :, 3 * state:4 * state]
    turned = cmul((coef[0][:, None], coef[1][:, None]), (m_real, m_imag))
    c_grad = jnp.concatenate([turned[0], -turned[1]], axis=2)
    decay_grad = (small[:, 3, :state], small[:, 4, :state])
    scale = coef[0] * coef[0] + coef[1] * coef[1]
    coef_grad = cmul((small[:, 5, :state], small[:, 6, :state]), (coef[0] / scale, coef[1] / scale))
    lam_re_grad, lam_im_grad, step_grad = discretize_grads(lambda_re, lambda_im, log_step, decay_grad, coef_grad)
    return (
        output, x_grad, small[:, 0], lam_re_grad, lam_im_grad, step_grad,
        grads[:, :, :2 * state], c_grad, small[:, 1], grads[:, :, 4 * state:], small[:, 2],
    )


def solution(mesh):
    split, whole, rows = P("dp", "pipe", None), P(), P(None, "dp", None)
    return jax.shard_map(
        per_device,
        mesh=mesh,
        in_specs=(split, P("dp"), split, whole, whole, whole, whole, rows, rows, whole, rows, whole),
        out_specs=(split, split, whole, whole, whole, whole, rows, rows, whole, rows, whole),
        check_vma=False,
    )
```

```python
import functools

import jax
import jax.numpy as jnp
from jax import lax
from jax.experimental import pallas as pl
from jax.experimental.pallas import tpu as pltpu
from jax.sharding import PartitionSpec as P

EPSILON = 1e-05
CHUNKS = 8
TILE = 64
X, COT, NORM, PROJ, ENDS, SCAN, CDOT, GELU, GDOT, OUT, RESULT, GATE, GBACK, BEFORE, SRC, BENDS, BSCAN, CGRAD, GGRAD, BGRAD, XDOT, BNORM, XG = range(23)
FOLD, WSEND, WRELAY, WFORWARD, WSWAP, WREADY, FIRST, MIDDLE, SECOND, THIRD, FOURTH, SAVE, SSTART, SPIPE, SPLANE, SSAVE = range(23, 39)
ORDER = (
    (WSEND, 0), (WSEND, 1), (X, 0), (WSEND, 4), (FOLD, 0), (NORM, 0), (WSEND, 2), (FOLD, 1), (WSEND, 3), (WSEND, 5),
    (WRELAY, 0), (WRELAY, 1), (WRELAY, 4), (WSWAP, 0), (WRELAY, 2), (WSWAP, 1), (WRELAY, 3), (WREADY, 0), (WREADY, 1),
    (PROJ, 0), (WFORWARD, 4), (ENDS, 0), (WSEND, 6), (WFORWARD, 2), (COT, 0), (WFORWARD, 3), (WRELAY, 5), (WSWAP, 4),
    (WSWAP, 2), (WRELAY, 6), (WREADY, 4), (WSWAP, 3), (SCAN, 0), (WREADY, 2), (CDOT, 0), (GELU, 0), (WREADY, 3),
    (WFORWARD, 5), (GDOT, 0), (OUT, 0), (NORM, 1), (PROJ, 1), (ENDS, 1), (WSWAP, 6), (WSWAP, 5), (WREADY, 5),
    (WREADY, 6), (SCAN, 1), (CDOT, 1), (GELU, 1), (GDOT, 1), (OUT, 1), (GATE, 1), (GBACK, 1), (BEFORE, 1), (SRC, 1),
    (BENDS, 1), (GGRAD, 1), (CGRAD, 1), (FIRST, 1), (FIRST, 0), (BSCAN, 1), (BGRAD, 1), (XDOT, 1), (BNORM, 1),
    (GATE, 0), (GGRAD, 0), (FIRST, 2), (GBACK, 0), (BEFORE, 0), (CGRAD, 0), (FIRST, 3), (MIDDLE, 1), (SRC, 0),
    (BENDS, 0), (FIRST, 4), (MIDDLE, 0), (MIDDLE, 2), (SECOND, 1), (BSCAN, 0), (BGRAD, 0), (MIDDLE, 4), (XDOT, 0),
    (SSTART, 1), (SECOND, 0), (BNORM, 0), (FIRST, 6), (SSTART, 0), (RESULT, 0), (SECOND, 2), (FIRST, 5), (SECOND, 3),
    (SPIPE, 0), (SECOND, 4), (SECOND, 6), (SPIPE, 1), (THIRD, 1), (SECOND, 5), (XG, 0), (THIRD, 0), (THIRD, 2),
    (THIRD, 3), (SPLANE, 0), (THIRD, 4), (THIRD, 6), (FOURTH, 1), (SPLANE, 1), (FOURTH, 2), (FOURTH, 0), (FOURTH, 3),
    (THIRD, 5), (FOURTH, 4), (SSAVE, 0), (SAVE, 1), (SAVE, 6), (SAVE, 3), (SAVE, 2), (SAVE, 0), (SSAVE, 1), (SAVE, 4),
    (SAVE, 5),
)
RELAY, PIPE_FIRST, PLANE_ONLY, PLANE_FIRST = range(4)
WAYS = (RELAY, RELAY, RELAY, PLANE_FIRST, RELAY, PIPE_FIRST, PIPE_FIRST)
DIRECT = (True, True, False, False, False, False, True)


def grad_parts(state, model):
    wide = 4 * state + model
    return ((1, 4 * state, wide), (1, 2 * state, 4 * state), (1, 0, 2 * state), (0, 4 * state, wide), (0, 2 * state, 4 * state), (0, 0, state), (0, state, 2 * state))


def weight_parts(state, model):
    wide = 4 * state + model
    return ((0, 0, state), (0, state, 2 * state), (0, 2 * state, 4 * state), (0, 4 * state, wide), (1, 0, 2 * state), (1, 2 * state, 4 * state), (1, 4 * state, wide))


MESH = pl.DeviceIdType.MESH
F32 = jnp.float32
BF16 = jnp.bfloat16
NN = (((1,), (0,)), ((), ()))
NT = (((1,), (1,)), ((), ()))
TN = (((0,), (0,)), ((), ()))
FETCHES = ("lre", "lim", "lst", "b", "x", "c", "glu", "gain", "skip", "bias", "cot")


def cmul(u, v):
    return (u[0] * v[0] - u[1] * v[1], u[0] * v[1] + u[1] * v[0])


def conj(u):
    return (u[0], -u[1])


def dot(a, b, dims):
    return lax.dot_general(a, b, dims, preferred_element_type=F32)


def discretize(lam_re, lam_im, log_step):
    step = jnp.exp(log_step)
    radius = jnp.exp(lam_re * step)
    turn = lam_im * step
    decay = (radius * jnp.cos(turn), radius * jnp.sin(turn))
    modulus = lam_re * lam_re + lam_im * lam_im
    coef = (
        ((decay[0] - 1.0) * lam_re + decay[1] * lam_im) / modulus,
        (decay[1] * lam_re - (decay[0] - 1.0) * lam_im) / modulus,
    )
    return step, decay, coef


def discretize_grads(lam_re, lam_im, log_step, decay_grad, coef_grad):
    step, decay, coef = discretize(lam_re, lam_im, log_step)
    lam = (lam_re, lam_im)
    modulus = lam_re * lam_re + lam_im * lam_im
    inverse = (lam_re / modulus, -lam_im / modulus)
    through = cmul(coef_grad, conj(inverse))
    total = (decay_grad[0] + through[0], decay_grad[1] + through[1])
    first = cmul(total, (step * decay[0], -step * decay[1]))
    second = cmul(coef_grad, conj(cmul(coef, inverse)))
    turned = cmul(total, conj(cmul(lam, decay)))
    return first[0] - second[0], first[1] - second[1], step * turned[0]


def weight_gather(refs, pieces, depth, planes, me, plane, core, at_pipe, at_plane, at_core, remote):
    w_ref = refs["w"]
    sems = (refs["w_send"], refs["w_recv"])
    along, onward, across = {}, {}, {}
    (to_x, by_x), (to_y, by_y) = neighbours(me, at_pipe)

    def cols_of(piece, half=None):
        _, low, high = pieces[piece]
        middle = low + (high - low) // 256 * 128
        return pl.ds(*((low, high - low), (low, middle - low), (middle, high - middle))[0 if half is None else half + 1])

    def block(piece, z, member, half=None):
        return w_ref.at[pieces[piece][0], z, core, member, :, cols_of(piece, half)]

    def send(piece):
        own = block(piece, plane, me)
        along[piece] = [remote(own, own, sems, (piece, k - 1), at_plane(k)) for k in range(1, planes)]

    def place(k):
        return lax.rem(plane - k + planes, planes)

    def relay(piece):
        onward[piece] = []
        direct = DIRECT[piece]
        for k in range(1, planes):
            along[piece][k - 1].wait_recv()
            own = block(piece, place(k), me)
            for j, device in enumerate([at_pipe(j) for j in range(1, depth)] if direct else (to_x, to_y)):
                onward[piece].append(remote(own, own, sems, (piece, planes - 1 + 4 * (k - 1) + j), device))

    def forward(piece):
        made = []
        for k in range(1, planes):
            for j, (member, device) in enumerate(((by_x, to_y), (by_y, to_x))):
                onward[piece][2 * (k - 1) + j].wait_recv()
                half = block(piece, place(k), member, j)
                made.append(remote(half, half, sems, (piece, planes - 1 + 4 * (k - 1) + 2 + j), device))
        onward[piece] = made

    def swap(piece):
        for copy in onward[piece]:
            copy.wait_recv()
        both = w_ref.at[pieces[piece][0], :, core, :, :, cols_of(piece)]
        across[piece] = remote(both, both, sems, (piece, 5 * (planes - 1)), at_core)

    def ready(piece):
        across[piece].wait_recv()

    return send, relay, forward, swap, ready


def neighbours(me, at_pipe):
    x, y = lax.rem(me, 2), lax.div(me, 2)
    by_x, by_y = 2 * y + 1 - x, 2 * (1 - y) + x
    return (at_pipe(by_x - me + 4), by_x), (at_pipe(by_y - me + 4), by_y)


def gradient_sums(refs, depth, planes, me, plane, core, at_pipe, at_plane, at_core, remote):
    sems = (refs["g_send"], refs["g_recv"])
    copies = {}
    x, y = lax.rem(me, 2), lax.div(me, 2)
    (to_x, by_x), (to_y, by_y) = neighbours(me, at_pipe)

    def of(piece, *names):
        return [refs[f"{name}{piece}"] for name in names]

    def halves(piece):
        width = refs[f"done{piece}"].shape[-1]
        return pl.ds(0, width // 2), pl.ds(width // 2, width // 2)

    def back_by_relay(piece):
        return WAYS[piece] in (RELAY, PLANE_FIRST) and refs[f"done{piece}"].shape[-1] % 256 == 0

    def start(piece, matrix):
        part, other = of(piece, "part", "other")
        part[...] = matrix.astype(BF16).reshape(part.shape)
        copies[piece, 0] = remote(part.at[:, 1 - core], other, sems, (piece, 0), at_core)

    def first(piece):
        copies[piece, 0].wait_recv()
        part, other, pair, quad = of(piece, "part", "other", "pair", "quad")

        def add(i, carry):
            z, j = lax.div(i, depth), lax.rem(i, depth)
            total = part[z, core, j] + other[z, j]
            if WAYS[piece] in (PLANE_ONLY, PLANE_FIRST):
                pair[z, j] = total
            else:
                pair[j, z] = total
            return carry
        lax.fori_loop(0, planes * depth, add, 0, unroll=4)
        if WAYS[piece] == RELAY:
            low, high = halves(piece)
            made = []
            for i in range(2):
                made.append(remote(pair.at[2 * i + 1 - x, :, :, low], quad.at[0, i], sems, (piece, 1 + i), to_x))
                made.append(remote(pair.at[2 * (1 - y) + i, :, :, high], quad.at[1, i], sems, (piece, 3 + i), to_y))
        else:
            by_plane = WAYS[piece] in (PLANE_ONLY, PLANE_FIRST)
            count, here, there = (planes, plane, at_plane) if by_plane else (depth, me, at_pipe)
            made = [
                remote(pair.at[lax.rem(here + k, count)], quad.at[k - 1], sems, (piece, k), there(k))
                for k in range(1, count)
            ]
        copies[piece, 1] = made

    def middle(piece):
        pair, quad, pass_on, last = of(piece, "pair", "quad", "pass", "last")
        for copy in copies[piece, 1]:
            copy.wait_recv()
        low, high = halves(piece)

        def add(z, carry):
            pass_on[0, z] = pair[by_y, z, :, low] + quad[0, 1 - y, z]
            pass_on[1, z] = pair[by_x, z, :, high] + quad[1, 1 - x, z]
            return carry
        lax.fori_loop(0, planes, add, 0, unroll=2)
        copies[piece, 2] = [
            remote(pass_on.at[0], last.at[0], sems, (piece, 5), to_y),
            remote(pass_on.at[1], last.at[1], sems, (piece, 6), to_x),
        ]

    def second(piece):
        way = WAYS[piece]
        pair, quad, line, came = of(piece, "pair", "quad", "line", "came")
        for copy in copies[piece, 2 if way == RELAY else 1]:
            copy.wait_recv()
        if way == RELAY:
            low, high = halves(piece)
            last = refs[f"last{piece}"]

            def add(z, carry):
                for half, (cols, own) in enumerate(((low, y), (high, x))):
                    total = pair[me, z, :, cols].astype(F32) + quad[half, own, z].astype(F32) + last[half, z].astype(F32)
                    line[z, :, cols] = total.astype(BF16)
                return carry
        else:
            here, count = (plane, planes) if way in (PLANE_ONLY, PLANE_FIRST) else (me, depth)

            def add(i, carry):
                total = pair[here, i].astype(F32)
                for k in range(1, count):
                    total = total + quad[k - 1, i].astype(F32)
                if way == PLANE_ONLY:
                    came[me, i] = total.astype(BF16)
                else:
                    line[i] = total.astype(BF16)
                return carry
        lax.fori_loop(0, depth if way in (PLANE_ONLY, PLANE_FIRST) else planes, add, 0, unroll=2)
        if way == PLANE_ONLY:
            made = [remote(came.at[me], came.at[me], sems, (piece, 6 + k), at_pipe(k)) for k in range(1, depth)]
        elif way == PLANE_FIRST:
            made = [
                remote(line.at[lax.rem(me + k, depth)], came.at[k - 1], sems, (piece, 6 + k), at_pipe(k))
                for k in range(1, depth)
            ]
        else:
            made = [
                remote(line.at[lax.rem(plane + k, planes)], came.at[k - 1], sems, (piece, 6 + k), at_plane(k))
                for k in range(1, planes)
            ]
        copies[piece, 3] = made

    def third(piece):
        line, came, done = of(piece, "line", "came", "done")
        for copy in copies[piece, 3]:
            copy.wait_recv()
        by_plane = WAYS[piece] == PLANE_FIRST
        total = line[me if by_plane else plane].astype(F32)
        for k in range(1, depth if by_plane else planes):
            total = total + came[k - 1].astype(F32)
        done[me] = total.astype(BF16)
        devices = (to_x, to_y) if back_by_relay(piece) else [at_pipe(k) for k in range(1, depth)]
        copies[piece, 4] = [
            remote(done.at[me], done.at[me], sems, (piece, 6 + planes + i), device) for i, device in enumerate(devices)
        ]

    def fourth(piece):
        done = refs[f"done{piece}"]
        low, high = halves(piece)
        made = []
        for i, (member, cols, device) in enumerate(((by_x, low, to_y), (by_y, high, to_x))):
            copies[piece, 4][i].wait_recv()
            half = done.at[member, :, cols]
            made.append(remote(half, half, sems, (piece, 8 + planes + i), device))
        copies[piece, 4] = made

    def finish(piece):
        if WAYS[piece] == PLANE_ONLY:
            came = refs[f"came{piece}"]
            for copy in copies[piece, 3]:
                copy.wait_recv()
            done = came[0].astype(F32)
            for j in range(1, depth):
                done = done + came[j].astype(F32)
        else:
            for copy in copies[piece, 4]:
                copy.wait_recv()
            done = refs[f"done{piece}"][...].astype(F32)
        return done.reshape(done.shape[0] * done.shape[1], done.shape[2])

    return start, first, middle, second, third, fourth, finish


def small_sums(refs, depth, planes, me, plane, core, at_pipe, at_plane, at_core, remote):
    sems = (refs["s_send"], refs["s_recv"])
    own, other, quad, line = refs["small"], refs["s_other"], refs["s_quad"], refs["s_line"]
    copies = {}

    def start(layer):
        copies[layer, 0] = remote(own.at[layer], other.at[layer], sems, (layer, 0), at_core)

    def to_pipe(layer):
        copies[layer, 0].wait_recv()
        quad[layer, me] = own[layer] + other[layer]
        copies[layer, 1] = [
            remote(quad.at[layer, me], quad.at[layer, me], sems, (layer, k), at_pipe(k)) for k in range(1, depth)
        ]

    def to_plane(layer):
        for copy in copies[layer, 1]:
            copy.wait_recv()
        total = quad[layer, 0]
        for j in range(1, depth):
            total = total + quad[layer, j]
        line[layer, plane] = total
        copies[layer, 2] = [
            remote(line.at[layer, plane], line.at[layer, plane], sems, (layer, depth + k - 1), at_plane(k))
            for k in range(1, planes)
        ]

    def finish(layer):
        for copy in copies[layer, 2]:
            copy.wait_recv()
        total = line[layer, 0]
        for z in range(1, planes):
            total = total + line[layer, z]
        return total

    return start, to_pipe, to_plane, finish


def main_kernel(depth, planes, names, *refs):
    r_ = dict(zip(names, refs))
    x_ref, len_ref = r_["x"], r_["len"]
    small_ref = r_["small"]
    h_ref, go_ref, xhat_ref, rstd_ref, normed_ref = r_["h"], r_["go"], r_["xhat"], r_["rstd"], r_["normed"]
    p_ref, z_ref, zb_ref, dg_ref, gated_ref, sig_ref = r_["p"], r_["z"], r_["zb"], r_["dg"], r_["gated"], r_["sig"]
    gg_ref, gb_ref, gp_ref, src_ref, tmp_ref, acc_ref = r_["gg"], r_["gb"], r_["gp"], r_["src"], r_["tmp"], r_["acc"]
    ends_ref, got_ref, send_sems, recv_sems = r_["ends"], r_["got"], r_["send"], r_["recv"]
    w_ref = r_["w"]
    seqs, pos, model = x_ref.shape
    layers, state = r_["lre"].shape
    rows = seqs * pos
    steps = pos // CHUNKS
    me, dp = lax.axis_index("pipe"), lax.axis_index("dp")
    plane, core = lax.div(dp, 2), lax.rem(dp, 2)

    def peer(k):
        return lax.rem(me + k, depth)

    def at_pipe(k):
        return (peer(k), dp)

    def at_plane(k):
        return (me, 2 * lax.rem(plane + k, planes) + core)

    at_core = (me, 2 * plane + (1 - core))
    others = [at_pipe(k) for k in range(1, depth)]
    if planes:
        others += [at_plane(k) for k in range(1, planes)] + [at_core]
    barrier = pltpu.get_barrier_semaphore()
    for device in others:
        pl.semaphore_signal(barrier, inc=1, device_id=device, device_id_type=MESH)

    unsent = []

    def remote(src, dst, sems, at, device):
        copy = pltpu.make_async_remote_copy(
            src_ref=src, dst_ref=dst, send_sem=sems[0].at[at], recv_sem=sems[1].at[at],
            device_id=device, device_id_type=MESH,
        )
        copy.start()
        unsent.append(copy)
        return copy

    row = lax.broadcasted_iota(jnp.int32, (pos, pos), 0)
    col = lax.broadcasted_iota(jnp.int32, (pos, pos), 1)
    spread = (lax.rem(row, CHUNKS) * steps + lax.div(row, CHUNKS) == col).astype(F32).astype(BF16)
    masks = [(len_ref[q] > me * pos).astype(F32) for q in range(seqs)]
    sublane = lax.broadcasted_iota(jnp.int32, (CHUNKS, state), 0)

    def seq_rows(q):
        return pl.ds(q * pos, pos)

    def tiles(body, q, init=0, unroll=1):
        def step(i, carry):
            return body(pl.ds(pl.multiple_of(q * pos + i * TILE, TILE), TILE), masks[q], carry)
        return lax.fori_loop(0, pos // TILE, step, init, unroll=unroll)

    def all_tiles(body, init=0, unroll=4):
        for q in range(seqs):
            init = tiles(body, q, init, unroll)
        return init

    def fold(value):
        total = value[0:8]
        for r in range(8, value.shape[0], 8):
            total = total + value[r:r + 8]
        return total

    fetches = {}
    for at, name in enumerate(FETCHES):
        if name not in r_:
            continue
        fetches[name] = pltpu.make_async_copy(r_[name], r_[name + "_here"], r_["fetch"].at[at])
        fetches[name].start()
    x_here, cot_here = r_["x_here"], r_["cot_here"]
    gain_ref, skip_ref, bias_ref = r_["gain_here"], r_["skip_here"], r_["bias_here"]
    lre_ref, lim_ref, lst_ref = r_["lre_here"], r_["lim_here"], r_["lst_here"]
    for name in ("lre", "lim", "lst"):
        fetches[name].wait()
    step_all, decay_all, coef_all = discretize(lre_ref[...], lim_ref[...], lst_ref[...])
    if planes:
        ways = (depth, planes, me, plane, core, at_pipe, at_plane, at_core, remote)
        wide = 4 * state + model
        pieces = weight_parts(state, model)
        w_send, w_relay, w_forward, w_swap, w_ready = weight_gather(r_, pieces, *ways)
        g_start, g_first, g_middle, g_second, g_third, g_fourth, g_finish = gradient_sums(r_, *ways)
        parts = grad_parts(state, model)
        s_start, s_pipe, s_plane, s_finish = small_sums(r_, *ways)

        def keep(layer, matrix, low):
            high = low + matrix.shape[1]
            w_ref[layer, plane, core, :, :, low:high] = matrix.astype(BF16).reshape(depth, -1, high - low)

        fetches["b"].wait()
        for layer in range(layers):
            keep(layer, r_["b_here"][layer], 0)
    pl.semaphore_wait(barrier, len(others))

    def matrix(layer, which):
        low, high = (0, 2 * state, 4 * state)[which], (2 * state, 4 * state, w_ref.shape[-1])[which]
        value = w_ref[layer, ..., low:high]
        return value.reshape(model, high - low)

    def complex_rows(src, r):
        return (src[r, 0:state], src[r, state:2 * state])

    zero = jnp.zeros((CHUNKS, state), F32)

    def scan_ends(src, decay, down):
        def step(i, carry):
            s = (steps - 1 - i) if down else i
            made = []
            for q in range(seqs):
                r = pl.ds(pl.multiple_of(q * pos + s * CHUNKS, CHUNKS), CHUNKS)
                add = complex_rows(src, r)
                moved = cmul(decay, carry[q])
                made.append((moved[0] + add[0], moved[1] + add[1]))
            return tuple(made)
        return lax.fori_loop(0, steps, step, ((zero, zero),) * seqs, unroll=32)

    def shifted(value, k, down):
        rolled = pltpu.roll(value, CHUNKS - k if down else k, axis=0)
        keep = (sublane < CHUNKS - k) if down else (sublane >= k)
        return jnp.where(keep, rolled, 0.0)

    def squared(value, times):
        for _ in range(times):
            value = cmul(value, value)
        return value

    lanes = 128
    spans = state // lanes

    def chunk_powers(layer):
        powers = [squared(wide_decay(layer), steps.bit_length() - 1)]
        while len(powers) < CHUNKS.bit_length():
            powers.append(cmul(powers[-1], powers[-1]))
        return powers

    def place_table(powers, down):
        place = (CHUNKS - 1 - sublane) if down else sublane
        table = (jnp.ones((CHUNKS, state), F32), zero)
        for bit, factor in enumerate(powers[:-1]):
            moved = cmul(table, factor)
            take = lax.rem(lax.div(place, 1 << bit), 2) == 1
            table = (jnp.where(take, moved[0], table[0]), jnp.where(take, moved[1], table[1]))
        return table

    def start_exchange(number, ends, powers, down):
        sums = list(ends)
        for bit, jump in enumerate(powers[:-1]):
            for q in range(seqs):
                moved = cmul(jump, (shifted(sums[q][0], 1 << bit, down), shifted(sums[q][1], 1 << bit, down)))
                sums[q] = (sums[q][0] + moved[0], sums[q][1] + moved[1])
        last = 0 if down else CHUNKS - 1
        for q in range(seqs):
            for part in range(2):
                for j in range(spans):
                    at = (q * 2 + part) * spans + j
                    ends_ref[number, at:at + 1, :] = sums[q][part][last:last + 1, j * lanes:(j + 1) * lanes]
        copies = [
            remote(ends_ref.at[number], got_ref.at[number, k - 1], (send_sems, recv_sems), (number, k - 1),
                   at_pipe(depth - k if down else k))
            for k in range(1, depth)
        ]
        return copies, sums

    def finish_exchange(number, pending, powers, down):
        copies, sums = pending
        table = place_table(powers, down)
        exclusive = [(shifted(s[0], 1, down), shifted(s[1], 1, down)) for s in sums]
        for copy in copies:
            copy.wait_recv()
        jump = powers[-1]
        carries = []
        for q in range(seqs):
            total, factor = (zero, zero), (jnp.ones((CHUNKS, state), F32), zero)
            for k in range(1, depth):
                there = ((me + k < depth) if down else (me - k >= 0)).astype(F32)
                came = []
                for part in range(2):
                    at = (q * 2 + part) * spans
                    pieces_ = [
                        jnp.broadcast_to(got_ref[number, k - 1, at + j:at + j + 1, :], (CHUNKS, lanes))
                        for j in range(spans)
                    ]
                    came.append(jnp.concatenate(pieces_, axis=1) * there)
                moved = cmul(factor, came)
                total = (total[0] + moved[0], total[1] + moved[1])
                factor = cmul(factor, jump)
            moved = cmul(table, total)
            carries.append((exclusive[q][0] + moved[0], exclusive[q][1] + moved[1]))
        return carries

    def wide_decay(layer):
        return tuple(jnp.broadcast_to(part[layer:layer + 1], (CHUNKS, state)) for part in decay_all)

    small_ref[...] = jnp.zeros_like(small_ref)
    powers_of = [chunk_powers(layer) for layer in range(layers)]

    def back_powers(layer):
        return [conj(power) for power in powers_of[layer]]

    pad = pos + CHUNKS
    gather = (lax.rem(row, steps) * CHUNKS + lax.div(row, steps) == col).astype(F32).astype(BF16)
    zero_row = jnp.zeros((8, model), F32)
    puts, held = [], {}

    def put(name, at=None, cols=None):
        source, target = r_[name + "_here"], r_[name]
        if cols is not None:
            source, target = source.at[at, :, cols], target.at[at, :, cols]
        elif at is not None:
            source, target = source.at[at], target.at[at]
        copy = pltpu.make_async_copy(source, target, r_["put"].at[len(puts)])
        copy.start()
        puts.append(copy)

    def one(ref, layer):
        return ref[layer:layer + 1, :]

    def turn(layer, real, imag):
        return cmul((coef_all[0][layer:layer + 1], coef_all[1][layer:layer + 1]), (real, imag))

    def step_fold(layer):
        if layer == 0:
            fetches["c"].wait()
            fetches["glu"].wait()
        turned = turn(layer, r_["c_here"][layer, :, 0:state], r_["c_here"][layer, :, state:2 * state])
        keep(layer, turned[0], 2 * state)
        keep(layer, -turned[1], 3 * state)
        keep(layer, r_["glu_here"][layer], 4 * state)

    def step_x(_):
        for name in ("x", "gain", "skip", "bias"):
            fetches[name].wait()
        for q in range(seqs):
            h_ref[0, seq_rows(q), :] = dot(spread, x_here[q], NN).astype(BF16)

    def step_cot(_):
        fetches["cot"].wait()
        for q in range(seqs):
            go_ref[seq_rows(q), :] = dot(spread, cot_here[q], NN).astype(BF16)

    def step_norm(layer):
        gain = one(gain_ref, layer)

        def tile(r, mask, carry):
            h = h_ref[layer, r, :].astype(F32)
            mean = jnp.mean(h, axis=1, keepdims=True)
            centred = h - mean
            variance = jnp.mean(centred * centred, axis=1, keepdims=True)
            rstd = lax.rsqrt(variance + EPSILON)
            xhat = centred * rstd
            xhat_ref[layer, r, :] = xhat
            rstd_ref[layer, r, :] = jnp.broadcast_to(rstd, (TILE, 128))
            normed_ref[layer, r, :] = (xhat * gain * mask).astype(BF16)
            return carry
        all_tiles(tile, unroll=4)

    def step_proj(layer):
        p_ref[layer] = dot(normed_ref[layer], matrix(layer, 0), NN)

    def step_ends(layer):
        ends = scan_ends(p_ref.at[layer], wide_decay(layer), layer % 2 == 1)
        held["pending", layer] = start_exchange(layer, ends, powers_of[layer], layer % 2 == 1)

    def step_scan(layer):
        down = layer % 2 == 1
        decay = wide_decay(layer)
        carries = finish_exchange(layer, held["pending", layer], powers_of[layer], down)
        for q in range(seqs):
            at = q * pad + (pos if down else 0)
            z_ref[layer, at:at + CHUNKS, 0:state] = carries[q][0]
            z_ref[layer, at:at + CHUNKS, state:2 * state] = carries[q][1]

        def pair(i, carry):
            carry = list(carry)
            for q in range(seqs):
                pieces = []
                for half in range(2):
                    s = (steps - 1 - 2 * i - half) if down else 2 * i + half
                    r = pl.ds(pl.multiple_of(q * pos + s * CHUNKS, CHUNKS), CHUNKS)
                    add = complex_rows(p_ref.at[layer], r)
                    moved = cmul(decay, carry[q])
                    carry[q] = (moved[0] + add[0], moved[1] + add[1])
                    r = pl.ds(pl.multiple_of(q * pad + (s + (0 if down else 1)) * CHUNKS, CHUNKS), CHUNKS)
                    z_ref[layer, r, 0:state] = carry[q][0]
                    z_ref[layer, r, state:2 * state] = carry[q][1]
                    pieces.append(carry[q])
                if down:
                    pieces = pieces[::-1]
                low = (steps - 2 - 2 * i) if down else 2 * i
                r = pl.ds(pl.multiple_of(q * pos + low * CHUNKS, 2 * CHUNKS), 2 * CHUNKS)
                for part in range(2):
                    both = jnp.concatenate([pieces[0][part], pieces[1][part]], axis=0)
                    zb_ref[layer, r, part * state:(part + 1) * state] = both.astype(BF16)
            return tuple(carry)
        lax.fori_loop(0, steps // 2, pair, tuple(carries), unroll=16)

    def step_cdot(layer):
        tmp_ref[...] = dot(zb_ref[layer], matrix(layer, 1), NT)

    def step_gelu(layer):
        skip = one(skip_ref, layer)

        def tile(r, mask, carry):
            before = tmp_ref[r, :] + skip * normed_ref[layer, r, :].astype(F32)
            phi = 0.5 * (1.0 + lax.erf(before * 0.7071067811865476))
            dg_ref[layer, r, :] = phi + before * (0.3989422804014327 * jnp.exp(-0.5 * before * before))
            gated_ref[layer, r, :] = (before * phi).astype(BF16)
            return carry
        all_tiles(tile)

    def step_gdot(layer):
        tmp_ref[...] = dot(gated_ref[layer], matrix(layer, 2), NN)

    def step_out(layer):
        bias = one(bias_ref, layer)

        def tile(r, mask, carry):
            sig = 1.0 / (1.0 + jnp.exp(-(tmp_ref[r, :] + bias)))
            sig_ref[layer, r, :] = sig
            made = h_ref[layer, r, :].astype(F32) + mask * (gated_ref[layer, r, :].astype(F32) * sig)
            h_ref[layer + 1, r, :] = made.astype(BF16)
            return carry
        all_tiles(tile)

    def step_result(_):
        for q in range(seqs):
            r_["out_here"][q] = dot(gather, h_ref[layers, seq_rows(q), :], NN).astype(BF16)
        put("out")

    def step_gate(layer):
        def tile(r, mask, carry):
            sig = sig_ref[layer, r, :]
            branch = mask * go_ref[r, :].astype(F32) * sig
            grad = (branch * gated_ref[layer, r, :].astype(F32) * (1.0 - sig)).astype(BF16)
            gg_ref[r, :] = grad
            acc_ref[r, :] = branch
            return carry + fold(grad.astype(F32))
        held["bias", layer] = all_tiles(tile, zero_row)

    def step_gback(layer):
        tmp_ref[...] = dot(gg_ref[...], matrix(layer, 2), NT)

    def step_before(layer):
        def tile(r, mask, carry):
            gated_grad = (acc_ref[r, :] + tmp_ref[r, :]).astype(BF16).astype(F32)
            grad = (gated_grad * dg_ref[layer, r, :]).astype(BF16)
            gb_ref[r, :] = grad
            return carry + fold(grad.astype(F32) * normed_ref[layer, r, :].astype(F32))
        held["skip", layer] = all_tiles(tile, zero_row)

    def step_src(layer):
        src_ref[...] = dot(gb_ref[...], matrix(layer, 1), NN)

    def step_bends(layer):
        ends = scan_ends(src_ref, conj(wide_decay(layer)), layer % 2 == 0)
        held["back", layer] = start_exchange(layers + layer, ends, back_powers(layer), layer % 2 == 0)

    def step_bscan(layer):
        down = layer % 2 == 1
        back = conj(wide_decay(layer))
        carries = finish_exchange(layers + layer, held["back", layer], back_powers(layer), not down)

        def pair(i, loop):
            carry, sums = list(loop[0]), list(loop[1])
            for q in range(seqs):
                pieces = []
                for half in range(2):
                    s = 2 * i + half if down else (steps - 1 - 2 * i - half)
                    r = pl.ds(pl.multiple_of(q * pos + s * CHUNKS, CHUNKS), CHUNKS)
                    add = complex_rows(src_ref, r)
                    moved = cmul(back, carry[q])
                    adj = (moved[0] + add[0], moved[1] + add[1])
                    carry[q] = adj
                    pieces.append(adj)
                    proj = complex_rows(p_ref.at[layer], r)
                    r = pl.ds(pl.multiple_of(q * pad + (s + (1 if down else 0)) * CHUNKS, CHUNKS), CHUNKS)
                    prior = complex_rows(z_ref.at[layer], r)
                    sums[0] = sums[0] + (adj[0] * prior[0] + adj[1] * prior[1])
                    sums[1] = sums[1] + (adj[1] * prior[0] - adj[0] * prior[1])
                    sums[2] = sums[2] + (adj[0] * proj[0] + adj[1] * proj[1])
                    sums[3] = sums[3] + (adj[1] * proj[0] - adj[0] * proj[1])
                if not down:
                    pieces = pieces[::-1]
                low = 2 * i if down else (steps - 2 - 2 * i)
                r = pl.ds(pl.multiple_of(q * pos + low * CHUNKS, 2 * CHUNKS), 2 * CHUNKS)
                for part in range(2):
                    both = jnp.concatenate([pieces[0][part], pieces[1][part]], axis=0)
                    gp_ref[r, part * state:(part + 1) * state] = both.astype(BF16)
            return tuple(carry), tuple(sums)
        held["sums", layer] = lax.fori_loop(0, steps // 2, pair, (tuple(carries), (zero,) * 4), unroll=16)[1]

    def send_part(layer, low, made):
        high = low + made.shape[1]
        if not planes:
            r_["gpart"][layer, :, low:high] = made
            return
        for piece, (of_layer, first, last) in enumerate(parts):
            if of_layer == layer and low <= first and last <= high:
                g_start(piece, made[:, first - low:last - low])

    def step_cgrad(layer):
        send_part(layer, 2 * state, dot(gb_ref[...], zb_ref[layer], TN))

    def step_ggrad(layer):
        send_part(layer, 4 * state, dot(gated_ref[layer], gg_ref[...], TN))

    def step_bgrad(layer):
        send_part(layer, 0, dot(normed_ref[layer], gp_ref[...], TN))

    def step_xdot(layer):
        tmp_ref[...] = dot(gp_ref[...], matrix(layer, 0), NT)

    def step_bnorm(layer):
        gain, skip = one(gain_ref, layer), one(skip_ref, layer)

        def tile(r, mask, carry):
            grad = (tmp_ref[r, :] + skip * gb_ref[r, :].astype(F32)) * mask
            xhat = xhat_ref[layer, r, :]
            rstd = jnp.concatenate([rstd_ref[layer, r, :]] * (model // 128), axis=1)
            scaled = grad * gain
            first = jnp.mean(scaled, axis=1, keepdims=True)
            second = jnp.mean(scaled * xhat, axis=1, keepdims=True)
            made = go_ref[r, :].astype(F32) + rstd * (scaled - first - xhat * second)
            go_ref[r, :] = made.astype(BF16)
            return carry + fold(grad * xhat)
        gain_sum = all_tiles(tile, zero_row, unroll=4)
        for at, value in enumerate((gain_sum, held["skip", layer], held["bias", layer])):
            small_ref[layer, at:at + 1, :] = jnp.sum(value, axis=0, keepdims=True)
        for at, value in enumerate(held["sums", layer]):
            small_ref[layer, 3 + at:4 + at, 0:state] = jnp.sum(value, axis=0, keepdims=True)

    def step_xg(_):
        for q in range(seqs):
            r_["xg_here"][q] = dot(gather, go_ref[seq_rows(q), :], NN).astype(BF16)
        put("xg")

    def step_ssave(layer):
        total = s_finish(layer)
        for at, name in enumerate(("gain_grad", "skip_grad", "bias_grad")):
            r_[name + "_here"][layer:layer + 1, :] = total[at:at + 1, :]
        coef = (coef_all[0][layer:layer + 1], coef_all[1][layer:layer + 1])
        sums = [total[at:at + 1, 0:state] for at in range(3, 7)]
        scale = coef[0] * coef[0] + coef[1] * coef[1]
        coef_grad = cmul((sums[2], sums[3]), (coef[0] / scale, coef[1] / scale))
        made = discretize_grads(
            one(lre_ref, layer), one(lim_ref, layer), one(lst_ref, layer), (sums[0], sums[1]), coef_grad)
        for name, value in zip(("lre_grad", "lim_grad", "lst_grad"), made):
            r_[name + "_here"][layer:layer + 1, :] = value

    def step_save(piece):
        layer, low, high = parts[piece]
        done = g_finish(piece)
        if low >= 4 * state:
            r_["glu_grad_here"][layer] = done
            put("glu_grad", layer)
        elif low >= 2 * state:
            turned = turn(layer, done[:, 0:state], done[:, state:2 * state])
            r_["c_grad_here"][layer, :, 0:state] = turned[0]
            r_["c_grad_here"][layer, :, state:2 * state] = -turned[1]
            put("c_grad", layer)
        else:
            r_["b_grad_here"][layer, :, low:high] = done
            put("b_grad", layer, pl.ds(low, high - low))

    do = {
        X: step_x, COT: step_cot, NORM: step_norm, PROJ: step_proj, ENDS: step_ends, SCAN: step_scan, CDOT: step_cdot,
        GELU: step_gelu, GDOT: step_gdot, OUT: step_out, RESULT: step_result, GATE: step_gate, GBACK: step_gback,
        BEFORE: step_before, SRC: step_src, BENDS: step_bends, BSCAN: step_bscan, CGRAD: step_cgrad, GGRAD: step_ggrad,
        BGRAD: step_bgrad, XDOT: step_xdot, BNORM: step_bnorm, XG: step_xg,
    }
    if planes:
        do.update({
            FOLD: step_fold, WSEND: w_send, WRELAY: w_relay, WFORWARD: w_forward, WSWAP: w_swap, WREADY: w_ready,
            FIRST: g_first, MIDDLE: g_middle, SECOND: g_second, THIRD: g_third, FOURTH: g_fourth, SAVE: step_save,
            SSTART: s_start, SPIPE: s_pipe, SPLANE: s_plane, SSAVE: step_ssave,
        })
    for name, at in ORDER:
        if name in do:
            do[name](at)
    if planes:
        for name in ("gain_grad", "skip_grad", "bias_grad", "lre_grad", "lim_grad", "lst_grad"):
            put(name)
    for copy in puts:
        copy.wait()
    for copy in unsent:
        copy.wait_send()


def copy_kernel(*refs):
    count = (len(refs) - 2) // 3
    sources, targets, held, (in_sems, out_sems) = refs[:count], refs[count:2 * count], refs[2 * count:3 * count], refs[3 * count:]
    arrive = [pltpu.make_async_copy(sources[i], held[i], in_sems.at[i]) for i in range(count)]
    leave = [pltpu.make_async_copy(held[i], targets[i], out_sems.at[i]) for i in range(count)]
    for copy in arrive:
        copy.start()
    for first, then in zip(arrive, leave):
        first.wait()
        then.start()
    for copy in leave:
        copy.wait()


def copied(results):
    anywhere = pl.BlockSpec(memory_space=pl.ANY)
    return pl.pallas_call(
        copy_kernel,
        out_shape=tuple(jax.ShapeDtypeStruct(r.shape, r.dtype) for r in results),
        in_specs=[anywhere] * len(results),
        out_specs=(anywhere,) * len(results),
        scratch_shapes=[pltpu.VMEM(r.shape, r.dtype) for r in results] + [pltpu.SemaphoreType.DMA((len(results),))] * 2,
        compiler_params=pltpu.CompilerParams(vmem_limit_bytes=60 * 2**20),
    )(*results)


def run_main(planes, x_in, lengths, cotangent, norm_gain, lambda_re, lambda_im, log_step, skip_weight, glu_bias, weights):
    depth = lax.axis_size("pipe")
    seqs, pos, model = x_in.shape
    layers, state = lambda_re.shape
    rows = seqs * pos
    wide = 4 * state + model
    message = -(-seqs * 2 * state // (8 * 128)) * 8
    vmem = pl.BlockSpec(memory_space=pltpu.VMEM)
    smem = pl.BlockSpec(memory_space=pltpu.SMEM)
    anywhere = pl.BlockSpec(memory_space=pl.ANY)
    ins = dict(x=x_in, cot=cotangent, len=lengths, gain=norm_gain, lre=lambda_re, lim=lambda_im, lst=log_step,
               skip=skip_weight, bias=glu_bias)
    ins.update(zip(("b", "c", "glu") if planes else ("w",), weights))
    outs = dict(out=(x_in.shape, BF16), xg=(x_in.shape, BF16))
    scratch = dict(
        h=pltpu.VMEM((layers + 1, rows, model), BF16),
        go=pltpu.VMEM((rows, model), BF16),
        xhat=pltpu.VMEM((layers, rows, model), F32),
        rstd=pltpu.VMEM((layers, rows, 128), F32),
        normed=pltpu.VMEM((layers, rows, model), BF16),
        p=pltpu.VMEM((layers, rows, 2 * state), F32),
        z=pltpu.VMEM((layers, rows + seqs * CHUNKS, 2 * state), F32),
        zb=pltpu.VMEM((layers, rows, 2 * state), BF16),
        dg=pltpu.VMEM((layers, rows, model), F32),
        gated=pltpu.VMEM((layers, rows, model), BF16),
        sig=pltpu.VMEM((layers, rows, model), F32),
        gg=pltpu.VMEM((rows, model), BF16),
        gb=pltpu.VMEM((rows, model), BF16),
        gp=pltpu.VMEM((rows, 2 * state), BF16),
        src=pltpu.VMEM((rows, 2 * state), F32),
        tmp=pltpu.VMEM((rows, model), F32),
        acc=pltpu.VMEM((rows, model), F32),
        ends=pltpu.VMEM((2 * layers, message, 128), F32),
        got=pltpu.VMEM((2 * layers, depth - 1, message, 128), F32),
        fetch=pltpu.SemaphoreType.DMA((len(FETCHES),)),
        put=pltpu.SemaphoreType.DMA((8 + len(WAYS),)),
        send=pltpu.SemaphoreType.DMA((2 * layers, depth - 1)),
        recv=pltpu.SemaphoreType.DMA((2 * layers, depth - 1)),
    )
    if planes:
        local = weights[0].shape[1]
        part = local // depth
        full, halves = (layers, model), (layers, state)
        outs.update(
            gain_grad=(full, F32), lre_grad=(halves, F32), lim_grad=(halves, F32), lst_grad=(halves, F32),
            b_grad=((layers, local, 2 * state), F32), c_grad=((layers, local, 2 * state), F32),
            skip_grad=(full, F32), glu_grad=((layers, local, model), F32), bias_grad=(full, F32),
        )
        scratch.update(
            small=pltpu.VMEM((layers, 8, model), F32),
            s_other=pltpu.VMEM((layers, 8, model), F32),
            s_quad=pltpu.VMEM((layers, depth, 8, model), F32),
            s_line=pltpu.VMEM((layers, planes, 8, model), F32),
            w=pltpu.VMEM((layers, planes, 2, depth, part, wide), BF16),
        )
        spans = [high - low for _, low, high in grad_parts(state, model)]
        for piece, way in enumerate(WAYS):
            width = spans[piece]
            count, other = (planes, depth) if way in (PLANE_ONLY, PLANE_FIRST) else (depth, planes)
            shapes = dict(
                part=(planes, 2, depth, part, width), other=(planes, depth, part, width),
                pair=(count, other, part, width), quad=(count - 1, other, part, width),
                line=(other, part, width), came=(other - 1, part, width), done=(depth, part, width),
            )
            if way == RELAY:
                shapes.update(quad=(2, 2, planes, part, width // 2))
                shapes.update({"pass": (2, planes, part, width // 2), "last": (2, planes, part, width // 2)})
            if way == PLANE_ONLY:
                shapes.update(came=(depth, depth, part, width))
            scratch.update({f"{name}{piece}": pltpu.VMEM(shape, BF16) for name, shape in shapes.items()})
        for name, shape in dict(
            w=(len(DIRECT), 5 * planes - 4), g=(len(WAYS), 10 + planes), s=(layers, depth + planes - 1)
        ).items():
            scratch[name + "_send"] = pltpu.SemaphoreType.DMA(shape)
            scratch[name + "_recv"] = pltpu.SemaphoreType.DMA(shape)
    else:
        outs.update(gpart=((layers, model, wide), F32), small=((layers, 8, model), F32))
    fetched = tuple(name for name in FETCHES if name in ins)
    for name in fetched:
        scratch[name + "_here"] = pltpu.VMEM(ins[name].shape, ins[name].dtype)
    stored = tuple(name for name in outs if name not in ("gpart", "small"))
    for name in stored:
        scratch[name + "_here"] = pltpu.VMEM(*outs[name])
    names = tuple(ins) + tuple(outs) + tuple(scratch)
    return pl.pallas_call(
        functools.partial(main_kernel, depth, planes, names),
        out_shape=tuple(jax.ShapeDtypeStruct(*o) for o in outs.values()),
        in_specs=[smem if name == "len" else anywhere if name in fetched else vmem for name in ins],
        out_specs=tuple(anywhere if name in stored else vmem for name in outs),
        scratch_shapes=list(scratch.values()),
        compiler_params=pltpu.CompilerParams(
            collective_id=0, has_side_effects=True, vmem_limit_bytes=60 * 2**20
        ),
    )(*ins.values())


def per_device(
    x_in, lengths, cotangent, norm_gain, lambda_re, lambda_im, log_step,
    b_weight, c_weight, skip_weight, glu_weight, glu_bias,
):
    depth, owners = lax.axis_size("pipe"), lax.axis_size("dp")
    state = lambda_re.shape[1]
    rest = (lambda_re, lambda_im, log_step, skip_weight, glu_bias)
    if depth == 4 and b_weight.shape[1] % (16 * depth) == 0 and owners % 2 == 0:
        return copied(run_main(owners // 2, x_in, lengths, cotangent, norm_gain, *rest, (b_weight, c_weight, glu_weight)))
    _, _, coef = discretize(lambda_re, lambda_im, log_step)
    c_real, c_imag = c_weight[:, :, :state], c_weight[:, :, state:]
    turned = cmul((coef[0][:, None], coef[1][:, None]), (c_real, c_imag))
    shard = jnp.concatenate([b_weight, turned[0], -turned[1], glu_weight], axis=2).astype(BF16)
    weights = lax.all_gather(shard, "dp", axis=1, tiled=True)
    output, x_grad, gpart, small = run_main(
        0, x_in, lengths, cotangent, norm_gain, *rest, (weights,)
    )
    grads = lax.psum_scatter(gpart, "dp", scatter_dimension=1, tiled=True)
    grads = lax.psum(grads.astype(BF16), "pipe").astype(F32)
    small = lax.psum(small, ("pipe", "dp"))
    m_real, m_imag = grads[:, :, 2 * state:3 * state], grads[:, :, 3 * state:4 * state]
    turned = cmul((coef[0][:, None], coef[1][:, None]), (m_real, m_imag))
    c_grad = jnp.concatenate([turned[0], -turned[1]], axis=2)
    decay_grad = (small[:, 3, :state], small[:, 4, :state])
    scale = coef[0] * coef[0] + coef[1] * coef[1]
    coef_grad = cmul((small[:, 5, :state], small[:, 6, :state]), (coef[0] / scale, coef[1] / scale))
    lam_re_grad, lam_im_grad, step_grad = discretize_grads(lambda_re, lambda_im, log_step, decay_grad, coef_grad)
    return (
        output, x_grad, small[:, 0], lam_re_grad, lam_im_grad, step_grad,
        grads[:, :, :2 * state], c_grad, small[:, 1], grads[:, :, 4 * state:], small[:, 2],
    )


def solution(mesh):
    split, whole, rows = P("dp", "pipe", None), P(), P(None, "dp", None)
    return jax.shard_map(
        per_device,
        mesh=mesh,
        in_specs=(split, P("dp"), split, whole, whole, whole, whole, rows, rows, whole, rows, whole),
        out_specs=(split, split, whole, whole, whole, whole, rows, rows, whole, rows, whole),
        check_vma=False,
    )
```
